32 devices in a mesh: dp: 16 (over z, x, core), seq: 2 (over y).
Axes of the slice: x: 2, y: 2, z: 4, core: 2. Of those that a mesh axis runs over, the one named last changes fastest.
Arguments:
- entering_activations: bfloat16 [32, 1024, 1024], P('dp', 'seq'), may hold values from -6 to 6
- document_numbers: int32 [32, 1024], P('dp', 'seq'), may hold values from 0 to 3, never falling along the last dimension, each value on 1 to 800 neighbouring positions
- result_cotangent: bfloat16 [32, 1024, 1024], P('dp', 'seq'), may hold values from -6 to 6
- normalizer_scales: float32 [2, 2, 1024], replicated, may hold values from 0.5 to 1.5
- normalizer_offsets: float32 [2, 2, 1024], replicated, may hold values from -2.5 to 2.5
- shift_blend_factors: float32 [2, 5, 1024], replicated, may hold values from 0 to 1
- fading_natural_logs_per_feature: float32 [2, 1024], replicated, as said below
- feature_reward_logs: float32 [2, 1024], replicated, may hold values from -1 to 1
- attention_triple_matrix: bfloat16 [2, 3, 1024, 1024], P(None, None, 'dp', 'seq'), may hold values from -0.1875 to 0.1875
- attention_result_matrix: bfloat16 [2, 1024, 1024], P(None, 'dp', 'seq'), may hold values from -0.75 to 0.75
- channelmix_lookup_matrix: bfloat16 [2, 1024, 4096], P(None, 'dp', 'seq'), may hold values from -0.1875 to 0.1875
- channelmix_content_matrix: bfloat16 [2, 4096, 1024], P(None, 'dp', 'seq'), may hold values from -0.09375 to 0.09375
- channelmix_accept_matrix: bfloat16 [2, 1024, 1024], P(None, 'dp', 'seq'), may hold values from -0.1875 to 0.1875
Outputs:
- y_out: bfloat16 [32, 1024, 1024], P('dp', 'seq')
- grad_x: float32 [32, 1024, 1024], P('dp', 'seq')
- grad_norm_gain: float32 [2, 2, 1024], replicated
- grad_norm_bias: float32 [2, 2, 1024], replicated
- grad_mixes: float32 [2, 5, 1024], replicated
- grad_time_decay: float32 [2, 1024], replicated
- grad_time_first: float32 [2, 1024], replicated
- grad_att_kvr: float32 [2, 3, 1024, 1024], P(None, None, 'dp', 'seq')
- grad_att_out: float32 [2, 1024, 1024], P(None, 'dp', 'seq')
- grad_ffn_key: float32 [2, 1024, 4096], P(None, 'dp', 'seq')
- grad_ffn_value: float32 [2, 4096, 1024], P(None, 'dp', 'seq')
- grad_ffn_recept: float32 [2, 1024, 1024], P(None, 'dp', 'seq')
The draws below stay inside these ranges and needn't reach their ends.
Inputs may be any that keep to these rules, and one draw needn't show every extreme that they name: `document_numbers`: within each row the document numbers never fall; a document starts at the row's start and wherever the number changes. exp(fading_natural_logs_per_feature) is a channel's decay rate per token, at most 4 / 512.
All inputs are finite; a program needn't handle non-finite values.
Results may differ from the reference program's by a relative error of at most 0.018.
Values may be sent and summed in bfloat16 or wider, within the bound.
No kernel may reach another device: no remote copies, remote signals or barrier semaphores. Data moves between devices by JAX's collectives and lax.ppermute only.
A program may use at most 448 MiB of HBM per device.

```python
import math
import jax
import jax.numpy as jnp
import numpy as np
from jax import lax

WIDTH_MODEL = 1024
FF = 4096
DEPTH_TOTAL = 2
ROW_LEN = 1024
SEGS = 4
BLOCK = 512
SEG_MOST = 800
BATCH = 32


def draw_fading_natural_logs_per_feature(key, part):
    key_slow, key_fast, key_pick = jax.random.split(key, 3)
    shape_d = (DEPTH_TOTAL, WIDTH_MODEL)
    slow_rate = jnp.exp(jax.random.uniform(key_slow, shape_d, jnp.float32, math.log(0.1 / ROW_LEN), math.log(1.0 / ROW_LEN)))
    fast_rate = 1.0 / (BLOCK * jax.random.uniform(key_fast, shape_d, jnp.float32, 0.25, 0.4))
    picked = jax.random.uniform(key_pick, shape_d, jnp.float32) < 0.5
    rate_all = jnp.where(picked, fast_rate, slow_rate)
    return jnp.log(rate_all).astype(jnp.float32)


def level_of(stream_key, shape, cuts, low, top_value):
    loudness, own = 1.0, jax.random.fold_in(stream_key, 6)
    for position, parts in cuts:
        draws = jnp.exp(jax.random.uniform(jax.random.fold_in(own, position), (parts,), jnp.float32, low / len(cuts), top_value / len(cuts)))
        loudness = loudness * jnp.repeat(draws, shape[position] // parts).reshape([-1 if axis == position else 1 for axis in range(len(shape))])
    return loudness


def split_up(amount, total, reach, lean):
    portions = [(1 << 20) // math.isqrt(grade ** lean) + 1 for grade in range(2, amount + 1)]
    spare, holding = total - reach - (amount - 1), [1] * (amount - 1)
    while spare > 0:
        free = [i for i in range(amount - 1) if holding[i] < reach]
        mass, remaining = sum([portions[i] for i in free]), spare
        for i in free:
            addition = min(reach - holding[i], max(1, remaining * portions[i] // mass), spare)
            holding[i] = holding[i] + addition
            spare = spare - addition
    return np.array([reach] + holding)


def uneven_parts(stream_key, number_of, total, reach, slope):
    if number_of == 2:
        one = jax.random.randint(stream_key, (), max(1, total - reach), min(reach, total - 1) + 1)
        return jnp.stack([one, total - one])
    tallies = jnp.asarray(split_up(number_of, total, reach, slope), jnp.int32)
    pairs = (number_of - 1) // 2
    source_of, receiver = tallies[1:1 + 2 * pairs:2], tallies[2:2 + 2 * pairs:2]
    margin = jnp.minimum(source_of - 1, reach - receiver)
    passed = jax.random.randint(jax.random.fold_in(stream_key, 1), (pairs,), 0, 1 << 20) % (margin + 1)
    tallies = tallies.at[1:1 + 2 * pairs:2].set(source_of - passed).at[2:2 + 2 * pairs:2].set(receiver + passed)
    return tallies[jax.random.permutation(jax.random.fold_in(stream_key, 2), number_of)]


def bell_draw(stream_key, shape, scale, bound, shards=(), kind=jnp.bfloat16):
    drawn = jax.random.normal(stream_key, shape, jnp.float32) * scale
    if len(shards) > 0:
        drawn = level_of(stream_key, shape, shards, -0.22, 0.18) * drawn
    return jnp.clip(drawn, min=-bound, max=bound).astype(kind)


def setup_inputs(seed: int = 0) -> dict:
    streams_of = jax.random.split(jax.random.key(seed), 14)
    return {
        "entering_activations": bell_draw(streams_of[0], (BATCH, ROW_LEN, WIDTH_MODEL), 1.0, 6.0, ((0, 16), (1, 2))),
        "document_numbers": jax.vmap(lambda own: jnp.searchsorted(jnp.cumsum(uneven_parts(own, SEGS, ROW_LEN, SEG_MOST, 2)), jnp.arange(ROW_LEN), side="right"))(jax.random.split(streams_of[1], BATCH)).reshape((BATCH, ROW_LEN)).astype(jnp.int32),
        "result_cotangent": bell_draw(streams_of[2], (BATCH, ROW_LEN, WIDTH_MODEL), 1.0, 6.0, ((0, 16), (1, 2))),
        "normalizer_scales": jnp.clip(1.0 + 0.1 * jax.random.normal(streams_of[3], (DEPTH_TOTAL, 2, WIDTH_MODEL), jnp.float32), 0.5, 1.5),
        "normalizer_offsets": bell_draw(streams_of[4], (DEPTH_TOTAL, 2, WIDTH_MODEL), 0.3, 2.5, (), jnp.float32),
        "shift_blend_factors": jnp.clip(jax.random.uniform(streams_of[5], (DEPTH_TOTAL, 5, WIDTH_MODEL), jnp.float32, 0.0, 1.0), 0.0, 1.0),
        "fading_natural_logs_per_feature": draw_fading_natural_logs_per_feature(jax.random.fold_in(streams_of[13], 71), 0),
        "feature_reward_logs": jnp.clip(jax.random.uniform(streams_of[7], (DEPTH_TOTAL, WIDTH_MODEL), jnp.float32, -1.0, 1.0), -1.0, 1.0),
        "attention_triple_matrix": bell_draw(streams_of[8], (DEPTH_TOTAL, 3, WIDTH_MODEL, WIDTH_MODEL), WIDTH_MODEL ** -0.5, 0.1875, ((2, 16), (3, 2))),
        "attention_result_matrix": bell_draw(streams_of[9], (DEPTH_TOTAL, WIDTH_MODEL, WIDTH_MODEL), (WIDTH_MODEL // 16) ** -0.5, 0.75, ((1, 16), (2, 2))),
        "channelmix_lookup_matrix": bell_draw(streams_of[10], (DEPTH_TOTAL, WIDTH_MODEL, FF), WIDTH_MODEL ** -0.5, 0.1875, ((1, 16), (2, 2))),
        "channelmix_content_matrix": bell_draw(streams_of[11], (DEPTH_TOTAL, FF, WIDTH_MODEL), FF ** -0.5, 0.09375, ((1, 16), (2, 2))),
        "channelmix_accept_matrix": bell_draw(streams_of[12], (DEPTH_TOTAL, WIDTH_MODEL, WIDTH_MODEL), WIDTH_MODEL ** -0.5, 0.1875, ((1, 16), (2, 2))),
    }


EPS = 1e-05

@jax.custom_vjp
def low(v):
    return lax.optimization_barrier(v.astype(jnp.bfloat16)).astype(jnp.float32)

@jax.custom_vjp
def low_back(v):
    return v

def low_keep(v):
    return (low(v), None)

def low_pass(kept, grad):
    return (grad,)

def back_keep(v):
    return (v, None)

def back_low(kept, grad):
    return (low(grad),)
low.defvjp(low_keep, low_pass)
low_back.defvjp(back_keep, back_low)

def norm_apply(residual_flow, gain_vector, bias_vector):
    centre_of = lax.optimization_barrier(jnp.mean(residual_flow, axis=-1, keepdims=True))
    centred = residual_flow - centre_of
    spread = lax.optimization_barrier(jnp.mean(centred * centred, axis=-1, keepdims=True))
    return centred * lax.rsqrt(spread + EPS) * gain_vector + bias_vector

def product(left_op, right_op):
    return jnp.einsum('gtd,de->gte', left_op, right_op, precision=lax.Precision.HIGHEST, preferred_element_type=jnp.float32)

def shift_tokens(normed, active_token_flags):
    return jnp.concatenate([jnp.zeros_like(normed[:, :1]), normed[:, :-1]], axis=1) * active_token_flags[:, :, None]

def affine_scan_update(entering_lookups, entering_contents, active_token_flags, fading_feature_factor, reward_feature_factor):

    def advance(carried, inputs):
        state_a, state_b = carried
        key_t, content_current, live_t = inputs
        visited_first = live_t[:, None] * state_a
        visited_second = live_t[:, None] * state_b
        powered_lookup = jnp.exp(key_t)
        reward_scaled = powered_lookup * reward_feature_factor
        final_answer = (visited_first + reward_scaled * content_current) / (visited_second + reward_scaled)
        return ((fading_feature_factor * visited_first + powered_lookup * content_current, fading_feature_factor * visited_second + powered_lookup), final_answer)
    initial = jnp.zeros(entering_lookups[:, 0].shape, jnp.float32)
    final_state, outs_seq = lax.scan(advance, (initial, initial), (jnp.swapaxes(entering_lookups, 0, 1), jnp.swapaxes(entering_contents, 0, 1), jnp.swapaxes(active_token_flags, 0, 1)))
    return jnp.swapaxes(outs_seq, 0, 1)

def model(residual_flow, active_token_flags, weight_collection):
    scale_terms, shift_terms, blend_entire, fading_natural_logs, reward_natural_logs, triple_mapping_weight, attention_result_weight, channelmix_lookup_weight, channelmix_content_weight, channelmix_accept_weight = weight_collection
    for depth_position in range(DEPTH_TOTAL):
        mix_row = blend_entire[depth_position]
        normed = norm_apply(residual_flow, scale_terms[depth_position, 0], shift_terms[depth_position, 0])
        before = shift_tokens(normed, active_token_flags)
        change = normed - before
        input_k = low(before + mix_row[0] * change)
        input_v = low(before + mix_row[1] * change)
        input_r = low(before + mix_row[2] * change)
        lookup_mapping = low_back(product(input_k, triple_mapping_weight[depth_position, 0]))
        content_mapping = low_back(product(input_v, triple_mapping_weight[depth_position, 1]))
        recept = low_back(product(input_r, triple_mapping_weight[depth_position, 2]))
        fading_feature_factor = jnp.exp(-jnp.exp(fading_natural_logs[depth_position]))
        reward_feature_factor = jnp.exp(reward_natural_logs[depth_position])
        attention_sum_result = affine_scan_update(lookup_mapping, content_mapping, active_token_flags, fading_feature_factor, reward_feature_factor)
        gated_z = low(jax.nn.sigmoid(recept) * attention_sum_result)
        residual_flow = residual_flow + low_back(product(gated_z, attention_result_weight[depth_position]))
        normed = norm_apply(residual_flow, scale_terms[depth_position, 1], shift_terms[depth_position, 1])
        before = shift_tokens(normed, active_token_flags)
        change = normed - before
        input_k = low(before + mix_row[3] * change)
        input_r = low(before + mix_row[4] * change)
        hidden = low_back(product(input_k, channelmix_lookup_weight[depth_position]))
        relu_h = jax.nn.relu(hidden)
        active = low(relu_h * relu_h)
        carried_v = low_back(product(active, channelmix_content_weight[depth_position]))
        recept = low_back(product(input_r, channelmix_accept_weight[depth_position]))
        residual_flow = residual_flow + jax.nn.sigmoid(recept) * carried_v
    return residual_flow

def reference(entering_activations, document_numbers, result_cotangent, normalizer_scales, normalizer_offsets, shift_blend_factors, fading_natural_logs_per_feature, feature_reward_logs, attention_triple_matrix, attention_result_matrix, channelmix_lookup_matrix, channelmix_content_matrix, channelmix_accept_matrix):
    group_rows = math.gcd(BATCH, 4)
    count_g = BATCH // group_rows
    model_weights = (normalizer_scales, normalizer_offsets, shift_blend_factors, fading_natural_logs_per_feature, feature_reward_logs, attention_triple_matrix.astype(jnp.float32), attention_result_matrix.astype(jnp.float32), channelmix_lookup_matrix.astype(jnp.float32), channelmix_content_matrix.astype(jnp.float32), channelmix_accept_matrix.astype(jnp.float32))
    earlier = jnp.concatenate([jnp.full((BATCH, 1), -1, jnp.int32), document_numbers[:, :-1]], axis=1)
    alive_all = (document_numbers == earlier).astype(jnp.float32)

    def one_group(totals, inputs):
        rows_x, rows_live, rows_grad = inputs

        def forward(residual_flow, weight_collection):
            return model(residual_flow, rows_live, weight_collection)
        results, pullback = jax.vjp(forward, rows_x, model_weights)
        grads_x, grads_p = pullback(rows_grad)
        return (jax.tree.map(jnp.add, totals, grads_p), (results, grads_x))
    zero_totals = jax.tree.map(jnp.zeros_like, model_weights)
    shape_g = (count_g, group_rows, ROW_LEN, WIDTH_MODEL)
    totals, (results, grads_x) = lax.scan(one_group, zero_totals, (entering_activations.astype(jnp.float32).reshape(shape_g), alive_all.reshape(count_g, group_rows, ROW_LEN), result_cotangent.astype(jnp.float32).reshape(shape_g)))
    return (results.reshape(BATCH, ROW_LEN, WIDTH_MODEL).astype(jnp.bfloat16), grads_x.reshape(BATCH, ROW_LEN, WIDTH_MODEL), totals[0], totals[1], totals[2], totals[3], totals[4], totals[5], totals[6], totals[7], totals[8], totals[9])
```

```python
import functools

import jax
import jax.numpy as jnp
import numpy as np
from jax import lax
from jax.experimental import pallas as pl
from jax.experimental.pallas import tpu as pltpu
from jax.sharding import PartitionSpec as P

EPS = 1e-05
BF = jnp.bfloat16
F32 = jnp.float32
BOTH = ("dp", "seq")
VMEM = 58 * 2**20


def sizes():
    return lax.axis_size("dp"), lax.axis_size("seq")


def paired():
    dp, seq = sizes()
    return seq == 2 and dp % 4 == 0


def place(d):
    return d // 4, d // 2 % 2, d % 2


def core_of():
    if not paired():
        return jnp.int32(0)
    return lax.rem(lax.axis_index("dp"), 2)


def moved(array, target):
    dp, seq = sizes()
    pairs = []
    for d in range(dp):
        for y in range(seq):
            z, x, c, y2 = target(*place(d), y)
            pairs.append((d * seq + y, (z * 4 + x * 2 + c) * seq + y2))
    return lax.ppermute(array, BOTH, pairs)


def to_core(z, x, c, y):
    return z, x, 1 - c, y


def to_second(z, x, c, y):
    return (z, 1 - x, c, y) if c == 0 else (z, x, c, 1 - y)


def to_third(z, x, c, y):
    return (z, x, c, 1 - y) if c == 0 else (z, 1 - x, c, y)


def along_z(step):
    depth = sizes()[0] // 4

    def target(z, x, c, y):
        return (z + step) % depth, x, c, y

    return target


def unit_tables():
    dp, seq = sizes()
    depth = dp // 4
    rows = []
    for d in range(dp):
        for y in range(seq):
            z, x, c = place(d)
            half, index = [], []
            for yy in range(2):
                for zz in range(depth):
                    for xx in range(2):
                        dx, dy, dz = xx ^ x, yy ^ y, (z - zz) % depth
                        half.append(dy if c == 0 else dx)
                        index.append((dx if c == 0 else dy) * depth + dz)
            held = []
            for side in range(2):
                own = [i for i, h in zip(index, half) if h == side]
                last, line = own[0], []
                for i, h in zip(index, half):
                    last = i if h == side else last
                    line.append(last)
                held.append(line)
            order = [0] * (4 * depth)
            for unit, (i, h) in enumerate(zip(index, half)):
                order[h * 2 * depth + i] = unit
            rows.append([half, held[0], held[1], order])
    table = jnp.asarray(np.array(rows, np.int32))
    me = lax.axis_index("dp") * seq + lax.axis_index("seq")
    return lax.dynamic_index_in_dim(table, me, 0, keepdims=False)


def arrange(table, own, other):
    units, block = 2 * own.shape[0], (1,) + own.shape[1:]

    def body(table_ref, own_ref, other_ref, out_ref):
        half = table_ref[0, pl.program_id(0)]

        @pl.when(half == 0)
        def _():
            out_ref[...] = own_ref[...]

        @pl.when(half == 1)
        def _():
            out_ref[...] = other_ref[...]

    return pl.pallas_call(
        body,
        grid_spec=pltpu.PrefetchScalarGridSpec(
            num_scalar_prefetch=1,
            grid=(units,),
            in_specs=[
                pl.BlockSpec(block, lambda i, t: (t[1, i], 0, 0)),
                pl.BlockSpec(block, lambda i, t: (t[2, i], 0, 0)),
            ],
            out_specs=pl.BlockSpec(block, lambda i, t: (i, 0, 0)),
        ),
        out_shape=jax.ShapeDtypeStruct((units,) + own.shape[1:], own.dtype),
        compiler_params=pltpu.CompilerParams(vmem_limit_bytes=VMEM),
        cost_estimate=pl.CostEstimate(flops=0, bytes_accessed=4 * own.size * 2, transcendentals=0),
    )(table, own, other)


def split_units(table, whole):
    units, block = whole.shape[0], (1,) + whole.shape[1:]
    half = units // 2

    def body(table_ref, in_ref, away_ref, keep_ref):
        step = pl.program_id(0)

        @pl.when(step < half)
        def _():
            away_ref[...] = in_ref[...]

        @pl.when(step >= half)
        def _():
            keep_ref[...] = in_ref[...]

    shape = jax.ShapeDtypeStruct((half,) + whole.shape[1:], whole.dtype)
    return pl.pallas_call(
        body,
        grid_spec=pltpu.PrefetchScalarGridSpec(
            num_scalar_prefetch=1,
            grid=(units,),
            in_specs=[pl.BlockSpec(block, lambda i, t: (t[3, lax.rem(i + half, units)], 0, 0))],
            out_specs=[
                pl.BlockSpec(block, lambda i, t: (jnp.minimum(i, half - 1), 0, 0)),
                pl.BlockSpec(block, lambda i, t: (jnp.maximum(i - half, 0), 0, 0)),
            ],
        ),
        out_shape=[shape, shape],
        compiler_params=pltpu.CompilerParams(vmem_limit_bytes=VMEM),
        cost_estimate=pl.CostEstimate(flops=0, bytes_accessed=4 * whole.size, transcendentals=0),
    )(table, whole)


def gather_pair(core, table, first, second):
    dp, seq = sizes()
    if not paired():
        return tuple(
            lax.all_gather(part, ("seq", "dp")).reshape((seq, dp) + part.shape)
            for part in (first, second)
        )
    depth = dp // 4
    kept = jnp.where(core == 0, first, second)
    came = moved(jnp.where(core == 0, second, first), to_core)
    pair = jnp.where(core == 0, jnp.stack([kept, came]), jnp.stack([came, kept]))
    line = jnp.stack([pair] + [moved(pair, along_z(step)) for step in range(1, depth)])
    line = line.reshape((depth, -1) + first.shape[1:])
    half = jnp.concatenate([line, moved(line, to_second)])
    mine = arrange(table, half, moved(half, to_third))
    other = moved(mine, to_core)
    shape = (seq, dp) + first.shape
    return mine.reshape(shape), other.reshape(shape)


def scatter_pair(core, table, stores):
    dp, seq = sizes()
    shape = stores.shape[3:]
    if not paired():
        flat = stores.reshape((2, seq * dp) + shape)
        return tuple(
            lax.psum_scatter(flat[i], ("seq", "dp"), scatter_dimension=0).astype(F32)
            for i in range(2)
        )
    depth = dp // 4
    groups = [[2 * i, 2 * i + 1] for i in range(dp // 2)]
    flat = stores.reshape((2, 4 * depth, 2 * shape[0]) + shape[1:])
    own = lax.psum_scatter(flat, "dp", scatter_dimension=0, axis_index_groups=groups)
    away, keep = split_units(table, own)
    came = moved(away, to_third)
    away = (keep[depth:].astype(F32) + came[depth:].astype(F32)).astype(BF)
    keep = (keep[:depth].astype(F32) + came[:depth].astype(F32)).astype(BF)
    came = moved(away, to_second)
    line = (keep.astype(F32) + came.astype(F32)).astype(BF)
    total = line[0].astype(F32)
    for step in range(1, depth):
        total = total + moved(line[step], along_z(-step)).astype(F32)
    total = total.reshape((2,) + shape)
    kept = jnp.where(core == 0, total[0], total[1])
    came = moved(jnp.where(core == 0, total[1], total[0]), to_core)
    return jnp.where(core == 0, kept, came), jnp.where(core == 0, came, kept)


def summed_everywhere(array):
    dp, seq = sizes()
    if not paired():
        return lax.psum(array, BOTH)
    steps = [to_core, lambda z, x, c, y: (z, x, c, 1 - y), lambda z, x, c, y: (z, 1 - x, c, y)]
    for target in steps:
        array = array + moved(array, target)
    total = array
    if dp // 4 == 4:
        for bit in (1, 2):
            total = total + moved(total, lambda z, x, c, y, bit=bit: (z ^ bit, x, c, y))
        return total
    for step in range(1, dp // 4):
        total = total + moved(array, along_z(step))
    return total


def passed_along(array, axis, by):
    devices = lax.axis_size(axis)
    pairs = [(i, i + by) for i in range(devices) if 0 <= i + by < devices]
    return lax.ppermute(array, axis, pairs)


def norm_apply(residual_flow, gain_vector, bias_vector):
    centre_of = jnp.mean(residual_flow, axis=-1, keepdims=True)
    centred = residual_flow - centre_of
    spread = jnp.mean(centred * centred, axis=-1, keepdims=True)
    return centred * lax.rsqrt(spread + EPS) * gain_vector + bias_vector


def matmul(first_op, second_op):
    return jnp.dot(first_op, second_op, preferred_element_type=jnp.float32)


def matmul_nt(first_op, second_op):
    return lax.dot_general(
        first_op, second_op, (((1,), (1,)), ((), ())), preferred_element_type=jnp.float32
    )


def matmul_tn(first_op, second_op):
    return lax.dot_general(
        first_op, second_op, (((0,), (0,)), ((), ())), preferred_element_type=jnp.float32
    )


def power_tables(fading_feature_factor, length):
    log_decay = jnp.log(fading_feature_factor)
    places = jnp.arange(length, dtype=jnp.float32)[:, None]
    return (jnp.exp(places * log_decay), jnp.exp(-places * log_decay))


def document_mask(active_token_flags, later):
    breaks = jnp.cumsum(1.0 - active_token_flags, axis=1)
    length = active_token_flags.shape[1]
    places = jnp.arange(length)
    if later:
        order = places[:, None] <= places[None, :]
    else:
        order = places[:, None] >= places[None, :]
    same_doc = breaks[:, :, None] == breaks[:, None, :]
    return (jnp.logical_and(same_doc, order[None]).astype(jnp.float32), breaks)


def masked_sum(mask, terms):
    return jnp.einsum(
        "rts,rsc->rtc",
        mask,
        terms,
        precision=lax.Precision.HIGHEST,
        preferred_element_type=jnp.float32,
    )


def shifted(normed, active_token_flags):
    border = passed_along(normed[:, -1:, :], "seq", 1)
    return jnp.concatenate([border, normed[:, :-1, :]], axis=1) * active_token_flags[:, :, None]


def unshifted(grad_prev, active_token_flags):
    masked = grad_prev * active_token_flags[:, :, None]
    border = passed_along(masked[:, :1, :], "seq", -1)
    return jnp.concatenate([masked[:, 1:, :], border], axis=1)


def mix_back(grads_in, mixing_rows, change):
    grad_normed = jnp.zeros_like(change)
    grad_before = jnp.zeros_like(change)
    grad_list = []
    for slot_idx, grad_part in enumerate(grads_in):
        grad_normed = grad_normed + mixing_rows[slot_idx] * grad_part
        grad_before = grad_before + (1.0 - mixing_rows[slot_idx]) * grad_part
        grad_list.append(jnp.sum(change * grad_part, axis=(0, 1)))
    return (grad_normed, grad_before, jnp.stack(grad_list))


def weighted_kv_forward(
    entering_lookups,
    entering_contents,
    active_token_flags,
    fading_feature_factor,
    reward_feature_factor,
):
    powered_lookups = jnp.exp(entering_lookups)
    reward_scaled = powered_lookups * reward_feature_factor
    length = entering_lookups.shape[1]
    width = entering_lookups.shape[2]
    rising, falling = power_tables(fading_feature_factor, length)
    mask, breaks = document_mask(active_token_flags, False)
    terms = jnp.concatenate(
        [falling * powered_lookups * entering_contents, falling * powered_lookups], axis=2
    )
    summed = masked_sum(mask, terms)
    state_a = rising * summed[:, :, :width]
    state_b = rising * summed[:, :, width:]
    running = rising * fading_feature_factor * (breaks == 0.0).astype(jnp.float32)[:, :, None]
    enter_a, enter_b = entering(running[:, -1], state_a[:, -1], state_b[:, -1], 1)
    whole_a = state_a + running * enter_a[:, None]
    whole_b = state_b + running * enter_b[:, None]
    visited_first = (
        jnp.concatenate([enter_a[:, None], whole_a[:, :-1]], axis=1)
        * active_token_flags[:, :, None]
    )
    visited_second = (
        jnp.concatenate([enter_b[:, None], whole_b[:, :-1]], axis=1)
        * active_token_flags[:, :, None]
    )
    denominator_total = visited_second + reward_scaled
    final_answer = (visited_first + reward_scaled * entering_contents) / denominator_total
    return (
        final_answer,
        (
            visited_first,
            visited_second,
            denominator_total,
            final_answer,
            reward_scaled,
            powered_lookups,
            entering_contents,
            active_token_flags,
        ),
    )


def attention_sum_pullback(grad_out, stored_weighted_kv, fading_feature_factor):
    (
        visited_first,
        visited_second,
        denominator_total,
        final_answer,
        reward_scaled,
        powered_lookups,
        entering_contents,
        active_token_flags,
    ) = stored_weighted_kv
    numerator_cotangent = grad_out / denominator_total
    grad_bottom = -grad_out * final_answer / denominator_total
    length = grad_out.shape[1]
    width = grad_out.shape[2]
    next_live = active_token_flags[:, 1:, None]
    edge_zero = jnp.zeros_like(numerator_cotangent[:, :1])
    feed_a = jnp.concatenate([next_live * numerator_cotangent[:, 1:], edge_zero], axis=1)
    feed_b = jnp.concatenate([next_live * grad_bottom[:, 1:], edge_zero], axis=1)
    rising, falling = power_tables(fading_feature_factor, length)
    mask, breaks = document_mask(active_token_flags, True)
    summed = masked_sum(mask, jnp.concatenate([rising * feed_a, rising * feed_b], axis=2))
    local_a = falling * summed[:, :, :width]
    local_b = falling * summed[:, :, width:]
    running = falling * rising[-1] * (breaks == breaks[:, -1:]).astype(jnp.float32)[:, :, None]
    start_live = active_token_flags[:, 0][:, None]
    chain_m = start_live * fading_feature_factor * running[:, 0]
    chain_a = start_live * (numerator_cotangent[:, 0] + fading_feature_factor * local_a[:, 0])
    chain_b = start_live * (grad_bottom[:, 0] + fading_feature_factor * local_b[:, 0])
    leave_a, leave_b = entering(chain_m, chain_a, chain_b, -1)
    cotangent_first = local_a + running * leave_a[:, None]
    grad_b = local_b + running * leave_b[:, None]
    amplified_cotangent = numerator_cotangent * entering_contents + grad_bottom
    content_cotangent = numerator_cotangent * reward_scaled + powered_lookups * cotangent_first
    lookup_cotangent = amplified_cotangent * reward_scaled + powered_lookups * (
        entering_contents * cotangent_first + grad_b
    )
    reward_cotangent = jnp.sum(amplified_cotangent * reward_scaled, axis=(0, 1))
    fading_cotangent = jnp.sum(
        cotangent_first * visited_first + grad_b * visited_second, axis=(0, 1)
    )
    return (lookup_cotangent, content_cotangent, reward_cotangent, fading_cotangent)


def time_forward(
    residual_flow,
    active_token_flags,
    gain_vector,
    bias_vector,
    mixing_rows,
    fading_feature_factor,
    reward_feature_factor,
    complete_group,
):
    normed, norm_back = jax.vjp(norm_apply, residual_flow, gain_vector, bias_vector)
    before = shifted(normed, active_token_flags)
    change = normed - before
    dim_n = normed.shape[-1]
    flat_k = (before + mixing_rows[0] * change).astype(jnp.bfloat16).reshape(-1, dim_n)
    flat_v = (before + mixing_rows[1] * change).astype(jnp.bfloat16).reshape(-1, dim_n)
    flat_r = (before + mixing_rows[2] * change).astype(jnp.bfloat16).reshape(-1, dim_n)
    lookup_mapping = matmul(flat_k, complete_group[0][0]).reshape(normed.shape)
    content_mapping = matmul(flat_v, complete_group[0][1]).reshape(normed.shape)
    recept = matmul(flat_r, complete_group[0][2])
    attention_sum_result, stored_weighted_kv = weighted_kv_forward(
        lookup_mapping,
        content_mapping,
        active_token_flags,
        fading_feature_factor,
        reward_feature_factor,
    )
    gate_r = jax.nn.sigmoid(recept)
    gated_z = (gate_r * attention_sum_result.reshape(-1, dim_n)).astype(jnp.bfloat16)
    output = matmul(gated_z, complete_group[1])
    kept_vals = (
        norm_back,
        change,
        flat_k,
        flat_v,
        flat_r,
        gate_r,
        attention_sum_result,
        gated_z,
        stored_weighted_kv,
    )
    return (residual_flow + output.reshape(residual_flow.shape), kept_vals)


def time_backward(
    grad_stream, kept_vals, mixing_rows, fading_feature_factor, active_token_flags, complete_group
):
    (
        norm_back,
        change,
        flat_k,
        flat_v,
        flat_r,
        gate_r,
        attention_sum_result,
        gated_z,
        stored_weighted_kv,
    ) = kept_vals
    dim_n = grad_stream.shape[-1]
    grad_output = grad_stream.reshape(-1, dim_n).astype(jnp.bfloat16)
    grad_wout = matmul_tn(gated_z, grad_output)
    grad_gated = matmul_nt(grad_output, complete_group[1])
    weighted_kv_gradient = (grad_gated * gate_r).reshape(attention_sum_result.shape)
    grad_recept = (
        grad_gated * attention_sum_result.reshape(-1, dim_n) * gate_r * (1.0 - gate_r)
    ).astype(jnp.bfloat16)
    lookup_cotangent, content_cotangent, reward_cotangent, fading_cotangent = (
        attention_sum_pullback(weighted_kv_gradient, stored_weighted_kv, fading_feature_factor)
    )
    lookup_cotangent = lookup_cotangent.reshape(-1, dim_n).astype(jnp.bfloat16)
    content_cotangent = content_cotangent.reshape(-1, dim_n).astype(jnp.bfloat16)
    grad_kvr = tuple(
        [
            matmul_tn(flat_k, lookup_cotangent),
            matmul_tn(flat_v, content_cotangent),
            matmul_tn(flat_r, grad_recept),
        ]
    )
    grad_xk = matmul_nt(lookup_cotangent, complete_group[0][0]).reshape(change.shape)
    grad_xv = matmul_nt(content_cotangent, complete_group[0][1]).reshape(change.shape)
    grad_xr = matmul_nt(grad_recept, complete_group[0][2]).reshape(change.shape)
    grad_normed, grad_before, blend_cotangent = mix_back(
        (grad_xk, grad_xv, grad_xr), mixing_rows, change
    )
    grad_normed = grad_normed + unshifted(grad_before, active_token_flags)
    grad_in, scale_term_cotangent, shift_term_cotangent = norm_back(grad_normed)
    return (
        grad_stream + grad_in,
        (
            scale_term_cotangent,
            shift_term_cotangent,
            blend_cotangent,
            fading_cotangent,
            reward_cotangent,
        ),
        (grad_kvr, grad_wout),
    )


def channel_forward(
    residual_flow, active_token_flags, gain_vector, bias_vector, mixing_rows, complete_group
):
    normed, norm_back = jax.vjp(norm_apply, residual_flow, gain_vector, bias_vector)
    before = shifted(normed, active_token_flags)
    change = normed - before
    dim_n = normed.shape[-1]
    flat_k = (before + mixing_rows[0] * change).astype(jnp.bfloat16).reshape(-1, dim_n)
    flat_r = (before + mixing_rows[1] * change).astype(jnp.bfloat16).reshape(-1, dim_n)
    hidden = matmul(flat_k, complete_group[2])
    relu_h = jnp.maximum(hidden, 0.0)
    active = (relu_h * relu_h).astype(jnp.bfloat16)
    carried = matmul(active, complete_group[3])
    gate_r = jax.nn.sigmoid(matmul(flat_r, complete_group[4]))
    output = gate_r * carried
    kept_vals = (norm_back, change, flat_k, flat_r, relu_h, active, carried, gate_r)
    return (residual_flow + output.reshape(residual_flow.shape), kept_vals)


def channel_backward(grad_stream, kept_vals, mixing_rows, active_token_flags, complete_group):
    norm_back, change, flat_k, flat_r, relu_h, active, carried, gate_r = kept_vals
    dim_n = grad_stream.shape[-1]
    grad_flat = grad_stream.reshape(-1, dim_n)
    grad_carried = (grad_flat * gate_r).astype(jnp.bfloat16)
    grad_recept = (grad_flat * carried * gate_r * (1.0 - gate_r)).astype(jnp.bfloat16)
    grad_fval = matmul_tn(active, grad_carried)
    grad_active = matmul_nt(grad_carried, complete_group[3])
    grad_hidden = (grad_active * 2.0 * relu_h).astype(jnp.bfloat16)
    grad_fkey = matmul_tn(flat_k, grad_hidden)
    grad_frec = matmul_tn(flat_r, grad_recept)
    grad_xk = matmul_nt(grad_hidden, complete_group[2]).reshape(change.shape)
    grad_xr = matmul_nt(grad_recept, complete_group[4]).reshape(change.shape)
    grad_normed, grad_before, blend_cotangent = mix_back((grad_xk, grad_xr), mixing_rows, change)
    grad_normed = grad_normed + unshifted(grad_before, active_token_flags)
    grad_in, scale_term_cotangent, shift_term_cotangent = norm_back(grad_normed)
    return (
        grad_stream + grad_in,
        (scale_term_cotangent, shift_term_cotangent, blend_cotangent),
        (grad_fkey, grad_fval, grad_frec),
    )


def entering(chain, end_a, end_b, by):
    ends, chain = jnp.stack([end_a, end_b]), chain[None]
    came = passed_along(ends, "seq", by)
    for _ in range(lax.axis_size("seq") - 2):
        came = passed_along(ends + chain * came, "seq", by)
    return came[0], came[1]


def packed(parts):
    return jnp.concatenate(parts, axis=-2)


def gather_group(core, table, firsts, seconds):
    if not paired():
        pairs = [gather_pair(core, table, a, b) for a, b in zip(firsts, seconds)]
        return [a for a, _ in pairs], [b for _, b in pairs]
    mine, other = gather_pair(core, table, packed(firsts), packed(seconds))
    cuts = np.cumsum([a.shape[0] for a in firsts])[:-1].tolist()
    return jnp.split(mine, cuts, axis=2), jnp.split(other, cuts, axis=2)


def scatter_group(core, table, stores):
    if not paired():
        pairs = [scatter_pair(core, table, s) for s in stores]
        return [a for a, _ in pairs], [b for _, b in pairs]
    first, second = scatter_pair(core, table, packed(stores))
    cuts = np.cumsum([s.shape[3] for s in stores])[:-1].tolist()
    return jnp.split(first, cuts, axis=0), jnp.split(second, cuts, axis=0)


def whole_matrix(store):
    seq, dp, rows, columns = store.shape
    return store.transpose(1, 2, 0, 3).reshape(dp * rows, seq * columns)


def store_of(matrix):
    dp, seq = sizes()
    rows, columns = matrix.shape
    return matrix.reshape(dp, rows // dp, seq, columns // seq).transpose(2, 0, 1, 3)


def channel_width(shard):
    return min(512, shard.shape[1] // 2)


def cut_lookup(shard, grain):
    rows, columns = shard.shape
    width = min(512, columns // 2)
    cut = shard.reshape(rows, columns // (2 * grain), 2, grain).transpose(2, 0, 1, 3)
    cut = cut.reshape(2, rows, columns // 2 // width, width).transpose(0, 2, 1, 3)
    return cut.reshape(2, -1, width)


def join_lookup(first, second, rows, grain):
    width = first.shape[-1]
    cut = jnp.stack([first, second]).reshape(2, -1, rows, width).transpose(0, 2, 1, 3)
    cut = cut.reshape(2, rows, -1, grain).transpose(1, 2, 0, 3)
    return cut.reshape(rows, -1)


def per_device(
    entering_activations,
    document_numbers,
    result_cotangent,
    normalizer_scales,
    normalizer_offsets,
    shift_blend_factors,
    fading_natural_logs_per_feature,
    feature_reward_logs,
    attention_triple_matrix,
    attention_result_matrix,
    channelmix_lookup_matrix,
    channelmix_content_matrix,
    channelmix_accept_matrix,
):
    dp, seq = sizes()
    core = core_of()
    table = unit_tables() if paired() else None
    layer_count = attention_triple_matrix.shape[0]
    border_ids = passed_along(document_numbers[:, -1:] + 1, "seq", 1)
    earlier_ids = jnp.concatenate([border_ids - 1, document_numbers[:, :-1]], axis=1)
    alive = (document_numbers == earlier_ids).astype(jnp.float32)
    decay_all = jnp.exp(-jnp.exp(fading_natural_logs_per_feature))
    reward_all = jnp.exp(feature_reward_logs)
    grain = channelmix_content_matrix.shape[1] // 2
    half_rows = channelmix_accept_matrix.shape[1] // 2

    groups = []
    for depth in range(layer_count):
        triple, result = attention_triple_matrix[depth], attention_result_matrix[depth]
        mine, other = gather_group(core, table, [triple[0], triple[1]], [triple[2], result])
        first = [jnp.where(core == 0, a, b) for a, b in zip(mine, other)]
        second = [jnp.where(core == 0, b, a) for a, b in zip(mine, other)]
        kvr = [whole_matrix(w) for w in (first[0], first[1], second[0])]
        out = whole_matrix(second[1])
        lookup = cut_lookup(channelmix_lookup_matrix[depth], grain)
        content, accept = channelmix_content_matrix[depth], channelmix_accept_matrix[depth]
        mine, other = gather_group(
            core,
            table,
            [lookup[0], content[:grain], accept[:half_rows]],
            [lookup[1], content[grain:], accept[half_rows:]],
        )
        first = [jnp.where(core == 0, a, b) for a, b in zip(mine, other)]
        second = [jnp.where(core == 0, b, a) for a, b in zip(mine, other)]
        rows, width = channelmix_lookup_matrix.shape[1], lookup.shape[-1]
        def of_lookup(store):
            store = store.reshape(seq, dp, -1, rows, width).transpose(1, 3, 0, 2, 4)
            return store.reshape(dp * rows, -1)

        full_lookup = jnp.concatenate([of_lookup(first[0]), of_lookup(second[0])], axis=1)
        full_content = jnp.concatenate([whole_matrix(first[1]), whole_matrix(second[1])], axis=0)
        full_accept = whole_matrix(jnp.concatenate([first[2], second[2]], axis=2))
        groups.append((kvr, out, full_lookup, full_content, full_accept))

    residual_flow = entering_activations.astype(jnp.float32)
    kept_time, kept_chan = [], []
    for depth in range(layer_count):
        residual_flow, kept = time_forward(
            residual_flow,
            alive,
            normalizer_scales[depth, 0],
            normalizer_offsets[depth, 0],
            shift_blend_factors[depth, :3],
            decay_all[depth],
            reward_all[depth],
            groups[depth],
        )
        kept_time.append(kept)
        residual_flow, kept = channel_forward(
            residual_flow,
            alive,
            normalizer_scales[depth, 1],
            normalizer_offsets[depth, 1],
            shift_blend_factors[depth, 3:],
            groups[depth],
        )
        kept_chan.append(kept)
    y_out = residual_flow.astype(jnp.bfloat16)
    grad_stream = result_cotangent.astype(jnp.float32)
    small, large = [None] * layer_count, [None] * layer_count
    for depth in reversed(range(layer_count)):
        grad_stream, small_chan, (grad_fkey, grad_fval, grad_frec) = channel_backward(
            grad_stream, kept_chan[depth], shift_blend_factors[depth, 3:], alive, groups[depth]
        )
        rows, width = channelmix_lookup_matrix.shape[1], min(512, grad_fkey.shape[1] // seq // 2)
        key = grad_fkey.astype(BF).reshape(dp, rows, 2, seq, -1, width)
        key = key.transpose(2, 3, 0, 4, 1, 5).reshape(2, seq, dp, -1, width)
        value = grad_fval.astype(BF).reshape(2, dp, grain, seq, -1).transpose(0, 3, 1, 2, 4)
        take = grad_frec.astype(BF).reshape(dp, 2, half_rows, seq, -1).transpose(1, 3, 0, 2, 4)
        first, second = scatter_group(core, table, [key, value, take])
        chan_shards = (
            join_lookup(first[0], second[0], rows, grain),
            jnp.concatenate([first[1], second[1]]),
            jnp.concatenate([first[2], second[2]]),
        )
        grad_stream, small_time, (grad_kvr, grad_wout) = time_backward(
            grad_stream,
            kept_time[depth],
            shift_blend_factors[depth, :3],
            decay_all[depth],
            alive,
            groups[depth],
        )
        parts = [store_of(g.astype(BF)) for g in (grad_kvr[0], grad_kvr[1], grad_kvr[2], grad_wout)]
        first, second = scatter_group(
            core, table, [jnp.stack([parts[0], parts[2]]), jnp.stack([parts[1], parts[3]])]
        )
        large[depth] = (jnp.stack([first[0], first[1], second[0]]), second[1]) + chan_shards
        grad_td = small_time[3] * decay_all[depth] * -jnp.exp(fading_natural_logs_per_feature[depth])
        small[depth] = jnp.concatenate(
            [
                jnp.stack([small_time[0], small_chan[0], small_time[1], small_chan[1]]),
                small_time[2],
                small_chan[2],
                jnp.stack([grad_td, small_time[4]]),
            ]
        )
    small = summed_everywhere(jnp.stack(small))
    large = [jnp.stack(members) for members in zip(*large)]
    return (
        y_out,
        grad_stream,
        small[:, 0:2],
        small[:, 2:4],
        small[:, 4:9],
        small[:, 9],
        small[:, 10],
        *large,
    )


def solution(mesh):
    return jax.shard_map(
        per_device,
        mesh=mesh,
        in_specs=(
            P("dp", "seq", None),
            P("dp", "seq"),
            P("dp", "seq", None),
            P(),
            P(),
            P(),
            P(),
            P(),
            P(None, None, "dp", "seq"),
            P(None, "dp", "seq"),
            P(None, "dp", "seq"),
            P(None, "dp", "seq"),
            P(None, "dp", "seq"),
        ),
        out_specs=(
            P("dp", "seq", None),
            P("dp", "seq", None),
            P(),
            P(),
            P(),
            P(),
            P(),
            P(None, None, "dp", "seq"),
            P(None, "dp", "seq"),
            P(None, "dp", "seq"),
            P(None, "dp", "seq"),
            P(None, "dp", "seq"),
        ),
        check_vma=False,
    )
```

```python
import jax
import jax.numpy as jnp
import numpy as np
from jax import lax
from jax.experimental import pallas as pl
from jax.experimental.pallas import tpu as pltpu
from jax.sharding import PartitionSpec as P

EPS = 1e-05
BF = jnp.bfloat16
F32 = jnp.float32
BOTH = ("dp", "seq")
VMEM = 58 * 2**20


def sizes():
    return lax.axis_size("dp"), lax.axis_size("seq")


def paired():
    dp, seq = sizes()
    return seq == 2 and dp % 4 == 0


def place(d):
    return d // 4, d // 2 % 2, d % 2


def core_of():
    if not paired():
        return jnp.int32(0)
    return lax.rem(lax.axis_index("dp"), 2)


def moved(array, target):
    dp, seq = sizes()
    pairs = []
    for d in range(dp):
        for y in range(seq):
            z, x, c, y2 = target(*place(d), y)
            pairs.append((d * seq + y, (z * 4 + x * 2 + c) * seq + y2))
    return lax.ppermute(array, BOTH, pairs)


def to_core(z, x, c, y):
    return z, x, 1 - c, y


def to_second(z, x, c, y):
    return (z, 1 - x, c, y) if c == 0 else (z, x, c, 1 - y)


def to_third(z, x, c, y):
    return (z, x, c, 1 - y) if c == 0 else (z, 1 - x, c, y)


def along_z(step):
    depth = sizes()[0] // 4

    def target(z, x, c, y):
        return (z + step) % depth, x, c, y

    return target


def unit_tables():
    dp, seq = sizes()
    depth = dp // 4
    rows = []
    for d in range(dp):
        for y in range(seq):
            z, x, c = place(d)
            half, index = [], []
            for yy in range(2):
                for zz in range(depth):
                    for xx in range(2):
                        dx, dy, dz = xx ^ x, yy ^ y, (z - zz) % depth
                        half.append(dy if c == 0 else dx)
                        index.append((dx if c == 0 else dy) * depth + dz)
            held = []
            for side in range(2):
                own = [i for i, h in zip(index, half) if h == side]
                last, line = own[0], []
                for i, h in zip(index, half):
                    last = i if h == side else last
                    line.append(last)
                held.append(line)
            order = [0] * (4 * depth)
            for unit, (i, h) in enumerate(zip(index, half)):
                order[h * 2 * depth + i] = unit
            rows.append([half, held[0], held[1], order])
    table = jnp.asarray(np.array(rows, np.int32))
    me = lax.axis_index("dp") * seq + lax.axis_index("seq")
    return lax.dynamic_index_in_dim(table, me, 0, keepdims=False)


def arrange(table, own, other):
    units, block = 2 * own.shape[0], (1,) + own.shape[1:]

    def body(table_ref, own_ref, other_ref, out_ref):
        half = table_ref[0, pl.program_id(0)]

        @pl.when(half == 0)
        def _():
            out_ref[...] = own_ref[...]

        @pl.when(half == 1)
        def _():
            out_ref[...] = other_ref[...]

    return pl.pallas_call(
        body,
        grid_spec=pltpu.PrefetchScalarGridSpec(
            num_scalar_prefetch=1,
            grid=(units,),
            in_specs=[
                pl.BlockSpec(block, lambda i, t: (t[1, i], 0, 0)),
                pl.BlockSpec(block, lambda i, t: (t[2, i], 0, 0)),
            ],
            out_specs=pl.BlockSpec(block, lambda i, t: (i, 0, 0)),
        ),
        out_shape=jax.ShapeDtypeStruct((units,) + own.shape[1:], own.dtype),
        compiler_params=pltpu.CompilerParams(vmem_limit_bytes=VMEM),
        cost_estimate=pl.CostEstimate(flops=0, bytes_accessed=4 * own.size * 2, transcendentals=0),
    )(table, own, other)


def split_units(table, whole):
    units, block = whole.shape[0], (1,) + whole.shape[1:]
    half = units // 2

    def body(table_ref, in_ref, away_ref, keep_ref):
        step = pl.program_id(0)

        @pl.when(step < half)
        def _():
            away_ref[...] = in_ref[...]

        @pl.when(step >= half)
        def _():
            keep_ref[...] = in_ref[...]

    shape = jax.ShapeDtypeStruct((half,) + whole.shape[1:], whole.dtype)
    return pl.pallas_call(
        body,
        grid_spec=pltpu.PrefetchScalarGridSpec(
            num_scalar_prefetch=1,
            grid=(units,),
            in_specs=[pl.BlockSpec(block, lambda i, t: (t[3, lax.rem(i + half, units)], 0, 0))],
            out_specs=[
                pl.BlockSpec(block, lambda i, t: (jnp.minimum(i, half - 1), 0, 0)),
                pl.BlockSpec(block, lambda i, t: (jnp.maximum(i - half, 0), 0, 0)),
            ],
        ),
        out_shape=[shape, shape],
        compiler_params=pltpu.CompilerParams(vmem_limit_bytes=VMEM),
        cost_estimate=pl.CostEstimate(flops=0, bytes_accessed=4 * whole.size, transcendentals=0),
    )(table, whole)


def gather_pair(core, table, first, second):
    dp, seq = sizes()
    if not paired():
        return tuple(
            lax.all_gather(part, ("seq", "dp")).reshape((seq, dp) + part.shape)
            for part in (first, second)
        )
    depth = dp // 4
    kept = jnp.where(core == 0, first, second)
    came = moved(jnp.where(core == 0, second, first), to_core)
    pair = jnp.where(core == 0, jnp.stack([kept, came]), jnp.stack([came, kept]))
    line = jnp.stack([pair] + [moved(pair, along_z(step)) for step in range(1, depth)])
    line = line.reshape((depth, -1) + first.shape[1:])
    half = jnp.concatenate([line, moved(line, to_second)])
    mine = arrange(table, half, moved(half, to_third))
    other = moved(mine, to_core)
    shape = (seq, dp) + first.shape
    return mine.reshape(shape), other.reshape(shape)


def scatter_pair(core, table, stores):
    dp, seq = sizes()
    shape = stores.shape[3:]
    if not paired():
        flat = stores.reshape((2, seq * dp) + shape)
        return tuple(
            lax.psum_scatter(flat[i], ("seq", "dp"), scatter_dimension=0).astype(F32)
            for i in range(2)
        )
    depth = dp // 4
    groups = [[2 * i, 2 * i + 1] for i in range(dp // 2)]
    flat = stores.reshape((2, 4 * depth, 2 * shape[0]) + shape[1:])
    own = lax.psum_scatter(flat, "dp", scatter_dimension=0, axis_index_groups=groups)
    away, keep = split_units(table, own)
    came = moved(away, to_third)
    away = (keep[depth:].astype(F32) + came[depth:].astype(F32)).astype(BF)
    keep = (keep[:depth].astype(F32) + came[:depth].astype(F32)).astype(BF)
    came = moved(away, to_second)
    line = (keep.astype(F32) + came.astype(F32)).astype(BF)
    total = line[0].astype(F32)
    for step in range(1, depth):
        total = total + moved(line[step], along_z(-step)).astype(F32)
    total = total.reshape((2,) + shape)
    kept = jnp.where(core == 0, total[0], total[1])
    came = moved(jnp.where(core == 0, total[1], total[0]), to_core)
    return jnp.where(core == 0, kept, came), jnp.where(core == 0, came, kept)


def summed_everywhere(array):
    dp, seq = sizes()
    if not paired():
        return lax.psum(array, BOTH)
    steps = [to_core, lambda z, x, c, y: (z, x, c, 1 - y), lambda z, x, c, y: (z, 1 - x, c, y)]
    for target in steps:
        array = array + moved(array, target)
    total = array
    if dp // 4 == 4:
        for bit in (1, 2):
            total = total + moved(total, lambda z, x, c, y, bit=bit: (z ^ bit, x, c, y))
        return total
    for step in range(1, dp // 4):
        total = total + moved(array, along_z(step))
    return total


def params(**more):
    return pltpu.CompilerParams(vmem_limit_bytes=VMEM, **more)


def cost(flops, bytes_accessed):
    return pl.CostEstimate(flops=int(flops), bytes_accessed=int(bytes_accessed), transcendentals=0)


def held(shape):
    zeros = (0,) * len(shape)
    return pl.BlockSpec(shape, lambda *_: zeros, pipeline_mode=pl.Buffered(1))


def fixed(shape):
    zeros = (0,) * len(shape)
    return pl.BlockSpec(shape, lambda *_: zeros)


SCALAR = pl.BlockSpec(memory_space=pltpu.SMEM)


def dot(a, b):
    return lax.dot_general(a, b, (((1,), (0,)), ((), ())), preferred_element_type=F32)


def dot_nt(a, b):
    return lax.dot_general(a, b, (((1,), (1,)), ((), ())), preferred_element_type=F32)


def dot_tn(a, b):
    return lax.dot_general(a, b, (((0,), (0,)), ((), ())), preferred_element_type=F32)


def split_sum(mask, terms):
    high = terms.astype(BF)
    low = (terms - high.astype(F32)).astype(BF)
    return dot(mask, high) + dot(mask, low)


def centred_norm(s):
    centred = s - jnp.mean(s, axis=-1, keepdims=True)
    rate = lax.rsqrt(jnp.mean(centred * centred, axis=-1, keepdims=True) + EPS)
    return centred * rate, rate


def norm_back(grad, unit, rate, gain):
    grad = grad * gain
    return rate * (
        grad
        - jnp.mean(grad, axis=-1, keepdims=True)
        - unit * jnp.mean(grad * unit, axis=-1, keepdims=True)
    )


def down_one(tile, first):
    rows = lax.broadcasted_iota(jnp.int32, tile.shape, 0)
    return jnp.where(rows == 0, first, pltpu.roll(tile, 1, 0))


def up_one(tile, last):
    size = tile.shape[0]
    rows = lax.broadcasted_iota(jnp.int32, tile.shape, 0)
    return jnp.where(rows == size - 1, last, pltpu.roll(tile, size - 1, 0))


def summed_rows(tile):
    return jnp.sum(tile, axis=0, keepdims=True)


def times(x, store, lo, hi, out_ref, rows=slice(None)):
    seq, dp, _, columns = store.shape
    for y in range(seq):
        weight = store[y, :, lo:hi, :].reshape(dp * (hi - lo), columns)
        out_ref[rows, y * columns : (y + 1) * columns] = dot(x, weight)


def times_back(g, store, lo, hi):
    seq, dp, _, columns = store.shape
    total = None
    for y in range(seq):
        weight = store[y, :, lo:hi, :].reshape(dp * (hi - lo), columns)
        part = dot_nt(g[:, y * columns : (y + 1) * columns], weight)
        total = part if total is None else total + part
    return total


def by_core(core_ref, mine, other, run):
    @pl.when(core_ref[0] == 0)
    def _():
        run(mine, other)

    @pl.when(core_ref[0] != 0)
    def _():
        run(other, mine)


def tile_rows(length):
    return min(256, length)


ALIVE, ENTERS, TAIL, HEAD, LEAVES = range(5)


def col(marks, which):
    return marks[:, which : which + 1]


def token_marks(document_numbers, earlier):
    rows, length = document_numbers.shape
    tile = tile_rows(length)
    tiles = document_numbers.reshape(rows, length // tile, tile)
    before = earlier.reshape(tiles.shape)[:, :, :1]
    marks = [
        document_numbers == earlier,
        (tiles == before).reshape(rows, length),
        document_numbers == document_numbers[:, -1:],
        document_numbers == document_numbers[:, :1],
        (tiles == tiles[:, :, -1:]).reshape(rows, length),
        jnp.zeros_like(document_numbers, dtype=bool),
        jnp.zeros_like(document_numbers, dtype=bool),
    ]
    marks = [m.astype(F32) for m in marks] + [document_numbers.astype(F32)]
    marks = jnp.stack(marks, axis=-1).reshape(rows * length, 8)
    lines = document_numbers.astype(F32).reshape(rows * length // tile, 1, tile)
    return marks, lines


def time_in(core, s, before, marks, gain, bias, mix, rate, mine, other, length):
    tokens, width = s.shape
    tile = tile_rows(length)
    per_run = length // tile
    runs = tokens // length

    def body(
        core_ref, s_ref, before_ref, marks_ref, gain_ref, bias_ref, mix_ref, rate_ref,
        mine_ref, other_ref,
        xk_ref, xv_ref, xr_ref, k_ref, v_ref, r_ref, end_ref, lead_ref, carry_ref,
    ):
        step = pl.program_id(0)
        run, part = lax.div(step, per_run), lax.rem(step, per_run)
        unit, _ = centred_norm(s_ref[...].astype(F32))
        normed = unit * gain_ref[...] + bias_ref[...]

        @pl.when(part == 0)
        def _():
            carry_ref[...] = before_ref[pl.ds(run, 1), :]
            end_ref[pl.ds(run, 1)] = jnp.zeros((1, 2, width), F32)

        lead_ref[0] = carry_ref[...]
        shifted = down_one(normed, carry_ref[...]) * col(marks_ref[...], ALIVE)
        carry_ref[...] = normed[tile - 1 :, :]
        change = normed - shifted
        xk_ref[...] = (shifted + mix_ref[0:1, :] * change).astype(BF)
        xv_ref[...] = (shifted + mix_ref[1:2, :] * change).astype(BF)
        xr_ref[...] = (shifted + mix_ref[2:3, :] * change).astype(BF)

        def project(first, second):
            rows = first.shape[2] // 2
            times(xk_ref[...], first, 0, rows, k_ref)
            times(xv_ref[...], first, rows, 2 * rows, v_ref)
            times(xr_ref[...], second, 0, rows, r_ref)

        by_core(core_ref, mine_ref, other_ref, project)
        places = lax.broadcasted_iota(jnp.int32, (tile, 1), 0).astype(F32)
        left = (length - 1 - part * tile).astype(F32) - places
        weight = jnp.exp(k_ref[...] - left * rate_ref[...]) * col(marks_ref[...], TAIL)
        ends = jnp.concatenate([summed_rows(weight * v_ref[...]), summed_rows(weight)], axis=0)
        end_ref[pl.ds(run, 1)] += ends[None]

    block = pl.BlockSpec((tile, width), lambda i: (i, 0))
    half, full = jax.ShapeDtypeStruct((tokens, width), BF), jax.ShapeDtypeStruct((tokens, width), F32)
    return pl.pallas_call(
        body,
        grid=(tokens // tile,),
        in_specs=[
            SCALAR, block, fixed(before.shape), pl.BlockSpec((tile, 8), lambda i: (i, 0)),
            fixed(gain.shape), fixed(bias.shape), fixed(mix.shape), fixed(rate.shape),
            held(mine.shape), held(other.shape),
        ],
        out_specs=[block] * 6 + [fixed((runs, 2, width)), pl.BlockSpec((1, 1, width), lambda i: (i, 0, 0))],
        out_shape=[half] * 3 + [full] * 3 + [
            jax.ShapeDtypeStruct((runs, 2, width), F32),
            jax.ShapeDtypeStruct((tokens // tile, 1, width), F32),
        ],
        scratch_shapes=[pltpu.VMEM((1, width), F32)],
        compiler_params=params(),
        cost_estimate=cost(6 * tokens * width * width, 22 * tokens * width + 4 * mine.size),
    )(core, s, before, marks, gain, bias, mix, rate, mine, other)


def time_out(core, s, k, v, r, enter, marks, lines, rate, bonus, mine, other, length):
    tokens, width = s.shape
    tile = tile_rows(length)
    per_run = length // tile

    def body(
        core_ref, s_ref, k_ref, v_ref, r_ref, enter_ref, marks_ref, line_ref, rate_ref, bonus_ref,
        mine_ref, other_ref, z_ref, sa_ref, sb_ref, out_ref, state_ref,
    ):
        step = pl.program_id(0)
        run, part = lax.div(step, per_run), lax.rem(step, per_run)

        @pl.when(part == 0)
        def _():
            state_ref[...] = enter_ref[pl.ds(run, 1)][0]

        marks = marks_ref[...]
        places = lax.broadcasted_iota(jnp.int32, (tile, 1), 0).astype(F32)
        spread = places * rate_ref[...]
        falling, decay = jnp.exp(-spread), jnp.exp(-rate_ref[...])
        powered = jnp.exp(k_ref[...])
        content = v_ref[...]
        raised = jnp.exp(k_ref[...] + spread)
        at = lax.broadcasted_iota(jnp.int32, (tile, tile), 0)
        source = lax.broadcasted_iota(jnp.int32, (tile, tile), 1)
        same = col(marks, 7) == line_ref[0]
        mask = jnp.where(jnp.logical_and(same, source < at), 1.0, 0.0).astype(BF)
        carried = falling * col(marks, ENTERS)
        ahead = falling * jnp.exp(rate_ref[...])
        state_a = ahead * split_sum(mask, raised * content) + carried * state_ref[0:1, :]
        state_b = ahead * split_sum(mask, raised) + carried * state_ref[1:2, :]
        sa_ref[...] = state_a
        sb_ref[...] = state_b
        state_ref[0:1, :] = decay * state_a[tile - 1 :] + (powered * content)[tile - 1 :]
        state_ref[1:2, :] = decay * state_b[tile - 1 :] + powered[tile - 1 :]
        scaled = powered * bonus_ref[...]
        answer = (state_a + scaled * content) / (state_b + scaled)
        z_ref[...] = (jax.nn.sigmoid(r_ref[...]) * answer).astype(BF)

        def project(first, second):
            rows = first.shape[2] // 2
            times(z_ref[...], second, rows, 2 * rows, out_ref)

        by_core(core_ref, mine_ref, other_ref, project)
        out_ref[...] += s_ref[...].astype(F32)

    block = pl.BlockSpec((tile, width), lambda i: (i, 0))
    half, full = jax.ShapeDtypeStruct((tokens, width), BF), jax.ShapeDtypeStruct((tokens, width), F32)
    return pl.pallas_call(
        body,
        grid=(tokens // tile,),
        in_specs=[
            SCALAR, block, block, block, block, fixed(enter.shape),
            pl.BlockSpec((tile, 8), lambda i: (i, 0)), pl.BlockSpec((1, 1, tile), lambda i: (i, 0, 0)),
            fixed(rate.shape), fixed(bonus.shape), held(mine.shape), held(other.shape),
        ],
        out_specs=[block] * 4,
        out_shape=[half, full, full, full],
        scratch_shapes=[pltpu.VMEM((2, width), F32)],
        compiler_params=params(),
        cost_estimate=cost(4 * tokens * width * width, 30 * tokens * width + 4 * mine.size),
    )(core, s, k, v, r, enter, marks, lines, rate, bonus, mine, other)


def lookup_block(store, rows, blocks, step):
    seq, dp, _, width = store.shape
    return pl.BlockSpec(
        (1, dp, rows, width), lambda i: (lax.div(step(i), blocks), 0, lax.rem(step(i), blocks), 0)
    )


def content_block(store, grain, at, group, step):
    seq, _, _, columns = store.shape
    return pl.BlockSpec((seq, group, grain, columns), lambda i: (0, step(i), at // grain, 0))


class Cut:
    def __init__(self, lookup, content, lookup_rows, grain):
        store, _ = lookup
        seq, dp, _, self.width = store.shape
        self.rows, self.grain = lookup_rows, grain
        self.group = self.width // grain
        self.steps = dp // self.group
        self.blocks = self.steps // seq
        self.at = content[1]

    def specs(self, lookup, content, step):
        return [
            lookup_block(lookup[0], self.rows, self.blocks, step),
            content_block(content[0], self.grain, self.at, self.group, step),
        ]


def hidden_step(x_ref, lookup_ref, content_ref, act_ref, total_ref, first):
    tokens = x_ref.shape[0]
    tile = min(256, tokens)
    _, dp, rows, width = lookup_ref.shape
    seq, group, grain, columns = content_ref.shape
    up = lookup_ref[0].reshape(dp * rows, width)
    for t in range(0, tokens, tile):
        hidden = jnp.maximum(dot(x_ref[t : t + tile, :], up), 0.0)
        act = (hidden * hidden).astype(BF)
        act_ref[0, t : t + tile, :] = act
        for y in range(seq):
            part = dot(act, content_ref[y].reshape(group * grain, columns))
            where = (slice(t, t + tile), slice(y * columns, (y + 1) * columns))
            total_ref[where] = part if first else total_ref[where] + part


def channel_one(s, before, marks, gain, bias, mix, lookup, content, cut, length):
    tokens, width = s.shape
    tile = tile_rows(length)
    tiles, per_run = tokens // tile, length // tile

    def body(
        s_ref, before_ref, marks_ref, gain_ref, bias_ref, mix_ref, lookup_ref, content_ref,
        xk_ref, xr_ref, lead_ref, act_ref, total_ref,
    ):
        @pl.when(pl.program_id(0) == 0)
        def _():
            last = None
            for i in range(tiles):
                rows = slice(i * tile, (i + 1) * tile)
                unit, _ = centred_norm(s_ref[rows, :])
                normed = unit * gain_ref[...] + bias_ref[...]
                if i % per_run == 0:
                    last = before_ref[i // per_run : i // per_run + 1, :]
                lead_ref[i] = last
                shifted = down_one(normed, last) * col(marks_ref[rows, :], ALIVE)
                last = normed[tile - 1 :, :]
                change = normed - shifted
                xk_ref[rows, :] = (shifted + mix_ref[0:1, :] * change).astype(BF)
                xr_ref[rows, :] = (shifted + mix_ref[1:2, :] * change).astype(BF)
            hidden_step(xk_ref, lookup_ref, content_ref, act_ref, total_ref, True)

        @pl.when(pl.program_id(0) > 0)
        def _():
            hidden_step(xk_ref, lookup_ref, content_ref, act_ref, total_ref, False)

    half, full = jax.ShapeDtypeStruct((tokens, width), BF), jax.ShapeDtypeStruct((tokens, width), F32)
    return pl.pallas_call(
        body,
        grid=(cut.steps,),
        in_specs=[
            held(s.shape), fixed(before.shape), held(marks.shape),
            fixed(gain.shape), fixed(bias.shape), fixed(mix.shape),
        ] + cut.specs(lookup, content, lambda i: i),
        out_specs=[
            fixed((tokens, width)), fixed((tokens, width)), fixed((tiles, 1, width)),
            pl.BlockSpec((1, tokens, cut.width), lambda i: (i, 0, 0)), fixed((tokens, width)),
        ],
        out_shape=[
            half, half, jax.ShapeDtypeStruct((tiles, 1, width), F32),
            jax.ShapeDtypeStruct((cut.steps, tokens, cut.width), BF), full,
        ],
        compiler_params=params(),
        cost_estimate=cost(
            4 * tokens * width * cut.width * cut.steps,
            14 * tokens * width + cut.steps * cut.width * (4 * width + 2 * tokens),
        ),
    )(s, before, marks, gain, bias, mix, lookup[0], content[0])


def channel_two(s, xk, xr, total, lookup, content, accept, cut, kind):
    tokens, width = s.shape
    tile = min(256, tokens)

    def body(
        s_ref, xk_ref, xr_ref, total_ref, accept_ref, lookup_ref, content_ref,
        act_ref, carried_ref, gate_ref, out_ref, sum_ref, take_ref,
    ):
        @pl.when(pl.program_id(0) == 0)
        def _():
            sum_ref[...] = total_ref[...]

        hidden_step(xk_ref, lookup_ref, content_ref, act_ref, sum_ref, False)

        @pl.when(pl.program_id(0) == cut.steps - 1)
        def _():
            for t in range(0, tokens, tile):
                rows = slice(t, t + tile)
                times(xr_ref[rows, :], accept_ref, 0, accept_ref.shape[2], take_ref)
                gate = jax.nn.sigmoid(take_ref[...])
                carried = sum_ref[rows, :]
                gate_ref[rows, :] = gate.astype(BF)
                carried_ref[rows, :] = carried.astype(BF)
                out_ref[rows, :] = (s_ref[rows, :] + gate * carried).astype(kind)

    half = jax.ShapeDtypeStruct((tokens, width), BF)
    return pl.pallas_call(
        body,
        grid=(cut.steps,),
        in_specs=[held(s.shape), held(xk.shape), held(xr.shape), held(total.shape), held(accept.shape)]
        + cut.specs(lookup, content, lambda i: i),
        out_specs=[pl.BlockSpec((1, tokens, cut.width), lambda i: (i, 0, 0))] + [fixed((tokens, width))] * 3,
        out_shape=[
            jax.ShapeDtypeStruct((cut.steps, tokens, cut.width), BF), half, half,
            jax.ShapeDtypeStruct((tokens, width), kind),
        ],
        scratch_shapes=[pltpu.VMEM((tokens, width), F32), pltpu.VMEM((tile, width), F32)],
        compiler_params=params(),
        cost_estimate=cost(
            4 * tokens * width * cut.width * cut.steps + 2 * tokens * width * width,
            20 * tokens * width + cut.steps * cut.width * (4 * width + 2 * tokens) + 2 * accept.size,
        ),
    )(s, xk, xr, total, accept, lookup[0], content[0])


def mixed_back(grads, s, lead, alive, gain, bias, mix_ref, after):
    unit, rate = centred_norm(s)
    normed = unit * gain + bias
    change = normed - down_one(normed, lead) * alive
    own, before, mixes = None, None, []
    for j, grad in enumerate(grads):
        mix = mix_ref[j : j + 1, :]
        a, b = mix * grad, (1.0 - mix) * grad
        own, before = (a, b) if own is None else (own + a, before + b)
        mixes.append(summed_rows(change * grad))
    before = before * alive
    grad = own + up_one(before, after)
    small = [summed_rows(grad * unit), summed_rows(grad)] + mixes
    return norm_back(grad, unit, rate, gain), before[0:1, :], small


def channel_back(
    core, g, fix, s, lead, marks, gain, bias, mix, gate, carried, xk, xr, acts, lookups, contents, accept,
    cut, length, packing,
):
    tokens, width = s.shape
    tile = tile_rows(length)
    tiles, per_run = tokens // tile, length // tile
    steps = cut.steps
    shapes, spots = packing
    seq, dp = accept.shape[:2]
    columns = width // seq
    half_rows = accept.shape[2] // 2
    last = 2 * steps - 1
    slots = len(shapes)

    def body(
        core_ref, g_ref, fix_ref, s_ref, lead_ref, marks_ref, gain_ref, bias_ref, mix_ref,
        gate_ref, carried_ref, xk_ref, xr_ref, act0_ref, act1_ref, accept_ref,
        lookup0_ref, content0_ref, lookup1_ref, content1_ref, *rest,
    ):
        outs, rest = rest[:slots], rest[slots:]
        out_ref, edge_ref, small_ref, gc_ref, gr_ref, sum_ref, key_ref, val_ref, take_ref, sem, stage_ref = rest
        lookup_out, content_out, accept_out = outs if slots == 3 else (outs[0],) * 3
        step = pl.program_id(0)
        slot = lax.rem(step, 2)

        def copies(which, store, q):
            y, block = lax.div(q, cut.blocks), lax.rem(q, cut.blocks)
            rows = pl.ds(pl.multiple_of(spots[0] + block * cut.rows, 16), cut.rows)
            key = pltpu.make_async_copy(
                key_ref.at[which], lookup_out.at[store, y, :, rows, :], sem.at[which, 0]
            )
            parts = pl.ds(q * cut.group, cut.group)
            rows = pl.ds(spots[1], cut.grain)
            val = pltpu.make_async_copy(
                val_ref.at[which], content_out.at[store, :, parts, rows, :], sem.at[which, 1]
            )
            return key, val

        def store_of_step(i):
            core = core_ref[0]
            return jnp.where(i < steps, core, 1 - core), lax.rem(i, steps)

        @pl.when(step == 0)
        def _():
            for i in range(tiles):
                rows = slice(i * tile, (i + 1) * tile)
                grad = g_ref[rows, :].astype(F32)
                if (i + 1) % per_run == 0:
                    at = lax.broadcasted_iota(jnp.int32, grad.shape, 0)
                    run = i // per_run
                    grad = jnp.where(at == tile - 1, grad + fix_ref[run : run + 1, :], grad)
                gate = gate_ref[rows, :].astype(F32)
                passed = grad * gate
                out_ref[rows, :] = grad
                gc_ref[rows, :] = passed.astype(BF)
                gr_ref[rows, :] = (passed * carried_ref[rows, :].astype(F32) * (1.0 - gate)).astype(BF)

        @pl.when(step >= 2)
        def _():
            for copy in copies(slot, *store_of_step(step - 2)):
                copy.wait()

        def work(act_ref, lookup_ref, content_ref, first):
            up = lookup_ref[0].reshape(dp * cut.rows, cut.width)
            size = min(256, tokens)
            for t in range(0, tokens, size):
                rows = slice(t, t + size)
                act = act_ref[0, rows, :].astype(F32)
                grad = None
                for y in range(seq):
                    part = dot_nt(
                        gc_ref[rows, y * columns : (y + 1) * columns],
                        content_ref[y].reshape(cut.group * cut.grain, columns),
                    )
                    grad = part if grad is None else grad + part
                grad = (grad * (2.0 * jnp.sqrt(act))).astype(BF)
                take_ref[rows, :] = grad
                part = dot_nt(grad, up)
                sum_ref[rows, :] = part if first else sum_ref[rows, :] + part
            key = dot_tn(xk_ref[...], take_ref[...])
            key_ref[slot] = key.astype(BF).reshape(dp, cut.rows, cut.width)
            for y in range(seq):
                val = dot_tn(act_ref[0], gc_ref[:, y * columns : (y + 1) * columns])
                val_ref[slot, y] = val.astype(BF).reshape(cut.group, cut.grain, columns)

        @pl.when(step == 0)
        def _():
            work(act0_ref, lookup0_ref, content0_ref, True)

        @pl.when(jnp.logical_and(step > 0, step < steps))
        def _():
            work(act0_ref, lookup0_ref, content0_ref, False)

        @pl.when(step >= steps)
        def _():
            work(act1_ref, lookup1_ref, content1_ref, False)

        for copy in copies(slot, *store_of_step(step)):
            copy.start()

        @pl.when(step == last)
        def _():
            for copy in copies(1 - slot, *store_of_step(step - 1)):
                copy.wait()
            for copy in copies(slot, *store_of_step(step)):
                copy.wait()
            rows = pl.ds(spots[2], half_rows)
            takes = []
            for y in range(seq):
                grad = dot_tn(xr_ref[...], gr_ref[:, y * columns : (y + 1) * columns])
                grad = grad.astype(BF).reshape(dp, 2 * half_rows, columns)
                for h in range(2):
                    buffer = stage_ref.at[h, y]
                    stage_ref[h, y] = grad[:, h * half_rows : (h + 1) * half_rows, :]
                    takes.append(
                        pltpu.make_async_copy(buffer, accept_out.at[h, y, :, rows, :], sem.at[h, 2 + y])
                    )
                    takes[-1].start()
            after = None
            small = None
            for i in reversed(range(tiles)):
                at = slice(i * tile, (i + 1) * tile)
                if (i + 1) % per_run == 0:
                    after = jnp.zeros((1, width), F32)
                grads = [sum_ref[at, :], times_back(gr_ref[at, :], accept_ref, 0, 2 * half_rows)]
                add, after, more = mixed_back(
                    grads, s_ref[at, :], lead_ref[i], col(marks_ref[at, :], ALIVE),
                    gain_ref[...], bias_ref[...], mix_ref, after,
                )
                out_ref[at, :] += add
                small = more if small is None else [a + b for a, b in zip(small, more)]
                if i % per_run == 0:
                    edge_ref[i // per_run : i // per_run + 1, :] = after
            for j, line in enumerate(small):
                small_ref[j : j + 1, :] = line
            for copy in takes:
                copy.wait()

    own = lambda i: jnp.minimum(i, steps - 1)
    partner = lambda i: jnp.maximum(i - steps, 0)
    act = lambda step: pl.BlockSpec((1, tokens, cut.width), lambda i: (step(i), 0, 0))
    any_space = pl.BlockSpec(memory_space=pl.ANY)
    return pl.pallas_call(
        body,
        grid=(2 * steps,),
        in_specs=[
            SCALAR, held(g.shape), fixed(fix.shape), held(s.shape), fixed(lead.shape), held(marks.shape),
            fixed(gain.shape), fixed(bias.shape), fixed(mix.shape), held(gate.shape), held(carried.shape),
            held(xk.shape), held(xr.shape), act(own), act(partner), held(accept.shape),
        ] + cut.specs(lookups[0], contents[0], own) + cut.specs(lookups[1], contents[1], partner),
        out_specs=[any_space] * slots + [fixed((tokens, width)), fixed(fix.shape), fixed((4, width))],
        out_shape=[jax.ShapeDtypeStruct(shape, BF) for shape in shapes] + [
            jax.ShapeDtypeStruct((tokens, width), F32), jax.ShapeDtypeStruct(fix.shape, F32),
            jax.ShapeDtypeStruct((4, width), F32),
        ],
        scratch_shapes=[
            pltpu.VMEM((tokens, width), BF), pltpu.VMEM((tokens, width), BF),
            pltpu.VMEM((tokens, width), F32),
            pltpu.VMEM((2, dp, cut.rows, cut.width), BF),
            pltpu.VMEM((2, seq, cut.group, cut.grain, columns), BF),
            pltpu.VMEM((tokens, cut.width), BF),
            pltpu.SemaphoreType.DMA((2, 2 + seq)),
            pltpu.VMEM((2, seq, dp, half_rows, columns), BF),
        ],
        compiler_params=params(),
        cost_estimate=cost(
            16 * tokens * width * cut.width * steps + 4 * tokens * width * width,
            30 * tokens * width + 2 * steps * cut.width * (8 * width + 2 * tokens),
        ),
    )(
        core, g, fix, s, lead, marks, gain, bias, mix, gate, carried, xk, xr, *acts, accept,
        lookups[0][0], contents[0][0], lookups[1][0], contents[1][0],
    )


def out_back(core, g, fix, k, v, r, sa, sb, marks, rate, bonus, mine, other, length):
    tokens, width = g.shape
    tile = tile_rows(length)
    per_run = length // tile
    runs = tokens // length

    def body(
        core_ref, g_ref, fix_ref, k_ref, v_ref, r_ref, sa_ref, sb_ref, marks_ref, rate_ref, bonus_ref,
        mine_ref, other_ref, go_ref, gr_ref, gn_ref, gd_ref, chain_ref, gz_ref,
    ):
        step = pl.program_id(0)
        run, part = lax.div(step, per_run), lax.rem(step, per_run)
        grad = g_ref[...]
        at = lax.broadcasted_iota(jnp.int32, grad.shape, 0)
        hit = jnp.logical_and(at == tile - 1, part == per_run - 1)
        go_ref[...] = jnp.where(hit, grad + fix_ref[pl.ds(run, 1), :], grad).astype(BF)

        def project(first, second):
            rows = first.shape[2] // 2
            gz_ref[...] = times_back(go_ref[...], second, rows, 2 * rows)

        by_core(core_ref, mine_ref, other_ref, project)
        gate = jax.nn.sigmoid(r_ref[...])
        scaled = jnp.exp(k_ref[...]) * bonus_ref[...]
        inverse = 1.0 / (sb_ref[...] + scaled)
        answer = (sa_ref[...] + scaled * v_ref[...]) * inverse
        gated = gz_ref[...] * gate
        gr_ref[...] = (gated * answer * (1.0 - gate)).astype(BF)
        gn = gated * inverse
        gd = -gn * answer
        gn_ref[...] = gn
        gd_ref[...] = gd

        @pl.when(part == 0)
        def _():
            chain_ref[pl.ds(run, 1)] = jnp.zeros((1, 2, width), F32)

        places = (lax.broadcasted_iota(jnp.int32, (tile, 1), 0) + part * tile).astype(F32)
        weight = jnp.exp(-places * rate_ref[...]) * col(marks_ref[...], HEAD)
        sums = jnp.concatenate([summed_rows(weight * gn), summed_rows(weight * gd)], axis=0)
        chain_ref[pl.ds(run, 1)] += sums[None]

    block = pl.BlockSpec((tile, width), lambda i: (i, 0))
    half, full = jax.ShapeDtypeStruct((tokens, width), BF), jax.ShapeDtypeStruct((tokens, width), F32)
    return pl.pallas_call(
        body,
        grid=(tokens // tile,),
        in_specs=[
            SCALAR, block, fixed(fix.shape), block, block, block, block, block,
            pl.BlockSpec((tile, 8), lambda i: (i, 0)), fixed(rate.shape), fixed(bonus.shape),
            held(mine.shape), held(other.shape),
        ],
        out_specs=[block] * 4 + [fixed((runs, 2, width))],
        out_shape=[half, half, full, full, jax.ShapeDtypeStruct((runs, 2, width), F32)],
        scratch_shapes=[pltpu.VMEM((tile, width), F32)],
        compiler_params=params(),
        cost_estimate=cost(2 * tokens * width * width, 36 * tokens * width + 4 * mine.size),
    )(core, g, fix, k, v, r, sa, sb, marks, rate, bonus, mine, other)


def time_back(
    core, g, fix, s, lead, k, v, sa, sb, gn, gd, gr, leave, marks, lines, gain, bias, mix, rate, bonus,
    mine, other, length,
):
    tokens, width = s.shape
    tile = tile_rows(length)
    tiles, per_run = tokens // tile, length // tile
    runs = tokens // length

    def body(
        core_ref, g_ref, fix_ref, s_ref, lead_ref, k_ref, v_ref, sa_ref, sb_ref, gn_ref, gd_ref, gr_ref,
        leave_ref, marks_ref, line_ref, gain_ref, bias_ref, mix_ref, rate_ref, bonus_ref,
        mine_ref, other_ref, gk_ref, gv_ref, out_ref, edge_ref, small_ref,
        state_ref, after_ref, xk_ref, xv_ref, xr_ref,
    ):
        step = pl.program_id(0)
        i = tiles - 1 - step
        run, part = lax.div(i, per_run), lax.rem(i, per_run)

        @pl.when(part == per_run - 1)
        def _():
            state_ref[...] = leave_ref[pl.ds(run, 1)][0]
            after_ref[...] = jnp.zeros((1, width), F32)

        marks = marks_ref[...]
        alive = col(marks, ALIVE)
        places = lax.broadcasted_iota(jnp.int32, (tile, 1), 0).astype(F32)
        spread = places * rate_ref[...]
        falling, decay = jnp.exp(-spread), jnp.exp(-rate_ref[...])
        rising = jnp.exp(spread + rate_ref[...])
        at = lax.broadcasted_iota(jnp.int32, (tile, tile), 0)
        source = lax.broadcasted_iota(jnp.int32, (tile, tile), 1)
        same = col(marks, 7) == line_ref[0]
        mask = jnp.where(jnp.logical_and(same, source > at), 1.0, 0.0).astype(BF)
        gn, gd = gn_ref[...], gd_ref[...]
        carried = jnp.exp(spread - (tile - 1) * rate_ref[...]) * col(marks, LEAVES)
        ga = rising * split_sum(mask, falling * gn) + carried * state_ref[0:1, :]
        gb = rising * split_sum(mask, falling * gd) + carried * state_ref[1:2, :]
        first = alive[0:1, :]
        state_ref[0:1, :] = first * (gn[0:1, :] + decay * ga[0:1, :])
        state_ref[1:2, :] = first * (gd[0:1, :] + decay * gb[0:1, :])
        powered, content = jnp.exp(k_ref[...]), v_ref[...]
        scaled = powered * bonus_ref[...]
        reward = (gn * content + gd) * scaled
        gv_ref[...] = (gn * scaled + powered * ga).astype(BF)
        gk_ref[...] = (reward + powered * (content * ga + gb)).astype(BF)
        sums = [summed_rows(ga * sa_ref[...] + gb * sb_ref[...]), summed_rows(reward)]

        def project(first, second):
            rows = first.shape[2] // 2
            xk_ref[...] = times_back(gk_ref[...], first, 0, rows)
            xv_ref[...] = times_back(gv_ref[...], first, rows, 2 * rows)
            xr_ref[...] = times_back(gr_ref[...], second, 0, rows)

        by_core(core_ref, mine_ref, other_ref, project)
        grads = [xk_ref[...], xv_ref[...], xr_ref[...]]
        add, after, small = mixed_back(
            grads, s_ref[...].astype(F32), lead_ref[0], alive, gain_ref[...], bias_ref[...], mix_ref,
            after_ref[...],
        )
        after_ref[...] = after
        grad = g_ref[...]
        row = lax.broadcasted_iota(jnp.int32, grad.shape, 0)
        hit = jnp.logical_and(row == tile - 1, part == per_run - 1)
        out_ref[...] = jnp.where(hit, grad + fix_ref[pl.ds(run, 1), :], grad) + add
        edge_ref[pl.ds(run, 1), :] = after

        @pl.when(step == 0)
        def _():
            small_ref[...] = jnp.zeros_like(small_ref)

        for j, line in enumerate(small + sums):
            small_ref[j : j + 1, :] += line

    back = lambda i: tiles - 1 - i
    block = pl.BlockSpec((tile, width), lambda i: (back(i), 0))
    half, full = jax.ShapeDtypeStruct((tokens, width), BF), jax.ShapeDtypeStruct((tokens, width), F32)
    return pl.pallas_call(
        body,
        grid=(tiles,),
        in_specs=[
            SCALAR, block, fixed(fix.shape), block, pl.BlockSpec((1, 1, width), lambda i: (back(i), 0, 0)),
            block, block, block, block, block, block, block, fixed(leave.shape),
            pl.BlockSpec((tile, 8), lambda i: (back(i), 0)),
            pl.BlockSpec((1, 1, tile), lambda i: (back(i), 0, 0)),
            fixed(gain.shape), fixed(bias.shape), fixed(mix.shape), fixed(rate.shape), fixed(bonus.shape),
            held(mine.shape), held(other.shape),
        ],
        out_specs=[block, block, block, fixed(fix.shape), fixed((7, width))],
        out_shape=[
            half, half, full, jax.ShapeDtypeStruct(fix.shape, F32), jax.ShapeDtypeStruct((7, width), F32),
        ],
        scratch_shapes=[
            pltpu.VMEM((2, width), F32), pltpu.VMEM((1, width), F32),
            pltpu.VMEM((tile, width), F32), pltpu.VMEM((tile, width), F32), pltpu.VMEM((tile, width), F32),
        ],
        compiler_params=params(),
        cost_estimate=cost(8 * tokens * width * width, 46 * tokens * width + 4 * mine.size),
    )(
        core, g, fix, s, lead, k, v, sa, sb, gn, gd, gr, leave, marks, lines, gain, bias, mix, rate, bonus,
        mine, other,
    )


def weight_grads(first, second, grads):
    dp, seq = sizes()
    tokens, width = grads[0].shape
    rows, columns = width // dp, width // seq
    pairs = list(zip(first + second, grads))

    def body(*refs):
        ins, (out_ref, x_ref, g_ref, sem) = refs[: 2 * len(pairs)], refs[2 * len(pairs) :]
        which, y = pl.program_id(0), pl.program_id(1)
        slot = lax.rem(which, 2)

        def copies(i):
            return (
                pltpu.make_async_copy(ins[2 * i], x_ref.at[i % 2], sem.at[i % 2, 0]),
                pltpu.make_async_copy(ins[2 * i + 1], g_ref.at[i % 2], sem.at[i % 2, 1]),
            )

        @pl.when(jnp.logical_and(which == 0, y == 0))
        def _():
            for copy in copies(0):
                copy.start()

        for i in range(len(pairs)):

            @pl.when(jnp.logical_and(which == i, y == 0))
            def _(i=i):
                for copy in copies(i):
                    copy.wait()
                if i + 1 < len(pairs):
                    for copy in copies(i + 1):
                        copy.start()

        at = pl.ds(pl.multiple_of(y * columns, columns), columns)
        grad = dot_tn(x_ref[slot], g_ref[slot, :, at])
        out_ref[0, 0] = grad.astype(BF).reshape(dp, rows, columns)

    return pl.pallas_call(
        body,
        grid=(len(pairs), seq),
        in_specs=[pl.BlockSpec(memory_space=pl.ANY)] * (2 * len(pairs)),
        out_specs=pl.BlockSpec((1, 1, dp, rows, columns), lambda m, y: (lax.div(m, 2), y, 0, lax.rem(m, 2), 0)),
        out_shape=jax.ShapeDtypeStruct((2, seq, dp, 2 * rows, columns), BF),
        scratch_shapes=[
            pltpu.VMEM((2, tokens, width), BF), pltpu.VMEM((2, tokens, width), BF),
            pltpu.SemaphoreType.DMA((2, 2)),
        ],
        compiler_params=params(),
        cost_estimate=cost(8 * tokens * width * width, 16 * tokens * width + 8 * width * width),
    )(*[array for pair in pairs for array in pair])


def passed_along(array, axis, by):
    devices = lax.axis_size(axis)
    pairs = [(i, i + by) for i in range(devices) if 0 <= i + by < devices]
    return lax.ppermute(array, axis, pairs)


def entering(chain, ends, by):
    came = passed_along(ends, "seq", by)
    for _ in range(lax.axis_size("seq") - 2):
        came = passed_along(ends + chain * came, "seq", by)
    return came


def last_tokens(s, length):
    return s.reshape(-1, length, s.shape[-1])[:, -1].astype(F32)


def edge_norm(s, length, gain, bias):
    unit, _ = centred_norm(last_tokens(s, length))
    return passed_along(unit * gain + bias, "seq", 1)


def edge_back(edge, s, length, gain):
    came = passed_along(edge, "seq", -1)
    unit, rate = centred_norm(last_tokens(s, length))
    small = jnp.concatenate([summed_rows(came * unit), summed_rows(came)])
    return norm_back(came, unit, rate, gain), small


def cut_lookup(shard, grain):
    rows, columns = shard.shape
    width = min(512, columns // 2)
    cut = shard.reshape(rows, columns // (2 * grain), 2, grain).transpose(2, 0, 1, 3)
    cut = cut.reshape(2, rows, columns // 2 // width, width).transpose(0, 2, 1, 3)
    return cut.reshape(2, -1, width)


def join_lookup(first, second, rows, grain):
    width = first.shape[-1]
    cut = jnp.stack([first, second]).reshape(2, -1, rows, width).transpose(0, 2, 1, 3)
    cut = cut.reshape(2, rows, -1, grain).transpose(1, 2, 0, 3)
    return cut.reshape(rows, -1)


def gather_group(core, table, firsts, seconds):
    if not paired():
        pairs = [gather_pair(core, table, a, b) for a, b in zip(firsts, seconds)]
        return [(a, 0) for a, _ in pairs], [(b, 0) for _, b in pairs]
    mine, other = gather_pair(core, table, jnp.concatenate(firsts), jnp.concatenate(seconds))
    spots = [0] + np.cumsum([a.shape[0] for a in firsts])[:-1].tolist()
    return [(mine, at) for at in spots], [(other, at) for at in spots]


def scatter_group(core, table, stores, sizes_of):
    if not paired():
        pairs = [scatter_pair(core, table, s) for s in stores]
        return [a for a, _ in pairs], [b for _, b in pairs]
    first, second = scatter_pair(core, table, stores[0])
    cuts = np.cumsum(sizes_of)[:-1].tolist()
    return jnp.split(first, cuts), jnp.split(second, cuts)


def per_device(
    entering_activations,
    document_numbers,
    result_cotangent,
    normalizer_scales,
    normalizer_offsets,
    shift_blend_factors,
    fading_natural_logs_per_feature,
    feature_reward_logs,
    attention_triple_matrix,
    attention_result_matrix,
    channelmix_lookup_matrix,
    channelmix_content_matrix,
    channelmix_accept_matrix,
):
    dp, seq = sizes()
    core = core_of()
    cores = core.reshape(1)
    table = unit_tables() if paired() else None
    layers = attention_triple_matrix.shape[0]
    runs, length, width = entering_activations.shape
    tokens = runs * length

    lookup_rows = channelmix_lookup_matrix.shape[1]
    grain = channelmix_content_matrix.shape[1] // 2
    half_rows = channelmix_accept_matrix.shape[1] // 2

    att, chan = [], []
    for depth in range(layers):
        triple, result = attention_triple_matrix[depth], attention_result_matrix[depth]
        att.append(
            gather_pair(
                core,
                table,
                jnp.concatenate([triple[0], triple[1]]),
                jnp.concatenate([triple[2], result]),
            )
        )
        lookup = cut_lookup(channelmix_lookup_matrix[depth], grain)
        content, accept = channelmix_content_matrix[depth], channelmix_accept_matrix[depth]
        mine, other = gather_group(
            core,
            table,
            [lookup[0], content[:grain], accept[:half_rows]],
            [lookup[1], content[grain:], accept[half_rows:]],
        )
        takes = [array[:, :, at : at + half_rows] for array, at in (mine[2], other[2])]
        first = jnp.where(core == 0, takes[0], takes[1])
        second = jnp.where(core == 0, takes[1], takes[0])
        cut = Cut(mine[0], mine[1], lookup_rows, grain)
        chan.append((mine, other, jnp.concatenate([first, second], axis=2), cut))

    border = passed_along(document_numbers[:, -1:] + 1, "seq", 1)
    earlier = jnp.concatenate([border - 1, document_numbers[:, :-1]], axis=1)
    marks, lines = token_marks(document_numbers, earlier)
    through = (earlier[:, :1] == document_numbers[:, -1:]).astype(F32)[:, :, None]
    begins = (earlier[:, :1] == document_numbers[:, :1]).astype(F32)[:, :, None]
    rates = jnp.exp(fading_natural_logs_per_feature)
    bonuses = jnp.exp(feature_reward_logs)

    flow = entering_activations.reshape(tokens, width)
    kept = []
    for depth in range(layers):
        gain, bias = normalizer_scales[depth], normalizer_offsets[depth]
        mix, rate, bonus = shift_blend_factors[depth], rates[depth : depth + 1], bonuses[depth : depth + 1]
        chain = jnp.exp(-length * rate)[None] * through
        mine, other = att[depth]
        before = edge_norm(flow, length, gain[0], bias[0])
        xk, xv, xr, k, v, r, ends, lead = time_in(
            cores, flow, before, marks, gain[0:1], bias[0:1], mix[:3], rate, mine, other, length
        )
        enter = entering(chain, ends, 1)
        z, sa, sb, middle = time_out(
            cores, flow, k, v, r, enter, marks, lines, rate, bonus, mine, other, length
        )
        time_kept = (flow, lead, xk, xv, xr, k, v, r, z, sa, sb)
        mine, other, accept, cut = chan[depth]
        before = edge_norm(middle, length, gain[1], bias[1])
        xk, xr, lead, act0, total = channel_one(
            middle, before, marks, gain[1:2], bias[1:2], mix[3:], mine[0], mine[1], cut, length
        )
        kind = BF if depth == layers - 1 else F32
        act1, carried, gate, flow = channel_two(middle, xk, xr, total, other[0], other[1], accept, cut, kind)
        kept.append((time_kept, (middle, lead, xk, xr, (act0, act1), carried, gate)))
    y_out = flow

    grad = result_cotangent.reshape(tokens, width)
    fix = jnp.zeros((runs, width), F32)
    small, large = [None] * layers, [None] * layers
    columns = width // seq
    for depth in reversed(range(layers)):
        gain, bias = normalizer_scales[depth], normalizer_offsets[depth]
        mix, rate, bonus = shift_blend_factors[depth], rates[depth : depth + 1], bonuses[depth : depth + 1]
        chain = jnp.exp(-length * rate)[None] * through
        (flow, lead_t, xk_t, xv_t, xr_t, k, v, r, z, sa, sb), channel_kept = kept[depth]
        middle, lead, xk, xr, acts, carried, gate = channel_kept
        mine, other, accept, cut = chan[depth]
        part_rows = [cut.blocks * lookup_rows, grain, half_rows]
        if paired():
            packing = [(2, seq, dp, sum(part_rows), columns)], [0, part_rows[0], part_rows[0] + grain]
        else:
            widths = [cut.width, columns, columns]
            packing = [(2, seq, dp, n, w) for n, w in zip(part_rows, widths)], [0, 0, 0]
        *stores, grad, edge, small_chan = channel_back(
            cores, grad, fix, middle, lead, marks, gain[1:2], bias[1:2], mix[3:], gate, carried, xk, xr,
            acts, (mine[0], other[0]), (mine[1], other[1]), accept, cut, length, packing,
        )
        first, second = scatter_group(core, table, stores, part_rows)
        chan_large = (
            join_lookup(first[0], second[0], lookup_rows, grain),
            jnp.concatenate([first[1], second[1]]),
            jnp.concatenate([first[2], second[2]]),
        )
        fix, edge_chan = edge_back(edge, middle, length, gain[1])
        mine, other = att[depth]
        go, gr, gn, gd, sums = out_back(
            cores, grad, fix, k, v, r, sa, sb, marks, rate, bonus, mine, other, length
        )
        leave = entering(chain, begins * sums, -1)
        gk, gv, grad, edge, small_time = time_back(
            cores, grad, fix, flow, lead_t, k, v, sa, sb, gn, gd, gr, leave, marks, lines,
            gain[0:1], bias[0:1], mix[:3], rate, bonus, mine, other, length,
        )
        store = weight_grads([xk_t, xv_t], [xr_t, z], [gk, gv, gr, go])
        rows = store.shape[3] // 2
        first, second = scatter_group(core, table, [store], [2 * rows])
        triple = jnp.stack([first[0][:rows], first[0][rows:], second[0][:rows]])
        large[depth] = (triple, second[0][rows:]) + chan_large
        fix, edge_time = edge_back(edge, flow, length, gain[0])
        fading = small_time[5:6] * -rate * jnp.exp(-rate)
        small[depth] = jnp.concatenate(
            [
                small_time[0:1] + edge_time[0:1],
                small_chan[0:1] + edge_chan[0:1],
                small_time[1:2] + edge_time[1:2],
                small_chan[1:2] + edge_chan[1:2],
                small_time[2:5],
                small_chan[2:4],
                fading,
                small_time[6:7],
            ]
        )
    grad = grad.reshape(runs, length, width).at[:, -1].add(fix)
    small = summed_everywhere(jnp.stack(small))
    large = [jnp.stack(members) for members in zip(*large)]
    return (
        y_out.reshape(runs, length, width),
        grad,
        small[:, 0:2],
        small[:, 2:4],
        small[:, 4:9],
        small[:, 9],
        small[:, 10],
        *large,
    )


def solution(mesh):
    return jax.shard_map(
        per_device,
        mesh=mesh,
        in_specs=(
            P("dp", "seq", None),
            P("dp", "seq"),
            P("dp", "seq", None),
            P(),
            P(),
            P(),
            P(),
            P(),
            P(None, None, "dp", "seq"),
            P(None, "dp", "seq"),
            P(None, "dp", "seq"),
            P(None, "dp", "seq"),
            P(None, "dp", "seq"),
        ),
        out_specs=(
            P("dp", "seq", None),
            P("dp", "seq", None),
            P(),
            P(),
            P(),
            P(),
            P(),
            P(None, None, "dp", "seq"),
            P(None, "dp", "seq"),
            P(None, "dp", "seq"),
            P(None, "dp", "seq"),
            P(None, "dp", "seq"),
        ),
        check_vma=False,
    )
```

```python
import jax
import jax.numpy as jnp
import numpy as np
from jax import lax
from jax.experimental import pallas as pl
from jax.experimental.pallas import tpu as pltpu
from jax.sharding import PartitionSpec as P

EPS = 1e-05
BF = jnp.bfloat16
F32 = jnp.float32
BOTH = ("dp", "seq")
VMEM = 58 * 2**20


def sizes():
    return lax.axis_size("dp"), lax.axis_size("seq")


def paired():
    dp, seq = sizes()
    return seq == 2 and dp % 4 == 0


def place(d):
    return d // 4, d // 2 % 2, d % 2


def core_of():
    if not paired():
        return jnp.int32(0)
    return lax.rem(lax.axis_index("dp"), 2)


def moved(array, target):
    dp, seq = sizes()
    pairs = []
    for d in range(dp):
        for y in range(seq):
            z, x, c, y2 = target(*place(d), y)
            pairs.append((d * seq + y, (z * 4 + x * 2 + c) * seq + y2))
    return lax.ppermute(array, BOTH, pairs)


def to_core(z, x, c, y):
    return z, x, 1 - c, y


def to_second(z, x, c, y):
    return (z, 1 - x, c, y) if c == 0 else (z, x, c, 1 - y)


def to_third(z, x, c, y):
    return (z, x, c, 1 - y) if c == 0 else (z, 1 - x, c, y)


def along_z(step):
    depth = sizes()[0] // 4

    def target(z, x, c, y):
        return (z + step) % depth, x, c, y

    return target


def unit_spots(z, x, c, y):
    depth = sizes()[0] // 4
    half, index = [], []
    for yy in range(2):
        for zz in range(depth):
            for xx in range(2):
                dx, dy, dz = xx ^ x, yy ^ y, (z - zz) % depth
                half.append(dy if c == 0 else dx)
                index.append((dx if c == 0 else dy) * depth + dz)
    return half, index


def unit_tables():
    dp, seq = sizes()
    rows = []
    for d in range(dp):
        for y in range(seq):
            z, x, c = place(d)
            half, index = unit_spots(z, x, c, y)
            lines = [half]
            for side in range(2):
                line, last = [], [i for i, h in zip(index, half) if h == side][0]
                for i, h in zip(index, half):
                    last = i if h == side else last
                    line.append(last)
                lines.append(line)
            for core in range(2):
                lines.extend(unit_spots(z, x, core, y))
            rows.append(lines)
    table = jnp.asarray(np.array(rows, np.int32))
    me = lax.axis_index("dp") * seq + lax.axis_index("seq")
    return lax.dynamic_index_in_dim(table, me, 0, keepdims=False)


SPOTS = 3


def arrange(table, own, other):
    units, block = 2 * own.shape[0], (1,) + own.shape[1:]

    def body(table_ref, own_ref, other_ref, out_ref):
        half = table_ref[0, pl.program_id(0)]

        @pl.when(half == 0)
        def _():
            out_ref[...] = own_ref[...]

        @pl.when(half == 1)
        def _():
            out_ref[...] = other_ref[...]

    return pl.pallas_call(
        body,
        grid_spec=pltpu.PrefetchScalarGridSpec(
            num_scalar_prefetch=1,
            grid=(units,),
            in_specs=[
                pl.BlockSpec(block, lambda i, t: (t[1, i], 0, 0)),
                pl.BlockSpec(block, lambda i, t: (t[2, i], 0, 0)),
            ],
            out_specs=pl.BlockSpec(block, lambda i, t: (i, 0, 0)),
        ),
        out_shape=jax.ShapeDtypeStruct((units,) + own.shape[1:], own.dtype),
        compiler_params=pltpu.CompilerParams(vmem_limit_bytes=VMEM),
        cost_estimate=pl.CostEstimate(flops=1, bytes_accessed=1, transcendentals=0),
    )(table, own, other)


def tie(arrays, *others):
    return lax.optimization_barrier((arrays, others))[0]


class Gathering:
    def __init__(self, table, pair):
        self.table, self.pair, self.depth = table, pair, sizes()[0] // 4

    def z(self, *after):
        pair = tie(self.pair, *after)
        self.parts = [moved(pair, along_z(step)) for step in range(1, self.depth)]

    def end_z(self, *after):
        line = jnp.stack([self.pair] + tie(self.parts, *after))
        self.line = line.reshape((self.depth, -1) + line.shape[3:])
        return self.line

    def second(self, *after):
        self.came = moved(tie(self.line, *after), to_second)
        return self.came

    def third(self, *after):
        self.half = jnp.concatenate(tie([self.line, self.came], *after))
        self.far = moved(self.half, to_third)
        return self.far

    def arrange(self, *after):
        self.mine = arrange(self.table, *tie((self.half, self.far), *after))
        return self.mine

    def swap(self):
        dp, seq = sizes()
        other = moved(self.mine, to_core)
        shape = (seq, dp, self.mine.shape[1] // 2) + self.mine.shape[2:]
        return self.mine.reshape(shape), other.reshape(shape)


class Scattering:
    def __init__(self, away, keep):
        self.depth = sizes()[0] // 4
        groups = [[2 * i, 2 * i + 1] for i in range(sizes()[0] // 2)]
        self.take = lambda array: lax.psum_scatter(array, "dp", scatter_dimension=0, axis_index_groups=groups)
        self.away, self.keep = self.take(away), keep

    def third(self, *after):
        self.away = tie(self.away, *after)
        self.keep = self.take(tie(self.keep, self.away))
        self.came = moved(self.away, to_third)
        return self.away

    def end_third(self, *after):
        depth, keep, came = self.depth, *tie((self.keep, self.came), *after)
        self.away = (keep[depth:].astype(F32) + came[depth:].astype(F32)).astype(BF)
        self.keep = (keep[:depth].astype(F32) + came[:depth].astype(F32)).astype(BF)
        return self.away

    def second(self, *after):
        self.came = moved(tie(self.away, *after), to_second)

    def end_second(self, *after):
        keep, came = tie((self.keep, self.came), *after)
        self.line = (keep.astype(F32) + came.astype(F32)).astype(BF)
        return self.line

    def z(self, *after):
        line = tie(self.line, *after)
        self.parts = [moved(line[step], along_z(-step)) for step in range(1, self.depth)]
        return self.parts

    def end_z(self, core):
        total = self.line[0].astype(F32)
        for part in self.parts:
            total = total + part.astype(F32)
        total = total.reshape((2, -1) + total.shape[1:])
        kept = jnp.where(core == 0, total[0], total[1])
        came = moved(jnp.where(core == 0, total[1], total[0]), to_core)
        return jnp.where(core == 0, kept, came), jnp.where(core == 0, came, kept)


def summed_z(array):
    dp, _ = sizes()
    return lax.psum(array, "dp", axis_index_groups=[list(range(i, dp, 4)) for i in range(4)])


def hop_y(array):
    return array + moved(array, lambda z, x, c, y: (z, x, c, 1 - y))


def hop_x(array):
    return array + moved(array, lambda z, x, c, y: (z, 1 - x, c, y))


def params(**more):
    return pltpu.CompilerParams(vmem_limit_bytes=VMEM, **more)


def cost(flops, bytes_accessed):
    return pl.CostEstimate(flops=1, bytes_accessed=1, transcendentals=0)


def held(shape):
    zeros = (0,) * len(shape)
    return pl.BlockSpec(shape, lambda *_: zeros, pipeline_mode=pl.Buffered(1))


def fixed(shape):
    zeros = (0,) * len(shape)
    return pl.BlockSpec(shape, lambda *_: zeros)


SCALAR = pl.BlockSpec(memory_space=pltpu.SMEM)


def dot(a, b):
    return lax.dot_general(a, b, (((1,), (0,)), ((), ())), preferred_element_type=F32)


def dot_nt(a, b):
    return lax.dot_general(a, b, (((1,), (1,)), ((), ())), preferred_element_type=F32)


def dot_tn(a, b):
    return lax.dot_general(a, b, (((0,), (0,)), ((), ())), preferred_element_type=F32)


def split_sum(mask, terms):
    high = terms.astype(BF)
    low = (terms - high.astype(F32)).astype(BF)
    return dot(mask, high) + dot(mask, low)


def centred_norm(s):
    centred = s - jnp.mean(s, axis=-1, keepdims=True)
    rate = lax.rsqrt(jnp.mean(centred * centred, axis=-1, keepdims=True) + EPS)
    return centred * rate, rate


def norm_back(grad, unit, rate, gain):
    grad = grad * gain
    return rate * (
        grad
        - jnp.mean(grad, axis=-1, keepdims=True)
        - unit * jnp.mean(grad * unit, axis=-1, keepdims=True)
    )


def down_one(tile, first):
    rows = lax.broadcasted_iota(jnp.int32, tile.shape, 0)
    return jnp.where(rows == 0, first, pltpu.roll(tile, 1, 0))


def up_one(tile, last):
    size = tile.shape[0]
    rows = lax.broadcasted_iota(jnp.int32, tile.shape, 0)
    return jnp.where(rows == size - 1, last, pltpu.roll(tile, size - 1, 0))


def summed_rows(tile):
    return jnp.sum(tile, axis=0, keepdims=True)


def times(x, store, lo, hi, out_ref, rows=slice(None)):
    seq, dp, _, columns = store.shape
    for y in range(seq):
        weight = store[y, :, lo:hi, :].reshape(dp * (hi - lo), columns)
        out_ref[rows, y * columns : (y + 1) * columns] = dot(x, weight)


def times_back(g, store, lo, hi):
    seq, dp, _, columns = store.shape
    total = None
    for y in range(seq):
        weight = store[y, :, lo:hi, :].reshape(dp * (hi - lo), columns)
        part = dot_nt(g[:, y * columns : (y + 1) * columns], weight)
        total = part if total is None else total + part
    return total


def by_core(core_ref, mine, other, run):
    @pl.when(core_ref[0] == 0)
    def _():
        run(mine, other)

    @pl.when(core_ref[0] != 0)
    def _():
        run(other, mine)


def tile_rows(length):
    return min(256, length)


ALIVE, ENTERS, TAIL, HEAD, LEAVES = range(5)


def col(marks, which):
    return marks[:, which : which + 1]


def token_marks(document_numbers, earlier):
    rows, length = document_numbers.shape
    tile = tile_rows(length)
    tiles = document_numbers.reshape(rows, length // tile, tile)
    before = earlier.reshape(tiles.shape)[:, :, :1]
    marks = [
        document_numbers == earlier,
        (tiles == before).reshape(rows, length),
        document_numbers == document_numbers[:, -1:],
        document_numbers == document_numbers[:, :1],
        (tiles == tiles[:, :, -1:]).reshape(rows, length),
        jnp.zeros_like(document_numbers, dtype=bool),
        jnp.zeros_like(document_numbers, dtype=bool),
    ]
    marks = [m.astype(F32) for m in marks] + [document_numbers.astype(F32)]
    marks = jnp.stack(marks, axis=-1).reshape(rows * length, 8)
    lines = document_numbers.astype(F32).reshape(rows * length // tile, 1, tile)
    return marks, lines


def time_in(core, s, before, marks, gain, bias, mix, rate, mine, other, length):
    tokens, width = s.shape
    tile = tile_rows(length)
    per_run = length // tile
    runs = tokens // length

    def body(
        core_ref, s_ref, before_ref, marks_ref, gain_ref, bias_ref, mix_ref, rate_ref,
        mine_ref, other_ref,
        xk_ref, xv_ref, xr_ref, k_ref, v_ref, r_ref, end_ref, lead_ref, carry_ref,
    ):
        step = pl.program_id(0)
        run, part = lax.div(step, per_run), lax.rem(step, per_run)
        unit, _ = centred_norm(s_ref[...].astype(F32))
        normed = unit * gain_ref[...] + bias_ref[...]

        @pl.when(part == 0)
        def _():
            carry_ref[...] = before_ref[pl.ds(run, 1), :]
            end_ref[pl.ds(run, 1)] = jnp.zeros((1, 2, width), F32)

        lead_ref[0] = carry_ref[...]
        shifted = down_one(normed, carry_ref[...]) * col(marks_ref[...], ALIVE)
        carry_ref[...] = normed[tile - 1 :, :]
        change = normed - shifted
        xk_ref[...] = (shifted + mix_ref[0:1, :] * change).astype(BF)
        xv_ref[...] = (shifted + mix_ref[1:2, :] * change).astype(BF)
        xr_ref[...] = (shifted + mix_ref[2:3, :] * change).astype(BF)

        def project(first, second):
            rows = first.shape[2] // 2
            times(xk_ref[...], first, 0, rows, k_ref)
            times(xv_ref[...], first, rows, 2 * rows, v_ref)
            times(xr_ref[...], second, 0, rows, r_ref)

        by_core(core_ref, mine_ref, other_ref, project)
        places = lax.broadcasted_iota(jnp.int32, (tile, 1), 0).astype(F32)
        left = (length - 1 - part * tile).astype(F32) - places
        weight = jnp.exp(k_ref[...] - left * rate_ref[...]) * col(marks_ref[...], TAIL)
        ends = jnp.concatenate([summed_rows(weight * v_ref[...]), summed_rows(weight)], axis=0)
        end_ref[pl.ds(run, 1)] += ends[None]

    block = pl.BlockSpec((tile, width), lambda i: (i, 0))
    half, full = jax.ShapeDtypeStruct((tokens, width), BF), jax.ShapeDtypeStruct((tokens, width), F32)
    return pl.pallas_call(
        body,
        grid=(tokens // tile,),
        in_specs=[
            SCALAR, block, fixed(before.shape), pl.BlockSpec((tile, 8), lambda i: (i, 0)),
            fixed(gain.shape), fixed(bias.shape), fixed(mix.shape), fixed(rate.shape),
            held(mine.shape), held(other.shape),
        ],
        out_specs=[block] * 6 + [fixed((runs, 2, width)), pl.BlockSpec((1, 1, width), lambda i: (i, 0, 0))],
        out_shape=[half] * 3 + [full] * 3 + [
            jax.ShapeDtypeStruct((runs, 2, width), F32),
            jax.ShapeDtypeStruct((tokens // tile, 1, width), F32),
        ],
        scratch_shapes=[pltpu.VMEM((1, width), F32)],
        compiler_params=params(),
        cost_estimate=cost(6 * tokens * width * width, 22 * tokens * width + 4 * mine.size),
    )(core, s, before, marks, gain, bias, mix, rate, mine, other)


def time_out(core, s, k, v, r, enter, marks, lines, rate, bonus, mine, other, length):
    tokens, width = s.shape
    tile = tile_rows(length)
    per_run = length // tile

    def body(
        core_ref, s_ref, k_ref, v_ref, r_ref, enter_ref, marks_ref, line_ref, rate_ref, bonus_ref,
        mine_ref, other_ref, z_ref, sa_ref, sb_ref, out_ref, state_ref,
    ):
        step = pl.program_id(0)
        run, part = lax.div(step, per_run), lax.rem(step, per_run)

        @pl.when(part == 0)
        def _():
            state_ref[...] = enter_ref[pl.ds(run, 1)][0]

        marks = marks_ref[...]
        places = lax.broadcasted_iota(jnp.int32, (tile, 1), 0).astype(F32)
        spread = places * rate_ref[...]
        falling, decay = jnp.exp(-spread), jnp.exp(-rate_ref[...])
        powered = jnp.exp(k_ref[...])
        content = v_ref[...]
        raised = jnp.exp(k_ref[...] + spread)
        at = lax.broadcasted_iota(jnp.int32, (tile, tile), 0)
        source = lax.broadcasted_iota(jnp.int32, (tile, tile), 1)
        same = col(marks, 7) == line_ref[0]
        mask = jnp.where(jnp.logical_and(same, source < at), 1.0, 0.0).astype(BF)
        carried = falling * col(marks, ENTERS)
        ahead = falling * jnp.exp(rate_ref[...])
        state_a = ahead * split_sum(mask, raised * content) + carried * state_ref[0:1, :]
        state_b = ahead * split_sum(mask, raised) + carried * state_ref[1:2, :]
        sa_ref[...] = state_a
        sb_ref[...] = state_b
        state_ref[0:1, :] = decay * state_a[tile - 1 :] + (powered * content)[tile - 1 :]
        state_ref[1:2, :] = decay * state_b[tile - 1 :] + powered[tile - 1 :]
        scaled = powered * bonus_ref[...]
        answer = (state_a + scaled * content) / (state_b + scaled)
        z_ref[...] = (jax.nn.sigmoid(r_ref[...]) * answer).astype(BF)

        def project(first, second):
            rows = first.shape[2] // 2
            times(z_ref[...], second, rows, 2 * rows, out_ref)

        by_core(core_ref, mine_ref, other_ref, project)
        out_ref[...] += s_ref[...].astype(F32)

    block = pl.BlockSpec((tile, width), lambda i: (i, 0))
    half, full = jax.ShapeDtypeStruct((tokens, width), BF), jax.ShapeDtypeStruct((tokens, width), F32)
    return pl.pallas_call(
        body,
        grid=(tokens // tile,),
        in_specs=[
            SCALAR, block, block, block, block, fixed(enter.shape),
            pl.BlockSpec((tile, 8), lambda i: (i, 0)), pl.BlockSpec((1, 1, tile), lambda i: (i, 0, 0)),
            fixed(rate.shape), fixed(bonus.shape), held(mine.shape), held(other.shape),
        ],
        out_specs=[block] * 4,
        out_shape=[half, full, full, full],
        scratch_shapes=[pltpu.VMEM((2, width), F32)],
        compiler_params=params(),
        cost_estimate=cost(4 * tokens * width * width, 30 * tokens * width + 4 * mine.size),
    )(core, s, k, v, r, enter, marks, lines, rate, bonus, mine, other)


def lookup_block(store, rows, blocks, step):
    seq, dp, _, width = store.shape
    return pl.BlockSpec(
        (1, dp, rows, width), lambda i: (lax.div(step(i), blocks), 0, lax.rem(step(i), blocks), 0)
    )


def content_block(store, grain, at, group, step):
    seq, _, _, columns = store.shape
    return pl.BlockSpec((seq, group, grain, columns), lambda i: (0, step(i), at // grain, 0))


class Cut:
    def __init__(self, lookup, content, lookup_rows, grain):
        store, _ = lookup
        seq, dp, _, self.width = store.shape
        self.rows, self.grain = lookup_rows, grain
        self.group = self.width // grain
        self.steps = dp // self.group
        self.blocks = self.steps // seq
        self.at = content[1]

    def specs(self, lookup, content, step):
        return [
            lookup_block(lookup[0], self.rows, self.blocks, step),
            content_block(content[0], self.grain, self.at, self.group, step),
        ]


def hidden_step(x_ref, lookup_ref, content_ref, act_ref, total_ref, first):
    tokens = x_ref.shape[0]
    tile = min(256, tokens)
    _, dp, rows, width = lookup_ref.shape
    seq, group, grain, columns = content_ref.shape
    up = lookup_ref[0].reshape(dp * rows, width)
    for t in range(0, tokens, tile):
        hidden = jnp.maximum(dot(x_ref[t : t + tile, :], up), 0.0)
        act = (hidden * hidden).astype(BF)
        act_ref[0, t : t + tile, :] = act
        for y in range(seq):
            part = dot(act, content_ref[y].reshape(group * grain, columns))
            where = (slice(t, t + tile), slice(y * columns, (y + 1) * columns))
            total_ref[where] = part if first else total_ref[where] + part


def channel_one(s, before, marks, gain, bias, mix, lookup, content, cut, length):
    tokens, width = s.shape
    tile = tile_rows(length)
    tiles, per_run = tokens // tile, length // tile

    def body(
        s_ref, before_ref, marks_ref, gain_ref, bias_ref, mix_ref, lookup_ref, content_ref,
        xk_ref, xr_ref, lead_ref, act_ref, total_ref,
    ):
        @pl.when(pl.program_id(0) == 0)
        def _():
            last = None
            for i in range(tiles):
                rows = slice(i * tile, (i + 1) * tile)
                unit, _ = centred_norm(s_ref[rows, :])
                normed = unit * gain_ref[...] + bias_ref[...]
                if i % per_run == 0:
                    last = before_ref[i // per_run : i // per_run + 1, :]
                lead_ref[i] = last
                shifted = down_one(normed, last) * col(marks_ref[rows, :], ALIVE)
                last = normed[tile - 1 :, :]
                change = normed - shifted
                xk_ref[rows, :] = (shifted + mix_ref[0:1, :] * change).astype(BF)
                xr_ref[rows, :] = (shifted + mix_ref[1:2, :] * change).astype(BF)
            hidden_step(xk_ref, lookup_ref, content_ref, act_ref, total_ref, True)

        @pl.when(pl.program_id(0) > 0)
        def _():
            hidden_step(xk_ref, lookup_ref, content_ref, act_ref, total_ref, False)

    half, full = jax.ShapeDtypeStruct((tokens, width), BF), jax.ShapeDtypeStruct((tokens, width), F32)
    return pl.pallas_call(
        body,
        grid=(cut.steps,),
        in_specs=[
            held(s.shape), fixed(before.shape), held(marks.shape),
            fixed(gain.shape), fixed(bias.shape), fixed(mix.shape),
        ] + cut.specs(lookup, content, lambda i: i),
        out_specs=[
            fixed((tokens, width)), fixed((tokens, width)), fixed((tiles, 1, width)),
            pl.BlockSpec((1, tokens, cut.width), lambda i: (i, 0, 0)), fixed((tokens, width)),
        ],
        out_shape=[
            half, half, jax.ShapeDtypeStruct((tiles, 1, width), F32),
            jax.ShapeDtypeStruct((cut.steps, tokens, cut.width), BF), full,
        ],
        compiler_params=params(),
        cost_estimate=cost(
            4 * tokens * width * cut.width * cut.steps,
            14 * tokens * width + cut.steps * cut.width * (4 * width + 2 * tokens),
        ),
    )(s, before, marks, gain, bias, mix, lookup[0], content[0])


def channel_two(s, xk, xr, total, lookup, content, accept, cut, kind):
    tokens, width = s.shape
    tile = min(256, tokens)

    def body(
        s_ref, xk_ref, xr_ref, total_ref, accept_ref, lookup_ref, content_ref,
        act_ref, carried_ref, gate_ref, out_ref, sum_ref, take_ref,
    ):
        @pl.when(pl.program_id(0) == 0)
        def _():
            sum_ref[...] = total_ref[...]

        hidden_step(xk_ref, lookup_ref, content_ref, act_ref, sum_ref, False)

        @pl.when(pl.program_id(0) == cut.steps - 1)
        def _():
            for t in range(0, tokens, tile):
                rows = slice(t, t + tile)
                times(xr_ref[rows, :], accept_ref, 0, accept_ref.shape[2], take_ref)
                gate = jax.nn.sigmoid(take_ref[...])
                carried = sum_ref[rows, :]
                gate_ref[rows, :] = gate.astype(BF)
                carried_ref[rows, :] = carried.astype(BF)
                out_ref[rows, :] = (s_ref[rows, :] + gate * carried).astype(kind)

    half = jax.ShapeDtypeStruct((tokens, width), BF)
    return pl.pallas_call(
        body,
        grid=(cut.steps,),
        in_specs=[held(s.shape), held(xk.shape), held(xr.shape), held(total.shape), held(accept.shape)]
        + cut.specs(lookup, content, lambda i: i),
        out_specs=[pl.BlockSpec((1, tokens, cut.width), lambda i: (i, 0, 0))] + [fixed((tokens, width))] * 3,
        out_shape=[
            jax.ShapeDtypeStruct((cut.steps, tokens, cut.width), BF), half, half,
            jax.ShapeDtypeStruct((tokens, width), kind),
        ],
        scratch_shapes=[pltpu.VMEM((tokens, width), F32), pltpu.VMEM((tile, width), F32)],
        compiler_params=params(),
        cost_estimate=cost(
            4 * tokens * width * cut.width * cut.steps + 2 * tokens * width * width,
            20 * tokens * width + cut.steps * cut.width * (4 * width + 2 * tokens) + 2 * accept.size,
        ),
    )(s, xk, xr, total, accept, lookup[0], content[0])


def mixed_back(grads, s, lead, alive, gain, bias, mix_ref, after):
    unit, rate = centred_norm(s)
    normed = unit * gain + bias
    change = normed - down_one(normed, lead) * alive
    own, before, mixes = None, None, []
    for j, grad in enumerate(grads):
        mix = mix_ref[j : j + 1, :]
        a, b = mix * grad, (1.0 - mix) * grad
        own, before = (a, b) if own is None else (own + a, before + b)
        mixes.append(summed_rows(change * grad))
    before = before * alive
    grad = own + up_one(before, after)
    small = [summed_rows(grad * unit), summed_rows(grad)] + mixes
    return norm_back(grad, unit, rate, gain), before[0:1, :], small


def channel_back(
    core, g, fix, s, lead, marks, gain, bias, mix, gate, carried, xk, xr, acts, lookups, contents, accept,
    cut, length, packing, table,
):
    tokens, width = s.shape
    tile = tile_rows(length)
    tiles, per_run = tokens // tile, length // tile
    steps = cut.steps
    shapes, spots = packing
    seq, dp = accept.shape[:2]
    columns = width // seq
    half_rows = accept.shape[2] // 2
    last = 2 * steps - 1
    slots = len(shapes)
    split = slots == 2
    units = dp // 2

    def body(
        core_ref, g_ref, fix_ref, s_ref, lead_ref, marks_ref, gain_ref, bias_ref, mix_ref,
        gate_ref, carried_ref, xk_ref, xr_ref, act0_ref, act1_ref, accept_ref,
        lookup0_ref, content0_ref, lookup1_ref, content1_ref, table_ref, *rest,
    ):
        outs, rest = rest[:slots], rest[slots:]
        out_ref, edge_ref, small_ref, gc_ref, gr_ref, sum_ref, key_ref, val_ref, take_ref, sem, stage_ref = rest
        if not split:
            lookup_out, content_out, accept_out = outs
        step = pl.program_id(0)
        slot = lax.rem(step, 2)

        def waits(which):
            if split:
                rows = pl.ds(0, cut.rows)
                key = outs[1].at[0, :, :, rows, :]
                val = outs[1].at[0, pl.ds(0, seq * cut.group // 2), :, pl.ds(0, cut.grain), :]
                val_from = val_ref.at[which].reshape(seq * cut.group // 2, 2, cut.grain, columns)
            else:
                key = lookup_out.at[0, 0, :, :, pl.ds(0, cut.rows), :]
                val = content_out.at[0, :, pl.ds(0, cut.group // 2), :, :, :]
                val_from = val_ref.at[which]
            pltpu.make_async_copy(key_ref.at[which], key, sem.at[which, 0]).wait()
            pltpu.make_async_copy(val_from, val, sem.at[which, 1]).wait()

        def send(source, unit, store, rows, sem):
            half = table_ref[SPOTS + 2 * store, unit]
            index = table_ref[SPOTS + 1 + 2 * store, unit]
            for side in range(2):

                @pl.when(half == 1 - side)
                def _(side=side):
                    pltpu.make_async_copy(source, outs[side].at[store, index, :, rows, :], sem).start()

        def start(which, store, q):
            y, block = lax.div(q, cut.blocks), lax.rem(q, cut.blocks)
            if split:
                rows = pl.ds(pl.multiple_of(spots[0] + block * cut.rows, 16), cut.rows)
                for unit in range(units):
                    send(key_ref.at[which, unit], y * units + unit, store, rows, sem.at[which, 0])
                for y in range(seq):
                    for part in range(cut.group // 2):
                        unit = y * units + q * (cut.group // 2) + part
                        rows = pl.ds(spots[1], cut.grain)
                        send(val_ref.at[which, y, part], unit, store, rows, sem.at[which, 1])
            else:
                rows = pl.ds(pl.multiple_of(block * cut.rows, 16), cut.rows)
                key = lookup_out.at[store, y, :, :, rows, :]
                pltpu.make_async_copy(key_ref.at[which], key, sem.at[which, 0]).start()
                val = content_out.at[store, :, pl.ds(q * (cut.group // 2), cut.group // 2), :, :, :]
                pltpu.make_async_copy(val_ref.at[which], val, sem.at[which, 1]).start()

        def store_of_step(i):
            core = core_ref[0]
            return jnp.where(i < steps, core, 1 - core), lax.rem(i, steps)

        @pl.when(step == 0)
        def _():
            for i in range(tiles):
                rows = slice(i * tile, (i + 1) * tile)
                grad = g_ref[rows, :].astype(F32)
                if (i + 1) % per_run == 0:
                    at = lax.broadcasted_iota(jnp.int32, grad.shape, 0)
                    run = i // per_run
                    grad = jnp.where(at == tile - 1, grad + fix_ref[run : run + 1, :], grad)
                gate = gate_ref[rows, :].astype(F32)
                passed = grad * gate
                out_ref[rows, :] = grad
                gc_ref[rows, :] = passed.astype(BF)
                gr_ref[rows, :] = (passed * carried_ref[rows, :].astype(F32) * (1.0 - gate)).astype(BF)

        @pl.when(step >= 2)
        def _():
            waits(slot)

        def work(act_ref, lookup_ref, content_ref, first):
            up = lookup_ref[0].reshape(dp * cut.rows, cut.width)
            size = min(256, tokens)
            for t in range(0, tokens, size):
                rows = slice(t, t + size)
                act = act_ref[0, rows, :].astype(F32)
                grad = None
                for y in range(seq):
                    part = dot_nt(
                        gc_ref[rows, y * columns : (y + 1) * columns],
                        content_ref[y].reshape(cut.group * cut.grain, columns),
                    )
                    grad = part if grad is None else grad + part
                grad = (grad * (2.0 * jnp.sqrt(act))).astype(BF)
                take_ref[rows, :] = grad
                part = dot_nt(grad, up)
                sum_ref[rows, :] = part if first else sum_ref[rows, :] + part
            key = dot_tn(xk_ref[...], take_ref[...])
            key_ref[slot] = key.astype(BF).reshape(units, 2, cut.rows, cut.width)
            for y in range(seq):
                val = dot_tn(act_ref[0], gc_ref[:, y * columns : (y + 1) * columns])
                val_ref[slot, y] = val.astype(BF).reshape(cut.group // 2, 2, cut.grain, columns)

        @pl.when(step == 0)
        def _():
            work(act0_ref, lookup0_ref, content0_ref, True)

        @pl.when(jnp.logical_and(step > 0, step < steps))
        def _():
            work(act0_ref, lookup0_ref, content0_ref, False)

        @pl.when(step >= steps)
        def _():
            work(act1_ref, lookup1_ref, content1_ref, False)

        start(slot, *store_of_step(step))

        @pl.when(step == last)
        def _():
            waits(1 - slot)
            waits(slot)
            rows = pl.ds(spots[2], half_rows)
            for y in range(seq):
                grad = dot_tn(xr_ref[...], gr_ref[:, y * columns : (y + 1) * columns])
                grad = grad.astype(BF).reshape(dp, 2 * half_rows, columns)
                for h in range(2):
                    part = grad[:, h * half_rows : (h + 1) * half_rows, :]
                    stage_ref[h, y] = part.reshape(units, 2, half_rows, columns)
                    if split:
                        for unit in range(units):
                            send(stage_ref.at[h, y, unit], y * units + unit, h, rows, sem.at[h, 2 + y])
                    else:
                        take = accept_out.at[h, y]
                        pltpu.make_async_copy(stage_ref.at[h, y], take, sem.at[h, 2 + y]).start()
            after = None
            small = None
            for i in reversed(range(tiles)):
                at = slice(i * tile, (i + 1) * tile)
                if (i + 1) % per_run == 0:
                    after = jnp.zeros((1, width), F32)
                grads = [sum_ref[at, :], times_back(gr_ref[at, :], accept_ref, 0, 2 * half_rows)]
                add, after, more = mixed_back(
                    grads, s_ref[at, :], lead_ref[i], col(marks_ref[at, :], ALIVE),
                    gain_ref[...], bias_ref[...], mix_ref, after,
                )
                out_ref[at, :] += add
                small = more if small is None else [a + b for a, b in zip(small, more)]
                if i % per_run == 0:
                    edge_ref[i // per_run : i // per_run + 1, :] = after
            for j, line in enumerate(small):
                small_ref[j : j + 1, :] = line
            for h in range(2):
                for y in range(seq):
                    if split:
                        take = outs[1].at[0, :, :, rows, :]
                    else:
                        take = accept_out.at[h, y]
                    pltpu.make_async_copy(stage_ref.at[h, y], take, sem.at[h, 2 + y]).wait()

    own = lambda i: jnp.minimum(i, steps - 1)
    partner = lambda i: jnp.maximum(i - steps, 0)
    act = lambda step: pl.BlockSpec((1, tokens, cut.width), lambda i: (step(i), 0, 0))
    any_space = pl.BlockSpec(memory_space=pl.ANY)
    return pl.pallas_call(
        body,
        grid=(2 * steps,),
        in_specs=[
            SCALAR, held(g.shape), fixed(fix.shape), held(s.shape), fixed(lead.shape), held(marks.shape),
            fixed(gain.shape), fixed(bias.shape), fixed(mix.shape), held(gate.shape), held(carried.shape),
            held(xk.shape), held(xr.shape), act(own), act(partner), held(accept.shape),
        ] + cut.specs(lookups[0], contents[0], own) + cut.specs(lookups[1], contents[1], partner) + [SCALAR],
        out_specs=[any_space] * slots + [fixed((tokens, width)), fixed(fix.shape), fixed((4, width))],
        out_shape=[jax.ShapeDtypeStruct(shape, BF) for shape in shapes] + [
            jax.ShapeDtypeStruct((tokens, width), F32), jax.ShapeDtypeStruct(fix.shape, F32),
            jax.ShapeDtypeStruct((4, width), F32),
        ],
        scratch_shapes=[
            pltpu.VMEM((tokens, width), BF), pltpu.VMEM((tokens, width), BF),
            pltpu.VMEM((tokens, width), F32),
            pltpu.VMEM((2, units, 2, cut.rows, cut.width), BF),
            pltpu.VMEM((2, seq, cut.group // 2, 2, cut.grain, columns), BF),
            pltpu.VMEM((tokens, cut.width), BF),
            pltpu.SemaphoreType.DMA((2, 2 + seq)),
            pltpu.VMEM((2, seq, units, 2, half_rows, columns), BF),
        ],
        compiler_params=params(),
        cost_estimate=cost(
            16 * tokens * width * cut.width * steps + 4 * tokens * width * width,
            30 * tokens * width + 2 * steps * cut.width * (8 * width + 2 * tokens),
        ),
    )(
        core, g, fix, s, lead, marks, gain, bias, mix, gate, carried, xk, xr, *acts, accept,
        lookups[0][0], contents[0][0], lookups[1][0], contents[1][0], table,
    )


def out_back(core, g, fix, k, v, r, sa, sb, marks, rate, bonus, mine, other, length):
    tokens, width = g.shape
    tile = tile_rows(length)
    per_run = length // tile
    runs = tokens // length

    def body(
        core_ref, g_ref, fix_ref, k_ref, v_ref, r_ref, sa_ref, sb_ref, marks_ref, rate_ref, bonus_ref,
        mine_ref, other_ref, go_ref, gr_ref, gn_ref, gd_ref, chain_ref, gz_ref,
    ):
        step = pl.program_id(0)
        run, part = lax.div(step, per_run), lax.rem(step, per_run)
        grad = g_ref[...]
        at = lax.broadcasted_iota(jnp.int32, grad.shape, 0)
        hit = jnp.logical_and(at == tile - 1, part == per_run - 1)
        go_ref[...] = jnp.where(hit, grad + fix_ref[pl.ds(run, 1), :], grad).astype(BF)

        def project(first, second):
            rows = first.shape[2] // 2
            gz_ref[...] = times_back(go_ref[...], second, rows, 2 * rows)

        by_core(core_ref, mine_ref, other_ref, project)
        gate = jax.nn.sigmoid(r_ref[...])
        scaled = jnp.exp(k_ref[...]) * bonus_ref[...]
        inverse = 1.0 / (sb_ref[...] + scaled)
        answer = (sa_ref[...] + scaled * v_ref[...]) * inverse
        gated = gz_ref[...] * gate
        gr_ref[...] = (gated * answer * (1.0 - gate)).astype(BF)
        gn = gated * inverse
        gd = -gn * answer
        gn_ref[...] = gn
        gd_ref[...] = gd

        @pl.when(part == 0)
        def _():
            chain_ref[pl.ds(run, 1)] = jnp.zeros((1, 2, width), F32)

        places = (lax.broadcasted_iota(jnp.int32, (tile, 1), 0) + part * tile).astype(F32)
        weight = jnp.exp(-places * rate_ref[...]) * col(marks_ref[...], HEAD)
        sums = jnp.concatenate([summed_rows(weight * gn), summed_rows(weight * gd)], axis=0)
        chain_ref[pl.ds(run, 1)] += sums[None]

    block = pl.BlockSpec((tile, width), lambda i: (i, 0))
    half, full = jax.ShapeDtypeStruct((tokens, width), BF), jax.ShapeDtypeStruct((tokens, width), F32)
    return pl.pallas_call(
        body,
        grid=(tokens // tile,),
        in_specs=[
            SCALAR, block, fixed(fix.shape), block, block, block, block, block,
            pl.BlockSpec((tile, 8), lambda i: (i, 0)), fixed(rate.shape), fixed(bonus.shape),
            held(mine.shape), held(other.shape),
        ],
        out_specs=[block] * 4 + [fixed((runs, 2, width))],
        out_shape=[half, half, full, full, jax.ShapeDtypeStruct((runs, 2, width), F32)],
        scratch_shapes=[pltpu.VMEM((tile, width), F32)],
        compiler_params=params(),
        cost_estimate=cost(2 * tokens * width * width, 36 * tokens * width + 4 * mine.size),
    )(core, g, fix, k, v, r, sa, sb, marks, rate, bonus, mine, other)


def time_back(
    core, g, fix, s, lead, k, v, sa, sb, gn, gd, gr, leave, marks, lines, gain, bias, mix, rate, bonus,
    mine, other, length,
):
    tokens, width = s.shape
    tile = tile_rows(length)
    tiles, per_run = tokens // tile, length // tile
    runs = tokens // length

    def body(
        core_ref, g_ref, fix_ref, s_ref, lead_ref, k_ref, v_ref, sa_ref, sb_ref, gn_ref, gd_ref, gr_ref,
        leave_ref, marks_ref, line_ref, gain_ref, bias_ref, mix_ref, rate_ref, bonus_ref,
        mine_ref, other_ref, gk_ref, gv_ref, out_ref, edge_ref, small_ref,
        state_ref, after_ref, xk_ref, xv_ref, xr_ref,
    ):
        step = pl.program_id(0)
        i = tiles - 1 - step
        run, part = lax.div(i, per_run), lax.rem(i, per_run)

        @pl.when(part == per_run - 1)
        def _():
            state_ref[...] = leave_ref[pl.ds(run, 1)][0]
            after_ref[...] = jnp.zeros((1, width), F32)

        marks = marks_ref[...]
        alive = col(marks, ALIVE)
        places = lax.broadcasted_iota(jnp.int32, (tile, 1), 0).astype(F32)
        spread = places * rate_ref[...]
        falling, decay = jnp.exp(-spread), jnp.exp(-rate_ref[...])
        rising = jnp.exp(spread + rate_ref[...])
        at = lax.broadcasted_iota(jnp.int32, (tile, tile), 0)
        source = lax.broadcasted_iota(jnp.int32, (tile, tile), 1)
        same = col(marks, 7) == line_ref[0]
        mask = jnp.where(jnp.logical_and(same, source > at), 1.0, 0.0).astype(BF)
        gn, gd = gn_ref[...], gd_ref[...]
        carried = jnp.exp(spread - (tile - 1) * rate_ref[...]) * col(marks, LEAVES)
        ga = rising * split_sum(mask, falling * gn) + carried * state_ref[0:1, :]
        gb = rising * split_sum(mask, falling * gd) + carried * state_ref[1:2, :]
        first = alive[0:1, :]
        state_ref[0:1, :] = first * (gn[0:1, :] + decay * ga[0:1, :])
        state_ref[1:2, :] = first * (gd[0:1, :] + decay * gb[0:1, :])
        powered, content = jnp.exp(k_ref[...]), v_ref[...]
        scaled = powered * bonus_ref[...]
        reward = (gn * content + gd) * scaled
        gv_ref[...] = (gn * scaled + powered * ga).astype(BF)
        gk_ref[...] = (reward + powered * (content * ga + gb)).astype(BF)
        sums = [summed_rows(ga * sa_ref[...] + gb * sb_ref[...]), summed_rows(reward)]

        def project(first, second):
            rows = first.shape[2] // 2
            xk_ref[...] = times_back(gk_ref[...], first, 0, rows)
            xv_ref[...] = times_back(gv_ref[...], first, rows, 2 * rows)
            xr_ref[...] = times_back(gr_ref[...], second, 0, rows)

        by_core(core_ref, mine_ref, other_ref, project)
        grads = [xk_ref[...], xv_ref[...], xr_ref[...]]
        add, after, small = mixed_back(
            grads, s_ref[...].astype(F32), lead_ref[0], alive, gain_ref[...], bias_ref[...], mix_ref,
            after_ref[...],
        )
        after_ref[...] = after
        grad = g_ref[...]
        row = lax.broadcasted_iota(jnp.int32, grad.shape, 0)
        hit = jnp.logical_and(row == tile - 1, part == per_run - 1)
        out_ref[...] = jnp.where(hit, grad + fix_ref[pl.ds(run, 1), :], grad) + add
        edge_ref[pl.ds(run, 1), :] = after

        @pl.when(step == 0)
        def _():
            small_ref[...] = jnp.zeros_like(small_ref)

        for j, line in enumerate(small + sums):
            small_ref[j : j + 1, :] += line

    back = lambda i: tiles - 1 - i
    block = pl.BlockSpec((tile, width), lambda i: (back(i), 0))
    half, full = jax.ShapeDtypeStruct((tokens, width), BF), jax.ShapeDtypeStruct((tokens, width), F32)
    return pl.pallas_call(
        body,
        grid=(tiles,),
        in_specs=[
            SCALAR, block, fixed(fix.shape), block, pl.BlockSpec((1, 1, width), lambda i: (back(i), 0, 0)),
            block, block, block, block, block, block, block, fixed(leave.shape),
            pl.BlockSpec((tile, 8), lambda i: (back(i), 0)),
            pl.BlockSpec((1, 1, tile), lambda i: (back(i), 0, 0)),
            fixed(gain.shape), fixed(bias.shape), fixed(mix.shape), fixed(rate.shape), fixed(bonus.shape),
            held(mine.shape), held(other.shape),
        ],
        out_specs=[block, block, block, fixed(fix.shape), fixed((7, width))],
        out_shape=[
            half, half, full, jax.ShapeDtypeStruct(fix.shape, F32), jax.ShapeDtypeStruct((7, width), F32),
        ],
        scratch_shapes=[
            pltpu.VMEM((2, width), F32), pltpu.VMEM((1, width), F32),
            pltpu.VMEM((tile, width), F32), pltpu.VMEM((tile, width), F32), pltpu.VMEM((tile, width), F32),
        ],
        compiler_params=params(),
        cost_estimate=cost(8 * tokens * width * width, 46 * tokens * width + 4 * mine.size),
    )(
        core, g, fix, s, lead, k, v, sa, sb, gn, gd, gr, leave, marks, lines, gain, bias, mix, rate, bonus,
        mine, other,
    )


def weight_grads(first, second, grads, table):
    dp, seq = sizes()
    tokens, width = grads[0].shape
    rows, columns = width // dp, width // seq
    pairs = list(zip(first + second, grads))
    split, units = paired(), dp // 2
    if split:
        shapes = [(2, units * seq // 2, 2, 2 * rows, columns)] * 2
    else:
        shapes = [(2, seq, units, 2, 2 * rows, columns)]

    def body(table_ref, *refs):
        ins, rest = refs[: 2 * len(pairs)], refs[2 * len(pairs) :]
        outs, (x_ref, g_ref, stage_ref, sem, out_sem) = rest[: len(shapes)], rest[len(shapes) :]
        which, y = pl.program_id(0), pl.program_id(1)
        slot = lax.rem(which, 2)
        step = which * seq + y
        place = lax.rem(step, 2)

        def copies(i):
            return (
                pltpu.make_async_copy(ins[2 * i], x_ref.at[i % 2], sem.at[i % 2, 0]),
                pltpu.make_async_copy(ins[2 * i + 1], g_ref.at[i % 2], sem.at[i % 2, 1]),
            )

        def wait(at):
            target = outs[0].at[0, :, :, pl.ds(0, rows), :] if split else outs[0].at[0, 0, :, :, pl.ds(0, rows), :]
            pltpu.make_async_copy(stage_ref.at[at], target, out_sem.at[at]).wait()

        @pl.when(step == 0)
        def _():
            for copy in copies(0):
                copy.start()

        for i in range(len(pairs)):

            @pl.when(jnp.logical_and(which == i, y == 0))
            def _(i=i):
                for copy in copies(i):
                    copy.wait()
                if i + 1 < len(pairs):
                    for copy in copies(i + 1):
                        copy.start()

        @pl.when(step >= 2)
        def _():
            wait(place)

        at = pl.ds(pl.multiple_of(y * columns, columns), columns)
        grad = dot_tn(x_ref[slot], g_ref[slot, :, at])
        stage_ref[place] = grad.astype(BF).reshape(units, 2, rows, columns)
        store = lax.div(which, 2)
        span = pl.ds(pl.multiple_of(lax.rem(which, 2) * rows, 16), rows)
        if split:
            for unit in range(units):
                half = table_ref[SPOTS + 2 * store, y * units + unit]
                index = table_ref[SPOTS + 1 + 2 * store, y * units + unit]
                for side in range(2):

                    @pl.when(half == 1 - side)
                    def _(side=side, unit=unit, index=index):
                        pltpu.make_async_copy(
                            stage_ref.at[place, unit], outs[side].at[store, index, :, span, :], out_sem.at[place]
                        ).start()
        else:
            target = outs[0].at[store, y, :, :, span, :]
            pltpu.make_async_copy(stage_ref.at[place], target, out_sem.at[place]).start()

        @pl.when(step == len(pairs) * seq - 1)
        def _():
            wait(1 - place)
            wait(place)

    any_space = pl.BlockSpec(memory_space=pl.ANY)
    return pl.pallas_call(
        body,
        grid=(len(pairs), seq),
        in_specs=[SCALAR] + [any_space] * (2 * len(pairs)),
        out_specs=[any_space] * len(shapes),
        out_shape=[jax.ShapeDtypeStruct(shape, BF) for shape in shapes],
        scratch_shapes=[
            pltpu.VMEM((2, tokens, width), BF), pltpu.VMEM((2, tokens, width), BF),
            pltpu.VMEM((2, units, 2, rows, columns), BF),
            pltpu.SemaphoreType.DMA((2, 2)), pltpu.SemaphoreType.DMA((2,)),
        ],
        compiler_params=params(),
        cost_estimate=cost(8 * tokens * width * width, 16 * tokens * width + 8 * width * width),
    )(table, *[array for pair in pairs for array in pair])


def passed_along(array, axis, by):
    devices = lax.axis_size(axis)
    pairs = [(i, i + by) for i in range(devices) if 0 <= i + by < devices]
    return lax.ppermute(array, axis, pairs)


def entering(chain, ends, by):
    came = passed_along(ends, "seq", by)
    for _ in range(lax.axis_size("seq") - 2):
        came = passed_along(ends + chain * came, "seq", by)
    return came


def last_tokens(s, length):
    return s.reshape(-1, length, s.shape[-1])[:, -1].astype(F32)


def edge_norm(s, length, gain, bias):
    unit, _ = centred_norm(last_tokens(s, length))
    return passed_along(unit * gain + bias, "seq", 1)


def edge_back(edge, s, length, gain):
    came = passed_along(edge, "seq", -1)
    unit, rate = centred_norm(last_tokens(s, length))
    small = jnp.concatenate([summed_rows(came * unit), summed_rows(came)])
    return norm_back(came, unit, rate, gain), small


def cut_lookup(shard, grain):
    rows, columns = shard.shape
    width = min(512, columns // 2)
    cut = shard.reshape(rows, columns // (2 * grain), 2, grain).transpose(2, 0, 1, 3)
    cut = cut.reshape(2, rows, columns // 2 // width, width).transpose(0, 2, 1, 3)
    return cut.reshape(2, -1, width)


def join_lookup(first, second, rows, grain):
    width = first.shape[-1]
    cut = jnp.stack([first, second]).reshape(2, -1, rows, width).transpose(0, 2, 1, 3)
    cut = cut.reshape(2, rows, -1, grain).transpose(1, 2, 0, 3)
    return cut.reshape(rows, -1)


def spots_of(shards):
    return [0] + np.cumsum([shard.shape[0] for shard in shards]).tolist()


def cut_at(array, spots):
    return [array[a:b] for a, b in zip(spots, spots[1:])]


def gather_plain(first, second):
    dp, seq = sizes()
    whole = lambda a: (lax.all_gather(a, ("seq", "dp")).reshape((seq, dp) + a.shape), 0)
    return [whole(a) for a in first], [whole(a) for a in second]


def scatter_plain(stores):
    dp, seq = sizes()
    take = lambda a: lax.psum_scatter(
        a.reshape((seq * dp,) + a.shape[-2:]), ("seq", "dp"), scatter_dimension=0
    ).astype(F32)
    return [take(s[0]) for s in stores], [take(s[1]) for s in stores]


def by_half(first_is_low, low, high):
    return jnp.where(first_is_low, low, high), jnp.where(first_is_low, high, low)


def partner_y(array):
    return lax.ppermute(array, "seq", [(0, 1), (1, 0)])


def rows_cut(array):
    half = array.shape[0] // 2
    return by_half(lax.axis_index("seq") == 0, array[:half], array[half:])


def rows_joined(kept, came):
    low = lax.axis_index("seq") == 0
    return jnp.concatenate(by_half(low, kept, came), axis=1)


def runs_cut(array):
    length = array.shape[1] // 2
    return by_half(lax.axis_index("seq") == 0, array[:, :length], array[:, length:])


def runs_joined(kept, came):
    low = lax.axis_index("seq") == 0
    return jnp.concatenate(by_half(low, kept, came), axis=0)


def per_device(
    entering_activations,
    document_numbers,
    result_cotangent,
    normalizer_scales,
    normalizer_offsets,
    shift_blend_factors,
    fading_natural_logs_per_feature,
    feature_reward_logs,
    attention_triple_matrix,
    attention_result_matrix,
    channelmix_lookup_matrix,
    channelmix_content_matrix,
    channelmix_accept_matrix,
):
    dp, seq = sizes()
    staged = paired()
    core = core_of()
    cores = core.reshape(1)
    table = unit_tables() if staged else jnp.zeros((1, 1), jnp.int32)
    layers = attention_triple_matrix.shape[0]
    runs, length, width = entering_activations.shape
    tokens, columns = runs * length, width // seq
    swapped = staged and layers == 2 and runs % 2 == 0
    if swapped:
        kept_rows, sent_rows = rows_cut(document_numbers)
        document_numbers = rows_joined(kept_rows, partner_y(sent_rows))
        kept_rows, sent_rows = rows_cut(entering_activations)
        entering_activations = rows_joined(kept_rows, partner_y(sent_rows))
        runs, length = runs // 2, length * 2

    lookup_rows = channelmix_lookup_matrix.shape[1]
    grain = channelmix_content_matrix.shape[1] // 2
    half_rows = channelmix_accept_matrix.shape[1] // 2

    shards = []
    for depth in range(layers):
        triple, result = attention_triple_matrix[depth], attention_result_matrix[depth]
        lookup = cut_lookup(channelmix_lookup_matrix[depth], grain)
        content, accept = channelmix_content_matrix[depth], channelmix_accept_matrix[depth]
        shards.append(([jnp.concatenate([triple[0], triple[1]])], [jnp.concatenate([triple[2], result])]))
        shards.append(
            (
                [lookup[0], content[:grain], accept[:half_rows]],
                [lookup[1], content[grain:], accept[half_rows:]],
            )
        )

    held = {}
    if staged:
        first = jnp.concatenate([shard for group in shards for shard in group[0]])
        second = jnp.concatenate([shard for group in shards for shard in group[1]])
        kept = jnp.where(core == 0, first, second)
        came = moved(jnp.where(core == 0, second, first), to_core)
        pair = jnp.where(core == 0, jnp.stack([kept, came]), jnp.stack([came, kept]))
        ends = spots_of([jnp.concatenate(group[0]) for group in shards])
        moves = [Gathering(table, pair[:, a:b]) for a, b in zip(ends, ends[1:])]
    else:
        moves = [gather_plain(*group) for group in shards]

    def give_att(depth, mine, other):
        held["att", depth] = (mine, other)

    def give_chan(depth, mine, other):
        takes = [array[:, :, at : at + half_rows] for array, at in (mine[2], other[2])]
        first = jnp.where(core == 0, takes[0], takes[1])
        second = jnp.where(core == 0, takes[1], takes[0])
        held["cut", depth] = Cut(mine[0], mine[1], lookup_rows, grain)
        held["chan", depth] = (mine, other, jnp.concatenate([first, second], axis=2))

    def with_rows(array, group):
        return [(array, at) for at in spots_of(shards[group][0])[:-1]]

    if swapped:
        border = jnp.full((runs, 1), -1, document_numbers.dtype)
    else:
        border = passed_along(document_numbers[:, -1:] + 1, "seq", 1) - 1
    earlier = jnp.concatenate([border, document_numbers[:, :-1]], axis=1)
    edges = jnp.zeros((runs, width), F32)
    states = jnp.zeros((runs, 2, width), F32)
    marks, lines = token_marks(document_numbers, earlier)
    through = (earlier[:, :1] == document_numbers[:, -1:]).astype(F32)[:, :, None]
    begins = (earlier[:, :1] == document_numbers[:, :1]).astype(F32)[:, :, None]
    rates = jnp.exp(fading_natural_logs_per_feature)
    bonuses = jnp.exp(feature_reward_logs)

    def layer_values(depth):
        gain, bias, mix = normalizer_scales[depth], normalizer_offsets[depth], shift_blend_factors[depth]
        rate, bonus = rates[depth : depth + 1], bonuses[depth : depth + 1]
        return gain, bias, mix, rate, bonus, jnp.exp(-length * rate)[None] * through

    kept = {}

    def run_time_in(depth, flow):
        gain, bias, mix, rate, _, _ = layer_values(depth)
        before = edges if swapped else edge_norm(flow, length, gain[0], bias[0])
        kept["time", depth] = (flow,) + tuple(
            time_in(
                cores, flow, before, marks, gain[0:1], bias[0:1], mix[:3], rate, *held["att", depth], length
            )
        )
        return kept["time", depth][4]

    def run_time_out(depth, *after):
        _, _, _, rate, bonus, chain = layer_values(depth)
        flow, xk, xv, xr, k, v, r, ends, lead = kept["time", depth]
        enter = states if swapped else entering(chain, ends, 1)
        k = tie(k, *after) if after else k
        z, sa, sb, middle = time_out(
            cores, flow, k, v, r, enter, marks, lines, rate, bonus, *held["att", depth], length
        )
        kept["time", depth] = (flow, lead, xk, xv, xr, k, v, r, z, sa, sb)
        gain, bias, _, _, _, _ = layer_values(depth)
        before = edges if swapped else edge_norm(middle, length, gain[1], bias[1])
        kept["middle", depth] = (middle, before)
        return middle

    def run_channel_one(depth, mine, cut, *after):
        gain, bias, mix, _, _, _ = layer_values(depth)
        middle, before = kept["middle", depth]
        before = tie(before, *after) if after else before
        kept["one", depth] = channel_one(
            middle, before, marks, gain[1:2], bias[1:2], mix[3:], mine[0], mine[1], cut, length
        )
        return kept["one", depth][4]

    def run_channel_two(depth, *after):
        middle, _ = kept["middle", depth]
        xk, xr, lead, act0, total = kept["one", depth]
        _, other, accept = held["chan", depth]
        total = tie(total, *after) if after else total
        kind = BF if depth == layers - 1 else F32
        act1, carried, gate, flow = channel_two(
            middle, xk, xr, total, other[0], other[1], accept, held["cut", depth], kind
        )
        kept["chan", depth] = (middle, lead, xk, xr, (act0, act1), carried, gate)
        return flow

    flow = entering_activations.reshape(tokens, width)
    if staged and layers == 2:
        att0, chan0, att1, chan1 = moves

        def place_att(depth, move):
            give_att(depth, *move.swap())

        def place_chan(depth, move, group):
            mine, other = move.swap()
            give_chan(depth, with_rows(mine, group), with_rows(other, group))

        att0.z()
        chan0.z(att0.end_z())
        att0.second(flow)
        far = att0.third(chan0.parts[0])
        att0.arrange()
        att0.mine = tie(att0.mine, chan0.parts)
        chan0.end_z(far)
        near = chan0.second()
        place_att(0, att0)
        done = run_time_in(0, flow)
        far = chan0.third(done)
        att1.z(done)
        done = run_time_out(0, near)
        line = att1.end_z(done)
        chan1.z(line)
        near = att1.second(far, done)
        mine = chan0.arrange(done, line, chan1.parts)
        place_chan(0, chan0, 1)
        far = att1.third(mine)
        own, _, _ = held["chan", 0]
        done = run_channel_one(0, own, held["cut", 0], near)
        line = chan1.end_z(done)
        near = chan1.second(far)
        mine = att1.arrange(done, line)
        place_att(1, att1)
        flow = run_channel_two(0, mine)
        far = chan1.third(flow)
        done = run_time_in(1, tie(flow, near))
        done = run_time_out(1)
        chan1.arrange(done)
        place_chan(1, chan1, 3)
        own, _, _ = held["chan", 1]
        run_channel_one(1, own, held["cut", 1])
        y_out = run_channel_two(1)
        if swapped:
            kept_rows, sent_rows = rows_cut(tie(result_cotangent, far))
            result_cotangent = rows_joined(kept_rows, partner_y(sent_rows))
            kept_runs, sent_runs = runs_cut(y_out.reshape(runs, length, width))
            y_out = runs_joined(kept_runs, partner_y(sent_runs))
    else:
        for depth in range(layers):
            if staged:
                for move in moves[2 * depth : 2 * depth + 2]:
                    move.z()
                    move.end_z()
                    move.second()
                    move.third()
                    move.arrange()
                give_att(depth, *moves[2 * depth].swap())
                mine, other = moves[2 * depth + 1].swap()
                group = 2 * depth + 1
                give_chan(depth, with_rows(mine, group), with_rows(other, group))
            else:
                mine, other = moves[2 * depth]
                give_att(depth, mine[0][0], other[0][0])
                give_chan(depth, *moves[2 * depth + 1])
            run_time_in(depth, flow)
            run_time_out(depth)
            run_channel_one(depth, held["chan", depth][0], held["cut", depth])
            flow = run_channel_two(depth)
        y_out = flow

    grad = result_cotangent.reshape(tokens, width)
    fix = jnp.zeros((runs, width), F32)
    small = [None] * layers
    sums = {}
    earlier_chan = earlier_att = None
    for depth in reversed(range(layers)):
        gain, bias, mix, rate, bonus, chain = layer_values(depth)
        flow, lead_t, xk_t, xv_t, xr_t, k, v, r, z, sa, sb = kept["time", depth]
        middle, lead, xk, xr, acts, carried, gate = kept["chan", depth]
        mine, other, accept = held["chan", depth]
        cut = held["cut", depth]
        part_rows = [cut.blocks * lookup_rows, grain, half_rows]
        part_spots = [0, part_rows[0], part_rows[0] + grain, part_rows[0] + grain + half_rows]
        if staged:
            packing = [(2, seq * dp // 4, 2, part_spots[3], columns)] * 2, part_spots
        else:
            widths = [cut.width, columns, columns]
            packing = [(2, seq, dp // 2, 2, n, w) for n, w in zip(part_rows, widths)], [0, 0, 0]
        *stores, grad, edge, small_chan = channel_back(
            cores, grad, fix, middle, lead, marks, gain[1:2], bias[1:2], mix[3:], gate, carried, xk, xr,
            acts, (mine[0], other[0]), (mine[1], other[1]), accept, cut, length, packing, table,
        )
        out_grad = grad
        if staged:
            flat = [s.reshape((2, seq * dp // 4, 2 * part_spots[3], columns)) for s in stores]
            if earlier_att:
                line = earlier_chan.end_second(grad)
                earlier_chan.z()
                away = earlier_att.third(line)
                edge, out_grad = tie((edge, grad), away)
                flat = tie(flat, away)
            elif swapped:
                edge, out_grad = tie((edge, grad), y_out)
                flat = tie(flat, y_out)
            chan_move = Scattering(*flat)
        if swapped:
            fix, edge_chan = edges, jnp.zeros((2, width), F32)
        else:
            fix, edge_chan = edge_back(edge, middle, length, gain[1])
        mine, other = held["att", depth]
        go, gr, gn, gd, ends = out_back(
            cores, out_grad, fix, k, v, r, sa, sb, marks, rate, bonus, mine, other, length
        )
        if staged:
            if earlier_att:
                near = earlier_att.end_third(go)
                earlier_att.second()
                go = tie(go, near, earlier_chan.parts[0])
            away = chan_move.third(go)
            gn = tie(gn, away)
        leave = states if swapped else entering(chain, begins * ends, -1)
        gk, gv, grad, edge, small_time = time_back(
            cores, grad, fix, flow, lead_t, k, v, sa, sb, gn, gd, gr, leave, marks, lines,
            gain[0:1], bias[0:1], mix[:3], rate, bonus, mine, other, length,
        )
        fading = small_time[5:6] * -rate * jnp.exp(-rate)
        small[depth] = jnp.concatenate(
            [
                small_time[0:1],
                small_chan[0:1] + edge_chan[0:1],
                small_time[1:2],
                small_chan[1:2] + edge_chan[1:2],
                small_time[2:5],
                small_chan[2:4],
                fading,
                small_time[6:7],
            ]
        )
        first_hop = None
        if staged and depth == 0:
            first_hop = hop_y(jnp.stack(small))
        if staged and earlier_chan:
            gk, gv = tie((gk, gv), earlier_chan.parts)
        stores_att = weight_grads([xk_t, xv_t], [xr_t, z], [gk, gv, gr, go], table)
        rows = width // dp
        if staged:
            more = []
            if depth == 0:
                sums_xy = hop_x(tie(first_hop, stores_att[0]))
                more.append(sums_xy)
            near = chan_move.end_third(stores_att[0], *more)
            if earlier_att:
                near = tie(near, earlier_att.end_second(near))
                earlier_att.z()
            flat = [s.reshape((2, seq * dp // 4, 4 * rows, columns)) for s in stores_att]
            att_move = Scattering(*tie(flat, near))
            chan_move.second()
            grad = tie(grad, near)
            if depth > 0:
                earlier_chan, earlier_att = chan_move, att_move
            sums["chan", depth], sums["att", depth] = chan_move, att_move
        else:
            sums["chan", depth] = scatter_plain(stores)
            sums["att", depth] = scatter_plain(stores_att)
        if swapped:
            edge_time = jnp.zeros((2, width), F32)
        else:
            fix, edge_time = edge_back(edge, flow, length, gain[0])
            small[depth] = small[depth].at[0].add(edge_time[0]).at[2].add(edge_time[1])
    small = jnp.stack(small)
    grad = grad.reshape(runs, length, width)
    if not swapped:
        grad = grad.at[:, -1].add(fix)
    if staged:
        last_chan, last_att = sums["chan", 0], sums["att", 0]
        sums_xy = sums_xy + moved(sums_xy, to_core)
        away, parts = last_att.away, earlier_att.parts
        line = last_chan.end_second(away)
        last_att.third(line, parts)
        last_chan.z(away, parts)
        small = summed_z(tie(sums_xy, line))
        last_att.end_third()
        last_att.second(last_chan.parts[0])
        line = last_att.end_second()
        last_att.z()
        small = tie(small, last_att.parts)
        for move in (earlier_chan, earlier_att, last_chan):
            move.parts = tie(move.parts, line)
        if swapped:
            kept_runs, sent_runs = runs_cut(tie(grad, line))
            came = partner_y(sent_runs.astype(BF))
            grad = runs_joined(kept_runs, came.astype(F32))
        for name in list(sums):
            first, second = sums[name].end_z(core)
            spots = part_spots if name[0] == "chan" else [0, 2 * rows]
            sums[name] = (cut_at(first, spots), cut_at(second, spots)) if name[0] == "chan" else ([first], [second])
    else:
        small = lax.psum(small, BOTH)
    large = []
    for depth in range(layers):
        first, second = sums["att", depth]
        triple = jnp.stack([first[0][:rows], first[0][rows:], second[0][:rows]])
        result = second[0][rows:]
        first, second = sums["chan", depth]
        lookup = join_lookup(first[0], second[0], lookup_rows, grain)
        content = jnp.concatenate([first[1], second[1]])
        large.append((triple, result, lookup, content, jnp.concatenate([first[2], second[2]])))
    large = [jnp.stack(members) for members in zip(*large)]
    return (
        y_out if swapped else y_out.reshape(runs, length, width),
        grad,
        small[:, 0:2],
        small[:, 2:4],
        small[:, 4:9],
        small[:, 9],
        small[:, 10],
        *large,
    )


def solution(mesh):
    return jax.shard_map(
        per_device,
        mesh=mesh,
        in_specs=(
            P("dp", "seq", None),
            P("dp", "seq"),
            P("dp", "seq", None),
            P(),
            P(),
            P(),
            P(),
            P(),
            P(None, None, "dp", "seq"),
            P(None, "dp", "seq"),
            P(None, "dp", "seq"),
            P(None, "dp", "seq"),
            P(None, "dp", "seq"),
        ),
        out_specs=(
            P("dp", "seq", None),
            P("dp", "seq", None),
            P(),
            P(),
            P(),
            P(),
            P(),
            P(None, None, "dp", "seq"),
            P(None, "dp", "seq"),
            P(None, "dp", "seq"),
            P(None, "dp", "seq"),
            P(None, "dp", "seq"),
        ),
        check_vma=False,
    )
```

```python
import jax
import jax.numpy as jnp
import numpy as np
from jax import lax
from jax.experimental import pallas as pl
from jax.experimental.pallas import tpu as pltpu
from jax.sharding import PartitionSpec as P

EPS = 1e-05
BF = jnp.bfloat16
F32 = jnp.float32
BOTH = ("dp", "seq")
VMEM = 58 * 2**20


def sizes():
    return lax.axis_size("dp"), lax.axis_size("seq")


def paired():
    dp, seq = sizes()
    return seq == 2 and dp % 4 == 0


def place(d):
    return d // 4, d // 2 % 2, d % 2


def core_of():
    if not paired():
        return jnp.int32(0)
    return lax.rem(lax.axis_index("dp"), 2)


def moved(array, target):
    dp, seq = sizes()
    pairs = []
    for d in range(dp):
        for y in range(seq):
            z, x, c, y2 = target(*place(d), y)
            pairs.append((d * seq + y, (z * 4 + x * 2 + c) * seq + y2))
    return lax.ppermute(array, BOTH, pairs)


def to_core(z, x, c, y):
    return z, x, 1 - c, y


def to_second(z, x, c, y):
    return (z, 1 - x, c, y) if c == 0 else (z, x, c, 1 - y)


def to_third(z, x, c, y):
    return (z, x, c, 1 - y) if c == 0 else (z, 1 - x, c, y)


def along_z(step):
    depth = sizes()[0] // 4

    def target(z, x, c, y):
        return (z + step) % depth, x, c, y

    return target


def unit_spots(z, x, c, y):
    depth = sizes()[0] // 4
    half, index = [], []
    for yy in range(2):
        for zz in range(depth):
            for xx in range(2):
                dx, dy, dz = xx ^ x, yy ^ y, (z - zz) % depth
                half.append(dy if c == 0 else dx)
                index.append((dx if c == 0 else dy) * depth + dz)
    return half, index


def unit_tables():
    dp, seq = sizes()
    rows = []
    for d in range(dp):
        for y in range(seq):
            z, x, c = place(d)
            half, index = unit_spots(z, x, c, y)
            lines = [half]
            for side in range(2):
                line, last = [], [i for i, h in zip(index, half) if h == side][0]
                for i, h in zip(index, half):
                    last = i if h == side else last
                    line.append(last)
                lines.append(line)
            for core in range(2):
                lines.extend(unit_spots(z, x, core, y))
            rows.append(lines)
    table = jnp.asarray(np.array(rows, np.int32))
    me = lax.axis_index("dp") * seq + lax.axis_index("seq")
    return lax.dynamic_index_in_dim(table, me, 0, keepdims=False)


SPOTS = 3


def arrange(table, own, other):
    units, block = 2 * own.shape[0], (1,) + own.shape[1:]

    def body(table_ref, own_ref, other_ref, out_ref):
        half = table_ref[0, pl.program_id(0)]

        @pl.when(half == 0)
        def _():
            out_ref[...] = own_ref[...]

        @pl.when(half == 1)
        def _():
            out_ref[...] = other_ref[...]

    return pl.pallas_call(
        body,
        grid_spec=pltpu.PrefetchScalarGridSpec(
            num_scalar_prefetch=1,
            grid=(units,),
            in_specs=[
                pl.BlockSpec(block, lambda i, t: (t[1, i], 0, 0)),
                pl.BlockSpec(block, lambda i, t: (t[2, i], 0, 0)),
            ],
            out_specs=pl.BlockSpec(block, lambda i, t: (i, 0, 0)),
        ),
        out_shape=jax.ShapeDtypeStruct((units,) + own.shape[1:], own.dtype),
        compiler_params=pltpu.CompilerParams(vmem_limit_bytes=VMEM),
        cost_estimate=pl.CostEstimate(flops=1, bytes_accessed=1, transcendentals=0),
    )(table, own, other)


def tie(arrays, *others):
    return lax.optimization_barrier((arrays, others))[0]


class Gathering:
    def __init__(self, table, pair):
        self.table, self.pair, self.depth = table, pair, sizes()[0] // 4

    def z(self, *after):
        pair = tie(self.pair, *after)
        self.parts = [moved(pair, along_z(step)) for step in range(1, self.depth)]

    def end_z(self, *after):
        line = jnp.stack([self.pair] + tie(self.parts, *after))
        self.line = line.reshape((self.depth, -1) + line.shape[3:])
        return self.line

    def second(self, *after):
        self.came = moved(tie(self.line, *after), to_second)
        return self.came

    def third(self, *after):
        self.half = jnp.concatenate(tie([self.line, self.came], *after))
        self.far = moved(self.half, to_third)
        return self.far

    def arrange(self, *after):
        self.mine = arrange(self.table, *tie((self.half, self.far), *after))
        return self.mine

    def swap(self):
        dp, seq = sizes()
        other = moved(self.mine, to_core)
        shape = (seq, dp, self.mine.shape[1] // 2) + self.mine.shape[2:]
        return self.mine.reshape(shape), other.reshape(shape)


class Scattering:
    def __init__(self, away, keep):
        self.depth = sizes()[0] // 4
        groups = [[2 * i, 2 * i + 1] for i in range(sizes()[0] // 2)]
        self.take = lambda array: lax.psum_scatter(array, "dp", scatter_dimension=0, axis_index_groups=groups)
        self.away, self.keep = self.take(away), keep

    def third(self, *after):
        self.away = tie(self.away, *after)
        self.keep = self.take(tie(self.keep, self.away))
        self.came = moved(self.away, to_third)
        return self.away

    def end_third(self, *after):
        depth, keep, came = self.depth, *tie((self.keep, self.came), *after)
        self.away = (keep[depth:].astype(F32) + came[depth:].astype(F32)).astype(BF)
        self.keep = (keep[:depth].astype(F32) + came[:depth].astype(F32)).astype(BF)
        return self.away

    def second(self, *after):
        self.came = moved(tie(self.away, *after), to_second)

    def end_second(self, *after):
        keep, came = tie((self.keep, self.came), *after)
        self.line = (keep.astype(F32) + came.astype(F32)).astype(BF)
        return self.line

    def z(self, *after):
        line = tie(self.line, *after)
        self.parts = [moved(line[step], along_z(-step)) for step in range(1, self.depth)]
        return self.parts

    def total(self):
        total = self.line[0].astype(F32)
        for part in self.parts:
            total = total + part.astype(F32)
        return total.reshape((2, -1) + total.shape[1:])


def summed_z(array):
    depth = sizes()[0] // 4
    if depth == 4:
        for bit in (1, 2):
            array = array + moved(array, lambda z, x, c, y, bit=bit: (z ^ bit, x, c, y))
        return array
    total = array
    for step in range(1, depth):
        total = total + moved(array, along_z(step))
    return total


def hop_y(array):
    return array + moved(array, lambda z, x, c, y: (z, x, c, 1 - y))


def hop_x(array):
    return array + moved(array, lambda z, x, c, y: (z, 1 - x, c, y))


def params(**more):
    return pltpu.CompilerParams(vmem_limit_bytes=VMEM, **more)


def cost(flops, bytes_accessed):
    return pl.CostEstimate(flops=1, bytes_accessed=1, transcendentals=0)


def held(shape):
    zeros = (0,) * len(shape)
    return pl.BlockSpec(shape, lambda *_: zeros, pipeline_mode=pl.Buffered(1))


def fixed(shape):
    zeros = (0,) * len(shape)
    return pl.BlockSpec(shape, lambda *_: zeros)


SCALAR = pl.BlockSpec(memory_space=pltpu.SMEM)


def dot(a, b):
    return lax.dot_general(a, b, (((1,), (0,)), ((), ())), preferred_element_type=F32)


def dot_nt(a, b):
    return lax.dot_general(a, b, (((1,), (1,)), ((), ())), preferred_element_type=F32)


def dot_tn(a, b):
    return lax.dot_general(a, b, (((0,), (0,)), ((), ())), preferred_element_type=F32)


def split_sum(mask, terms):
    high = terms.astype(BF)
    low = (terms - high.astype(F32)).astype(BF)
    return dot(mask, high) + dot(mask, low)


def centred_norm(s):
    centred = s - jnp.mean(s, axis=-1, keepdims=True)
    rate = lax.rsqrt(jnp.mean(centred * centred, axis=-1, keepdims=True) + EPS)
    return centred * rate, rate


def norm_back(grad, unit, rate, gain):
    grad = grad * gain
    return rate * (
        grad
        - jnp.mean(grad, axis=-1, keepdims=True)
        - unit * jnp.mean(grad * unit, axis=-1, keepdims=True)
    )


def down_one(tile, first):
    rows = lax.broadcasted_iota(jnp.int32, tile.shape, 0)
    return jnp.where(rows == 0, first, pltpu.roll(tile, 1, 0))


def up_one(tile, last):
    size = tile.shape[0]
    rows = lax.broadcasted_iota(jnp.int32, tile.shape, 0)
    return jnp.where(rows == size - 1, last, pltpu.roll(tile, size - 1, 0))


def summed_rows(tile):
    return jnp.sum(tile, axis=0, keepdims=True)


def times(x, store, lo, hi, out_ref, rows=slice(None)):
    seq, dp, _, columns = store.shape
    for y in range(seq):
        weight = store[y, :, lo:hi, :].reshape(dp * (hi - lo), columns)
        out_ref[rows, y * columns : (y + 1) * columns] = dot(x, weight)


def times_back(g, store, lo, hi):
    seq, dp, _, columns = store.shape
    total = None
    for y in range(seq):
        weight = store[y, :, lo:hi, :].reshape(dp * (hi - lo), columns)
        part = dot_nt(g[:, y * columns : (y + 1) * columns], weight)
        total = part if total is None else total + part
    return total


def by_core(core_ref, mine, other, run):
    @pl.when(core_ref[0] == 0)
    def _():
        run(mine, other)

    @pl.when(core_ref[0] != 0)
    def _():
        run(other, mine)


def tile_rows(length):
    return min(256, length)


ALIVE, ENTERS, TAIL, HEAD, LEAVES = range(5)


def col(marks, which):
    return marks[:, which : which + 1]


def token_marks(document_numbers, earlier):
    rows, length = document_numbers.shape
    tile = tile_rows(length)
    tiles = document_numbers.reshape(rows, length // tile, tile)
    before = earlier.reshape(tiles.shape)[:, :, :1]
    marks = [
        document_numbers == earlier,
        (tiles == before).reshape(rows, length),
        document_numbers == document_numbers[:, -1:],
        document_numbers == document_numbers[:, :1],
        (tiles == tiles[:, :, -1:]).reshape(rows, length),
        jnp.zeros_like(document_numbers, dtype=bool),
        jnp.zeros_like(document_numbers, dtype=bool),
    ]
    marks = [m.astype(F32) for m in marks] + [document_numbers.astype(F32)]
    marks = jnp.stack(marks, axis=-1).reshape(rows * length, 8)
    lines = document_numbers.astype(F32).reshape(rows * length // tile, 1, tile)
    return marks, lines


def time_in(core, s, before, marks, gain, bias, mix, rate, mine, other, length):
    tokens, width = s.shape
    tile = tile_rows(length)
    per_run = length // tile
    runs = tokens // length

    def body(
        core_ref, s_ref, before_ref, marks_ref, gain_ref, bias_ref, mix_ref, rate_ref,
        mine_ref, other_ref,
        xk_ref, xv_ref, xr_ref, k_ref, v_ref, r_ref, end_ref, lead_ref, carry_ref,
    ):
        step = pl.program_id(0)
        run, part = lax.div(step, per_run), lax.rem(step, per_run)
        unit, _ = centred_norm(s_ref[...].astype(F32))
        normed = unit * gain_ref[...] + bias_ref[...]

        @pl.when(part == 0)
        def _():
            carry_ref[...] = before_ref[pl.ds(run, 1), :]
            end_ref[pl.ds(run, 1)] = jnp.zeros((1, 2, width), F32)

        lead_ref[0] = carry_ref[...]
        shifted = down_one(normed, carry_ref[...]) * col(marks_ref[...], ALIVE)
        carry_ref[...] = normed[tile - 1 :, :]
        change = normed - shifted
        xk_ref[...] = (shifted + mix_ref[0:1, :] * change).astype(BF)
        xv_ref[...] = (shifted + mix_ref[1:2, :] * change).astype(BF)
        xr_ref[...] = (shifted + mix_ref[2:3, :] * change).astype(BF)

        def project(first, second):
            rows = first.shape[2] // 2
            times(xk_ref[...], first, 0, rows, k_ref)
            times(xv_ref[...], first, rows, 2 * rows, v_ref)
            times(xr_ref[...], second, 0, rows, r_ref)

        by_core(core_ref, mine_ref, other_ref, project)
        places = lax.broadcasted_iota(jnp.int32, (tile, 1), 0).astype(F32)
        left = (length - 1 - part * tile).astype(F32) - places
        weight = jnp.exp(k_ref[...] - left * rate_ref[...]) * col(marks_ref[...], TAIL)
        ends = jnp.concatenate([summed_rows(weight * v_ref[...]), summed_rows(weight)], axis=0)
        end_ref[pl.ds(run, 1)] += ends[None]

    block = pl.BlockSpec((tile, width), lambda i: (i, 0))
    half, full = jax.ShapeDtypeStruct((tokens, width), BF), jax.ShapeDtypeStruct((tokens, width), F32)
    return pl.pallas_call(
        body,
        grid=(tokens // tile,),
        in_specs=[
            SCALAR, block, fixed(before.shape), pl.BlockSpec((tile, 8), lambda i: (i, 0)),
            fixed(gain.shape), fixed(bias.shape), fixed(mix.shape), fixed(rate.shape),
            held(mine.shape), held(other.shape),
        ],
        out_specs=[block] * 6 + [fixed((runs, 2, width)), pl.BlockSpec((1, 1, width), lambda i: (i, 0, 0))],
        out_shape=[half] * 3 + [full] * 3 + [
            jax.ShapeDtypeStruct((runs, 2, width), F32),
            jax.ShapeDtypeStruct((tokens // tile, 1, width), F32),
        ],
        scratch_shapes=[pltpu.VMEM((1, width), F32)],
        compiler_params=params(),
        cost_estimate=cost(6 * tokens * width * width, 22 * tokens * width + 4 * mine.size),
    )(core, s, before, marks, gain, bias, mix, rate, mine, other)


def time_out(core, s, k, v, r, enter, marks, lines, rate, bonus, mine, other, length):
    tokens, width = s.shape
    tile = tile_rows(length)
    per_run = length // tile

    def body(
        core_ref, s_ref, k_ref, v_ref, r_ref, enter_ref, marks_ref, line_ref, rate_ref, bonus_ref,
        mine_ref, other_ref, z_ref, sa_ref, sb_ref, out_ref, state_ref,
    ):
        step = pl.program_id(0)
        run, part = lax.div(step, per_run), lax.rem(step, per_run)

        @pl.when(part == 0)
        def _():
            state_ref[...] = enter_ref[pl.ds(run, 1)][0]

        marks = marks_ref[...]
        places = lax.broadcasted_iota(jnp.int32, (tile, 1), 0).astype(F32)
        spread = places * rate_ref[...]
        falling, decay = jnp.exp(-spread), jnp.exp(-rate_ref[...])
        powered = jnp.exp(k_ref[...])
        content = v_ref[...]
        raised = jnp.exp(k_ref[...] + spread)
        at = lax.broadcasted_iota(jnp.int32, (tile, tile), 0)
        source = lax.broadcasted_iota(jnp.int32, (tile, tile), 1)
        same = col(marks, 7) == line_ref[0]
        mask = jnp.where(jnp.logical_and(same, source < at), 1.0, 0.0).astype(BF)
        carried = falling * col(marks, ENTERS)
        ahead = falling * jnp.exp(rate_ref[...])
        state_a = ahead * split_sum(mask, raised * content) + carried * state_ref[0:1, :]
        state_b = ahead * split_sum(mask, raised) + carried * state_ref[1:2, :]
        sa_ref[...] = state_a
        sb_ref[...] = state_b
        state_ref[0:1, :] = decay * state_a[tile - 1 :] + (powered * content)[tile - 1 :]
        state_ref[1:2, :] = decay * state_b[tile - 1 :] + powered[tile - 1 :]
        scaled = powered * bonus_ref[...]
        answer = (state_a + scaled * content) / (state_b + scaled)
        z_ref[...] = (jax.nn.sigmoid(r_ref[...]) * answer).astype(BF)

        def project(first, second):
            rows = first.shape[2] // 2
            times(z_ref[...], second, rows, 2 * rows, out_ref)

        by_core(core_ref, mine_ref, other_ref, project)
        out_ref[...] += s_ref[...].astype(F32)

    block = pl.BlockSpec((tile, width), lambda i: (i, 0))
    half, full = jax.ShapeDtypeStruct((tokens, width), BF), jax.ShapeDtypeStruct((tokens, width), F32)
    return pl.pallas_call(
        body,
        grid=(tokens // tile,),
        in_specs=[
            SCALAR, block, block, block, block, fixed(enter.shape),
            pl.BlockSpec((tile, 8), lambda i: (i, 0)), pl.BlockSpec((1, 1, tile), lambda i: (i, 0, 0)),
            fixed(rate.shape), fixed(bonus.shape), held(mine.shape), held(other.shape),
        ],
        out_specs=[block] * 4,
        out_shape=[half, full, full, full],
        scratch_shapes=[pltpu.VMEM((2, width), F32)],
        compiler_params=params(),
        cost_estimate=cost(4 * tokens * width * width, 30 * tokens * width + 4 * mine.size),
    )(core, s, k, v, r, enter, marks, lines, rate, bonus, mine, other)


def lookup_block(store, rows, blocks, step):
    seq, dp, _, width = store.shape
    return pl.BlockSpec(
        (1, dp, rows, width), lambda i: (lax.div(step(i), blocks), 0, lax.rem(step(i), blocks), 0)
    )


def content_block(store, grain, at, group, step):
    seq, _, _, columns = store.shape
    return pl.BlockSpec((seq, group, grain, columns), lambda i: (0, step(i), at // grain, 0))


class Cut:
    def __init__(self, lookup, content, lookup_rows, grain):
        store, _ = lookup
        seq, dp, _, self.width = store.shape
        self.rows, self.grain = lookup_rows, grain
        self.group = self.width // grain
        self.steps = dp // self.group
        self.blocks = self.steps // seq
        self.at = content[1]

    def specs(self, lookup, content, step):
        return [
            lookup_block(lookup[0], self.rows, self.blocks, step),
            content_block(content[0], self.grain, self.at, self.group, step),
        ]


def hidden_step(x_ref, lookup_ref, content_ref, act_ref, total_ref, first):
    tokens = x_ref.shape[0]
    tile = min(256, tokens)
    _, dp, rows, width = lookup_ref.shape
    seq, group, grain, columns = content_ref.shape
    up = lookup_ref[0].reshape(dp * rows, width)
    for t in range(0, tokens, tile):
        hidden = jnp.maximum(dot(x_ref[t : t + tile, :], up), 0.0)
        act = (hidden * hidden).astype(BF)
        act_ref[0, t : t + tile, :] = act
        for y in range(seq):
            part = dot(act, content_ref[y].reshape(group * grain, columns))
            where = (slice(t, t + tile), slice(y * columns, (y + 1) * columns))
            total_ref[where] = part if first else total_ref[where] + part


def channel_one(s, before, marks, gain, bias, mix, lookup, content, cut, length):
    tokens, width = s.shape
    tile = tile_rows(length)
    tiles, per_run = tokens // tile, length // tile

    def body(
        s_ref, before_ref, marks_ref, gain_ref, bias_ref, mix_ref, lookup_ref, content_ref,
        xk_ref, xr_ref, lead_ref, act_ref, total_ref,
    ):
        @pl.when(pl.program_id(0) == 0)
        def _():
            last = None
            for i in range(tiles):
                rows = slice(i * tile, (i + 1) * tile)
                unit, _ = centred_norm(s_ref[rows, :])
                normed = unit * gain_ref[...] + bias_ref[...]
                if i % per_run == 0:
                    last = before_ref[i // per_run : i // per_run + 1, :]
                lead_ref[i] = last
                shifted = down_one(normed, last) * col(marks_ref[rows, :], ALIVE)
                last = normed[tile - 1 :, :]
                change = normed - shifted
                xk_ref[rows, :] = (shifted + mix_ref[0:1, :] * change).astype(BF)
                xr_ref[rows, :] = (shifted + mix_ref[1:2, :] * change).astype(BF)
            hidden_step(xk_ref, lookup_ref, content_ref, act_ref, total_ref, True)

        @pl.when(pl.program_id(0) > 0)
        def _():
            hidden_step(xk_ref, lookup_ref, content_ref, act_ref, total_ref, False)

    half, full = jax.ShapeDtypeStruct((tokens, width), BF), jax.ShapeDtypeStruct((tokens, width), F32)
    return pl.pallas_call(
        body,
        grid=(cut.steps,),
        in_specs=[
            held(s.shape), fixed(before.shape), held(marks.shape),
            fixed(gain.shape), fixed(bias.shape), fixed(mix.shape),
        ] + cut.specs(lookup, content, lambda i: i),
        out_specs=[
            fixed((tokens, width)), fixed((tokens, width)), fixed((tiles, 1, width)),
            pl.BlockSpec((1, tokens, cut.width), lambda i: (i, 0, 0)), fixed((tokens, width)),
        ],
        out_shape=[
            half, half, jax.ShapeDtypeStruct((tiles, 1, width), F32),
            jax.ShapeDtypeStruct((cut.steps, tokens, cut.width), BF), full,
        ],
        compiler_params=params(),
        cost_estimate=cost(
            4 * tokens * width * cut.width * cut.steps,
            14 * tokens * width + cut.steps * cut.width * (4 * width + 2 * tokens),
        ),
    )(s, before, marks, gain, bias, mix, lookup[0], content[0])


def channel_two(s, xk, xr, total, lookup, content, accept, cut, kind):
    tokens, width = s.shape
    tile = min(256, tokens)

    def body(
        s_ref, xk_ref, xr_ref, total_ref, accept_ref, lookup_ref, content_ref,
        act_ref, carried_ref, gate_ref, out_ref, sum_ref, take_ref,
    ):
        @pl.when(pl.program_id(0) == 0)
        def _():
            sum_ref[...] = total_ref[...]

        hidden_step(xk_ref, lookup_ref, content_ref, act_ref, sum_ref, False)

        @pl.when(pl.program_id(0) == cut.steps - 1)
        def _():
            for t in range(0, tokens, tile):
                rows = slice(t, t + tile)
                times(xr_ref[rows, :], accept_ref, 0, accept_ref.shape[2], take_ref)
                gate = jax.nn.sigmoid(take_ref[...])
                carried = sum_ref[rows, :]
                gate_ref[rows, :] = gate.astype(BF)
                carried_ref[rows, :] = carried.astype(BF)
                out_ref[rows, :] = (s_ref[rows, :] + gate * carried).astype(kind)

    half = jax.ShapeDtypeStruct((tokens, width), BF)
    return pl.pallas_call(
        body,
        grid=(cut.steps,),
        in_specs=[held(s.shape), held(xk.shape), held(xr.shape), held(total.shape), held(accept.shape)]
        + cut.specs(lookup, content, lambda i: i),
        out_specs=[pl.BlockSpec((1, tokens, cut.width), lambda i: (i, 0, 0))] + [fixed((tokens, width))] * 3,
        out_shape=[
            jax.ShapeDtypeStruct((cut.steps, tokens, cut.width), BF), half, half,
            jax.ShapeDtypeStruct((tokens, width), kind),
        ],
        scratch_shapes=[pltpu.VMEM((tokens, width), F32), pltpu.VMEM((tile, width), F32)],
        compiler_params=params(),
        cost_estimate=cost(
            4 * tokens * width * cut.width * cut.steps + 2 * tokens * width * width,
            20 * tokens * width + cut.steps * cut.width * (4 * width + 2 * tokens) + 2 * accept.size,
        ),
    )(s, xk, xr, total, accept, lookup[0], content[0])


def mixed_back(grads, s, lead, alive, gain, bias, mix_ref, after):
    unit, rate = centred_norm(s)
    normed = unit * gain + bias
    change = normed - down_one(normed, lead) * alive
    own, before, mixes = None, None, []
    for j, grad in enumerate(grads):
        mix = mix_ref[j : j + 1, :]
        a, b = mix * grad, (1.0 - mix) * grad
        own, before = (a, b) if own is None else (own + a, before + b)
        mixes.append(summed_rows(change * grad))
    before = before * alive
    grad = own + up_one(before, after)
    small = [summed_rows(grad * unit), summed_rows(grad)] + mixes
    return norm_back(grad, unit, rate, gain), before[0:1, :], small


def channel_back(
    core, g, fix, s, lead, marks, gain, bias, mix, gate, carried, xk, xr, acts, lookups, contents, accept,
    cut, length, packing, table,
):
    tokens, width = s.shape
    tile = tile_rows(length)
    tiles, per_run = tokens // tile, length // tile
    steps = cut.steps
    shapes, spots = packing
    seq, dp = accept.shape[:2]
    columns = width // seq
    half_rows = accept.shape[2] // 2
    last = 2 * steps - 1
    slots = len(shapes)
    split = slots == 2
    units = dp // 2

    def body(
        core_ref, g_ref, fix_ref, s_ref, lead_ref, marks_ref, gain_ref, bias_ref, mix_ref,
        gate_ref, carried_ref, xk_ref, xr_ref, act0_ref, act1_ref, accept_ref,
        lookup0_ref, content0_ref, lookup1_ref, content1_ref, table_ref, *rest,
    ):
        outs, rest = rest[:slots], rest[slots:]
        out_ref, edge_ref, small_ref, gc_ref, gr_ref, sum_ref, key_ref, val_ref, take_ref, sem, stage_ref = rest
        if not split:
            lookup_out, content_out, accept_out = outs
        step = pl.program_id(0)
        slot = lax.rem(step, 2)

        def waits(which):
            if split:
                rows = pl.ds(0, cut.rows)
                key = outs[1].at[0, :, :, rows, :]
                val = outs[1].at[0, pl.ds(0, seq * cut.group // 2), :, pl.ds(0, cut.grain), :]
                val_from = val_ref.at[which].reshape(seq * cut.group // 2, 2, cut.grain, columns)
            else:
                key = lookup_out.at[0, 0, :, :, pl.ds(0, cut.rows), :]
                val = content_out.at[0, :, pl.ds(0, cut.group // 2), :, :, :]
                val_from = val_ref.at[which]
            pltpu.make_async_copy(key_ref.at[which], key, sem.at[which, 0]).wait()
            pltpu.make_async_copy(val_from, val, sem.at[which, 1]).wait()

        def send(source, unit, store, rows, sem):
            half = table_ref[SPOTS + 2 * store, unit]
            index = table_ref[SPOTS + 1 + 2 * store, unit]
            for side in range(2):

                @pl.when(half == 1 - side)
                def _(side=side):
                    pltpu.make_async_copy(source, outs[side].at[store, index, :, rows, :], sem).start()

        def start(which, store, q):
            y, block = lax.div(q, cut.blocks), lax.rem(q, cut.blocks)
            if split:
                rows = pl.ds(pl.multiple_of(spots[0] + block * cut.rows, 16), cut.rows)
                for unit in range(units):
                    send(key_ref.at[which, unit], y * units + unit, store, rows, sem.at[which, 0])
                for y in range(seq):
                    for part in range(cut.group // 2):
                        unit = y * units + q * (cut.group // 2) + part
                        rows = pl.ds(spots[1], cut.grain)
                        send(val_ref.at[which, y, part], unit, store, rows, sem.at[which, 1])
            else:
                rows = pl.ds(pl.multiple_of(block * cut.rows, 16), cut.rows)
                key = lookup_out.at[store, y, :, :, rows, :]
                pltpu.make_async_copy(key_ref.at[which], key, sem.at[which, 0]).start()
                val = content_out.at[store, :, pl.ds(q * (cut.group // 2), cut.group // 2), :, :, :]
                pltpu.make_async_copy(val_ref.at[which], val, sem.at[which, 1]).start()

        def store_of_step(i):
            core = core_ref[0]
            return jnp.where(i < steps, core, 1 - core), lax.rem(i, steps)

        @pl.when(step == 0)
        def _():
            for i in range(tiles):
                rows = slice(i * tile, (i + 1) * tile)
                grad = g_ref[rows, :].astype(F32)
                if (i + 1) % per_run == 0:
                    at = lax.broadcasted_iota(jnp.int32, grad.shape, 0)
                    run = i // per_run
                    grad = jnp.where(at == tile - 1, grad + fix_ref[run : run + 1, :], grad)
                gate = gate_ref[rows, :].astype(F32)
                passed = grad * gate
                out_ref[rows, :] = grad
                gc_ref[rows, :] = passed.astype(BF)
                gr_ref[rows, :] = (passed * carried_ref[rows, :].astype(F32) * (1.0 - gate)).astype(BF)

        @pl.when(step >= 2)
        def _():
            waits(slot)

        def work(act_ref, lookup_ref, content_ref, first):
            up = lookup_ref[0].reshape(dp * cut.rows, cut.width)
            size = min(256, tokens)
            for t in range(0, tokens, size):
                rows = slice(t, t + size)
                act = act_ref[0, rows, :].astype(F32)
                grad = None
                for y in range(seq):
                    part = dot_nt(
                        gc_ref[rows, y * columns : (y + 1) * columns],
                        content_ref[y].reshape(cut.group * cut.grain, columns),
                    )
                    grad = part if grad is None else grad + part
                grad = (grad * (2.0 * jnp.sqrt(act))).astype(BF)
                take_ref[rows, :] = grad
                part = dot_nt(grad, up)
                sum_ref[rows, :] = part if first else sum_ref[rows, :] + part
            key = dot_tn(xk_ref[...], take_ref[...])
            key_ref[slot] = key.astype(BF).reshape(units, 2, cut.rows, cut.width)
            for y in range(seq):
                val = dot_tn(act_ref[0], gc_ref[:, y * columns : (y + 1) * columns])
                val_ref[slot, y] = val.astype(BF).reshape(cut.group // 2, 2, cut.grain, columns)

        @pl.when(step == 0)
        def _():
            work(act0_ref, lookup0_ref, content0_ref, True)

        @pl.when(jnp.logical_and(step > 0, step < steps))
        def _():
            work(act0_ref, lookup0_ref, content0_ref, False)

        @pl.when(step >= steps)
        def _():
            work(act1_ref, lookup1_ref, content1_ref, False)

        start(slot, *store_of_step(step))

        @pl.when(step == last)
        def _():
            waits(1 - slot)
            waits(slot)
            rows = pl.ds(spots[2], half_rows)
            for y in range(seq):
                grad = dot_tn(xr_ref[...], gr_ref[:, y * columns : (y + 1) * columns])
                grad = grad.astype(BF).reshape(dp, 2 * half_rows, columns)
                for h in range(2):
                    part = grad[:, h * half_rows : (h + 1) * half_rows, :]
                    stage_ref[h, y] = part.reshape(units, 2, half_rows, columns)
                    if split:
                        for unit in range(units):
                            send(stage_ref.at[h, y, unit], y * units + unit, h, rows, sem.at[h, 2 + y])
                    else:
                        take = accept_out.at[h, y]
                        pltpu.make_async_copy(stage_ref.at[h, y], take, sem.at[h, 2 + y]).start()
            after = None
            small = None
            for i in reversed(range(tiles)):
                at = slice(i * tile, (i + 1) * tile)
                if (i + 1) % per_run == 0:
                    after = jnp.zeros((1, width), F32)
                grads = [sum_ref[at, :], times_back(gr_ref[at, :], accept_ref, 0, 2 * half_rows)]
                add, after, more = mixed_back(
                    grads, s_ref[at, :], lead_ref[i], col(marks_ref[at, :], ALIVE),
                    gain_ref[...], bias_ref[...], mix_ref, after,
                )
                out_ref[at, :] += add
                small = more if small is None else [a + b for a, b in zip(small, more)]
                if i % per_run == 0:
                    edge_ref[i // per_run : i // per_run + 1, :] = after
            for j, line in enumerate(small):
                small_ref[j : j + 1, :] = line
            for h in range(2):
                for y in range(seq):
                    if split:
                        take = outs[1].at[0, :, :, rows, :]
                    else:
                        take = accept_out.at[h, y]
                    pltpu.make_async_copy(stage_ref.at[h, y], take, sem.at[h, 2 + y]).wait()

    own = lambda i: jnp.minimum(i, steps - 1)
    partner = lambda i: jnp.maximum(i - steps, 0)
    act = lambda step: pl.BlockSpec((1, tokens, cut.width), lambda i: (step(i), 0, 0))
    any_space = pl.BlockSpec(memory_space=pl.ANY)
    return pl.pallas_call(
        body,
        grid=(2 * steps,),
        in_specs=[
            SCALAR, held(g.shape), fixed(fix.shape), held(s.shape), fixed(lead.shape), held(marks.shape),
            fixed(gain.shape), fixed(bias.shape), fixed(mix.shape), held(gate.shape), held(carried.shape),
            held(xk.shape), held(xr.shape), act(own), act(partner), held(accept.shape),
        ] + cut.specs(lookups[0], contents[0], own) + cut.specs(lookups[1], contents[1], partner) + [SCALAR],
        out_specs=[any_space] * slots + [fixed((tokens, width)), fixed(fix.shape), fixed((4, width))],
        out_shape=[jax.ShapeDtypeStruct(shape, BF) for shape in shapes] + [
            jax.ShapeDtypeStruct((tokens, width), F32), jax.ShapeDtypeStruct(fix.shape, F32),
            jax.ShapeDtypeStruct((4, width), F32),
        ],
        scratch_shapes=[
            pltpu.VMEM((tokens, width), BF), pltpu.VMEM((tokens, width), BF),
            pltpu.VMEM((tokens, width), F32),
            pltpu.VMEM((2, units, 2, cut.rows, cut.width), BF),
            pltpu.VMEM((2, seq, cut.group // 2, 2, cut.grain, columns), BF),
            pltpu.VMEM((tokens, cut.width), BF),
            pltpu.SemaphoreType.DMA((2, 2 + seq)),
            pltpu.VMEM((2, seq, units, 2, half_rows, columns), BF),
        ],
        compiler_params=params(),
        cost_estimate=cost(
            16 * tokens * width * cut.width * steps + 4 * tokens * width * width,
            30 * tokens * width + 2 * steps * cut.width * (8 * width + 2 * tokens),
        ),
    )(
        core, g, fix, s, lead, marks, gain, bias, mix, gate, carried, xk, xr, *acts, accept,
        lookups[0][0], contents[0][0], lookups[1][0], contents[1][0], table,
    )


def out_back(core, g, fix, k, v, r, sa, sb, marks, rate, bonus, mine, other, length):
    tokens, width = g.shape
    tile = tile_rows(length)
    per_run = length // tile
    runs = tokens // length

    def body(
        core_ref, g_ref, fix_ref, k_ref, v_ref, r_ref, sa_ref, sb_ref, marks_ref, rate_ref, bonus_ref,
        mine_ref, other_ref, go_ref, gr_ref, gn_ref, gd_ref, chain_ref, gz_ref,
    ):
        step = pl.program_id(0)
        run, part = lax.div(step, per_run), lax.rem(step, per_run)
        grad = g_ref[...]
        at = lax.broadcasted_iota(jnp.int32, grad.shape, 0)
        hit = jnp.logical_and(at == tile - 1, part == per_run - 1)
        go_ref[...] = jnp.where(hit, grad + fix_ref[pl.ds(run, 1), :], grad).astype(BF)

        def project(first, second):
            rows = first.shape[2] // 2
            gz_ref[...] = times_back(go_ref[...], second, rows, 2 * rows)

        by_core(core_ref, mine_ref, other_ref, project)
        gate = jax.nn.sigmoid(r_ref[...])
        scaled = jnp.exp(k_ref[...]) * bonus_ref[...]
        inverse = 1.0 / (sb_ref[...] + scaled)
        answer = (sa_ref[...] + scaled * v_ref[...]) * inverse
        gated = gz_ref[...] * gate
        gr_ref[...] = (gated * answer * (1.0 - gate)).astype(BF)
        gn = gated * inverse
        gd = -gn * answer
        gn_ref[...] = gn
        gd_ref[...] = gd

        @pl.when(part == 0)
        def _():
            chain_ref[pl.ds(run, 1)] = jnp.zeros((1, 2, width), F32)

        places = (lax.broadcasted_iota(jnp.int32, (tile, 1), 0) + part * tile).astype(F32)
        weight = jnp.exp(-places * rate_ref[...]) * col(marks_ref[...], HEAD)
        sums = jnp.concatenate([summed_rows(weight * gn), summed_rows(weight * gd)], axis=0)
        chain_ref[pl.ds(run, 1)] += sums[None]

    block = pl.BlockSpec((tile, width), lambda i: (i, 0))
    half, full = jax.ShapeDtypeStruct((tokens, width), BF), jax.ShapeDtypeStruct((tokens, width), F32)
    return pl.pallas_call(
        body,
        grid=(tokens // tile,),
        in_specs=[
            SCALAR, block, fixed(fix.shape), block, block, block, block, block,
            pl.BlockSpec((tile, 8), lambda i: (i, 0)), fixed(rate.shape), fixed(bonus.shape),
            held(mine.shape), held(other.shape),
        ],
        out_specs=[block] * 4 + [fixed((runs, 2, width))],
        out_shape=[half, half, full, full, jax.ShapeDtypeStruct((runs, 2, width), F32)],
        scratch_shapes=[pltpu.VMEM((tile, width), F32)],
        compiler_params=params(),
        cost_estimate=cost(2 * tokens * width * width, 36 * tokens * width + 4 * mine.size),
    )(core, g, fix, k, v, r, sa, sb, marks, rate, bonus, mine, other)


def time_back(
    core, g, fix, s, lead, k, v, sa, sb, gn, gd, gr, leave, marks, lines, gain, bias, mix, rate, bonus,
    mine, other, length,
):
    tokens, width = s.shape
    tile = tile_rows(length)
    tiles, per_run = tokens // tile, length // tile
    runs = tokens // length

    def body(
        core_ref, g_ref, fix_ref, s_ref, lead_ref, k_ref, v_ref, sa_ref, sb_ref, gn_ref, gd_ref, gr_ref,
        leave_ref, marks_ref, line_ref, gain_ref, bias_ref, mix_ref, rate_ref, bonus_ref,
        mine_ref, other_ref, gk_ref, gv_ref, out_ref, edge_ref, small_ref,
        state_ref, after_ref, xk_ref, xv_ref, xr_ref,
    ):
        step = pl.program_id(0)
        i = tiles - 1 - step
        run, part = lax.div(i, per_run), lax.rem(i, per_run)

        @pl.when(part == per_run - 1)
        def _():
            state_ref[...] = leave_ref[pl.ds(run, 1)][0]
            after_ref[...] = jnp.zeros((1, width), F32)

        marks = marks_ref[...]
        alive = col(marks, ALIVE)
        places = lax.broadcasted_iota(jnp.int32, (tile, 1), 0).astype(F32)
        spread = places * rate_ref[...]
        falling, decay = jnp.exp(-spread), jnp.exp(-rate_ref[...])
        rising = jnp.exp(spread + rate_ref[...])
        at = lax.broadcasted_iota(jnp.int32, (tile, tile), 0)
        source = lax.broadcasted_iota(jnp.int32, (tile, tile), 1)
        same = col(marks, 7) == line_ref[0]
        mask = jnp.where(jnp.logical_and(same, source > at), 1.0, 0.0).astype(BF)
        gn, gd = gn_ref[...], gd_ref[...]
        carried = jnp.exp(spread - (tile - 1) * rate_ref[...]) * col(marks, LEAVES)
        ga = rising * split_sum(mask, falling * gn) + carried * state_ref[0:1, :]
        gb = rising * split_sum(mask, falling * gd) + carried * state_ref[1:2, :]
        first = alive[0:1, :]
        state_ref[0:1, :] = first * (gn[0:1, :] + decay * ga[0:1, :])
        state_ref[1:2, :] = first * (gd[0:1, :] + decay * gb[0:1, :])
        powered, content = jnp.exp(k_ref[...]), v_ref[...]
        scaled = powered * bonus_ref[...]
        reward = (gn * content + gd) * scaled
        gv_ref[...] = (gn * scaled + powered * ga).astype(BF)
        gk_ref[...] = (reward + powered * (content * ga + gb)).astype(BF)
        sums = [summed_rows(ga * sa_ref[...] + gb * sb_ref[...]), summed_rows(reward)]

        def project(first, second):
            rows = first.shape[2] // 2
            xk_ref[...] = times_back(gk_ref[...], first, 0, rows)
            xv_ref[...] = times_back(gv_ref[...], first, rows, 2 * rows)
            xr_ref[...] = times_back(gr_ref[...], second, 0, rows)

        by_core(core_ref, mine_ref, other_ref, project)
        grads = [xk_ref[...], xv_ref[...], xr_ref[...]]
        add, after, small = mixed_back(
            grads, s_ref[...].astype(F32), lead_ref[0], alive, gain_ref[...], bias_ref[...], mix_ref,
            after_ref[...],
        )
        after_ref[...] = after
        grad = g_ref[...]
        row = lax.broadcasted_iota(jnp.int32, grad.shape, 0)
        hit = jnp.logical_and(row == tile - 1, part == per_run - 1)
        out_ref[...] = jnp.where(hit, grad + fix_ref[pl.ds(run, 1), :], grad) + add
        edge_ref[pl.ds(run, 1), :] = after

        @pl.when(step == 0)
        def _():
            small_ref[...] = jnp.zeros_like(small_ref)

        for j, line in enumerate(small + sums):
            small_ref[j : j + 1, :] += line

    back = lambda i: tiles - 1 - i
    block = pl.BlockSpec((tile, width), lambda i: (back(i), 0))
    half, full = jax.ShapeDtypeStruct((tokens, width), BF), jax.ShapeDtypeStruct((tokens, width), F32)
    return pl.pallas_call(
        body,
        grid=(tiles,),
        in_specs=[
            SCALAR, block, fixed(fix.shape), block, pl.BlockSpec((1, 1, width), lambda i: (back(i), 0, 0)),
            block, block, block, block, block, block, block, fixed(leave.shape),
            pl.BlockSpec((tile, 8), lambda i: (back(i), 0)),
            pl.BlockSpec((1, 1, tile), lambda i: (back(i), 0, 0)),
            fixed(gain.shape), fixed(bias.shape), fixed(mix.shape), fixed(rate.shape), fixed(bonus.shape),
            held(mine.shape), held(other.shape),
        ],
        out_specs=[block, block, block, fixed(fix.shape), fixed((7, width))],
        out_shape=[
            half, half, full, jax.ShapeDtypeStruct(fix.shape, F32), jax.ShapeDtypeStruct((7, width), F32),
        ],
        scratch_shapes=[
            pltpu.VMEM((2, width), F32), pltpu.VMEM((1, width), F32),
            pltpu.VMEM((tile, width), F32), pltpu.VMEM((tile, width), F32), pltpu.VMEM((tile, width), F32),
        ],
        compiler_params=params(),
        cost_estimate=cost(8 * tokens * width * width, 46 * tokens * width + 4 * mine.size),
    )(
        core, g, fix, s, lead, k, v, sa, sb, gn, gd, gr, leave, marks, lines, gain, bias, mix, rate, bonus,
        mine, other,
    )


def weight_grads(first, second, grads, table):
    dp, seq = sizes()
    tokens, width = grads[0].shape
    rows, columns = width // dp, width // seq
    pairs = list(zip(first + second, grads))
    split, units = paired(), dp // 2
    if split:
        shapes = [(2, units * seq // 2, 2, 2 * rows, columns)] * 2
    else:
        shapes = [(2, seq, units, 2, 2 * rows, columns)]

    def body(table_ref, *refs):
        ins, rest = refs[: 2 * len(pairs)], refs[2 * len(pairs) :]
        outs, (x_ref, g_ref, stage_ref, sem, out_sem) = rest[: len(shapes)], rest[len(shapes) :]
        which, y = pl.program_id(0), pl.program_id(1)
        slot = lax.rem(which, 2)
        step = which * seq + y
        place = lax.rem(step, 2)

        def copies(i):
            return (
                pltpu.make_async_copy(ins[2 * i], x_ref.at[i % 2], sem.at[i % 2, 0]),
                pltpu.make_async_copy(ins[2 * i + 1], g_ref.at[i % 2], sem.at[i % 2, 1]),
            )

        def wait(at):
            target = outs[0].at[0, :, :, pl.ds(0, rows), :] if split else outs[0].at[0, 0, :, :, pl.ds(0, rows), :]
            pltpu.make_async_copy(stage_ref.at[at], target, out_sem.at[at]).wait()

        @pl.when(step == 0)
        def _():
            for copy in copies(0):
                copy.start()

        for i in range(len(pairs)):

            @pl.when(jnp.logical_and(which == i, y == 0))
            def _(i=i):
                for copy in copies(i):
                    copy.wait()
                if i + 1 < len(pairs):
                    for copy in copies(i + 1):
                        copy.start()

        @pl.when(step >= 2)
        def _():
            wait(place)

        at = pl.ds(pl.multiple_of(y * columns, columns), columns)
        grad = dot_tn(x_ref[slot], g_ref[slot, :, at])
        stage_ref[place] = grad.astype(BF).reshape(units, 2, rows, columns)
        store = lax.div(which, 2)
        span = pl.ds(pl.multiple_of(lax.rem(which, 2) * rows, 16), rows)
        if split:
            for unit in range(units):
                half = table_ref[SPOTS + 2 * store, y * units + unit]
                index = table_ref[SPOTS + 1 + 2 * store, y * units + unit]
                for side in range(2):

                    @pl.when(half == 1 - side)
                    def _(side=side, unit=unit, index=index):
                        pltpu.make_async_copy(
                            stage_ref.at[place, unit], outs[side].at[store, index, :, span, :], out_sem.at[place]
                        ).start()
        else:
            target = outs[0].at[store, y, :, :, span, :]
            pltpu.make_async_copy(stage_ref.at[place], target, out_sem.at[place]).start()

        @pl.when(step == len(pairs) * seq - 1)
        def _():
            wait(1 - place)
            wait(place)

    any_space = pl.BlockSpec(memory_space=pl.ANY)
    return pl.pallas_call(
        body,
        grid=(len(pairs), seq),
        in_specs=[SCALAR] + [any_space] * (2 * len(pairs)),
        out_specs=[any_space] * len(shapes),
        out_shape=[jax.ShapeDtypeStruct(shape, BF) for shape in shapes],
        scratch_shapes=[
            pltpu.VMEM((2, tokens, width), BF), pltpu.VMEM((2, tokens, width), BF),
            pltpu.VMEM((2, units, 2, rows, columns), BF),
            pltpu.SemaphoreType.DMA((2, 2)), pltpu.SemaphoreType.DMA((2,)),
        ],
        compiler_params=params(),
        cost_estimate=cost(8 * tokens * width * width, 16 * tokens * width + 8 * width * width),
    )(table, *[array for pair in pairs for array in pair])


def passed_along(array, axis, by):
    devices = lax.axis_size(axis)
    pairs = [(i, i + by) for i in range(devices) if 0 <= i + by < devices]
    return lax.ppermute(array, axis, pairs)


def entering(chain, ends, by):
    came = passed_along(ends, "seq", by)
    for _ in range(lax.axis_size("seq") - 2):
        came = passed_along(ends + chain * came, "seq", by)
    return came


def last_tokens(s, length):
    return s.reshape(-1, length, s.shape[-1])[:, -1].astype(F32)


def edge_norm(s, length, gain, bias):
    unit, _ = centred_norm(last_tokens(s, length))
    return passed_along(unit * gain + bias, "seq", 1)


def edge_back(edge, s, length, gain):
    came = passed_along(edge, "seq", -1)
    unit, rate = centred_norm(last_tokens(s, length))
    small = jnp.concatenate([summed_rows(came * unit), summed_rows(came)])
    return norm_back(came, unit, rate, gain), small


def cut_lookup(shard, grain):
    rows, columns = shard.shape
    width = min(512, columns // 2)
    cut = shard.reshape(rows, columns // (2 * grain), 2, grain).transpose(2, 0, 1, 3)
    cut = cut.reshape(2, rows, columns // 2 // width, width).transpose(0, 2, 1, 3)
    return cut.reshape(2, -1, width)


def join_lookup(first, second, rows, grain):
    width = first.shape[-1]
    cut = jnp.stack([first, second]).reshape(2, -1, rows, width).transpose(0, 2, 1, 3)
    cut = cut.reshape(2, rows, -1, grain).transpose(1, 2, 0, 3)
    return cut.reshape(rows, -1)


def spots_of(shards):
    return [0] + np.cumsum([shard.shape[0] for shard in shards]).tolist()


def cut_at(array, spots):
    return [array[a:b] for a, b in zip(spots, spots[1:])]


def gather_plain(first, second):
    dp, seq = sizes()
    whole = lambda a: (lax.all_gather(a, ("seq", "dp")).reshape((seq, dp) + a.shape), 0)
    return [whole(a) for a in first], [whole(a) for a in second]


def scatter_plain(stores):
    dp, seq = sizes()
    take = lambda a: lax.psum_scatter(
        a.reshape((seq * dp,) + a.shape[-2:]), ("seq", "dp"), scatter_dimension=0
    ).astype(F32)
    return [take(s[0]) for s in stores], [take(s[1]) for s in stores]


def by_half(first_is_low, low, high):
    return jnp.where(first_is_low, low, high), jnp.where(first_is_low, high, low)


def partner_y(array):
    return lax.ppermute(array, "seq", [(0, 1), (1, 0)])


def rows_cut(array):
    half = array.shape[0] // 2
    return by_half(lax.axis_index("seq") == 0, array[:half], array[half:])


def rows_joined(kept, came):
    low = lax.axis_index("seq") == 0
    return jnp.concatenate(by_half(low, kept, came), axis=1)


def runs_cut(array):
    length = array.shape[1] // 2
    return by_half(lax.axis_index("seq") == 0, array[:, :length], array[:, length:])


def runs_joined(kept, came):
    low = lax.axis_index("seq") == 0
    return jnp.concatenate(by_half(low, kept, came), axis=0)


def per_device(
    entering_activations,
    document_numbers,
    result_cotangent,
    normalizer_scales,
    normalizer_offsets,
    shift_blend_factors,
    fading_natural_logs_per_feature,
    feature_reward_logs,
    attention_triple_matrix,
    attention_result_matrix,
    channelmix_lookup_matrix,
    channelmix_content_matrix,
    channelmix_accept_matrix,
):
    dp, seq = sizes()
    staged = paired()
    core = core_of()
    cores = core.reshape(1)
    table = unit_tables() if staged else jnp.zeros((1, 1), jnp.int32)
    layers = attention_triple_matrix.shape[0]
    runs, length, width = entering_activations.shape
    tokens, columns = runs * length, width // seq
    swapped = staged and layers == 2 and runs % 2 == 0
    if swapped:
        kept_rows, sent_rows = rows_cut(document_numbers)
        document_numbers = rows_joined(kept_rows, partner_y(sent_rows))
        kept_rows, sent_rows = rows_cut(entering_activations)
        entering_activations = rows_joined(kept_rows, partner_y(sent_rows))
        runs, length = runs // 2, length * 2

    lookup_rows = channelmix_lookup_matrix.shape[1]
    grain = channelmix_content_matrix.shape[1] // 2
    half_rows = channelmix_accept_matrix.shape[1] // 2

    shards = []
    for depth in range(layers):
        triple, result = attention_triple_matrix[depth], attention_result_matrix[depth]
        lookup = cut_lookup(channelmix_lookup_matrix[depth], grain)
        content, accept = channelmix_content_matrix[depth], channelmix_accept_matrix[depth]
        shards.append(([jnp.concatenate([triple[0], triple[1]])], [jnp.concatenate([triple[2], result])]))
        shards.append(
            (
                [lookup[0], content[:grain], accept[:half_rows]],
                [lookup[1], content[grain:], accept[half_rows:]],
            )
        )

    held = {}
    if staged:
        first = jnp.concatenate([shard for group in shards for shard in group[0]])
        second = jnp.concatenate([shard for group in shards for shard in group[1]])
        kept = jnp.where(core == 0, first, second)
        came = moved(jnp.where(core == 0, second, first), to_core)
        pair = jnp.where(core == 0, jnp.stack([kept, came]), jnp.stack([came, kept]))
        ends = spots_of([jnp.concatenate(group[0]) for group in shards])
        moves = [Gathering(table, pair[:, a:b]) for a, b in zip(ends, ends[1:])]
    else:
        moves = [gather_plain(*group) for group in shards]

    def give_att(depth, mine, other):
        held["att", depth] = (mine, other)

    def give_chan(depth, mine, other):
        takes = [array[:, :, at : at + half_rows] for array, at in (mine[2], other[2])]
        first = jnp.where(core == 0, takes[0], takes[1])
        second = jnp.where(core == 0, takes[1], takes[0])
        held["cut", depth] = Cut(mine[0], mine[1], lookup_rows, grain)
        held["chan", depth] = (mine, other, jnp.concatenate([first, second], axis=2))

    def with_rows(array, group):
        return [(array, at) for at in spots_of(shards[group][0])[:-1]]

    if swapped:
        border = jnp.full((runs, 1), -1, document_numbers.dtype)
    else:
        border = passed_along(document_numbers[:, -1:] + 1, "seq", 1) - 1
    earlier = jnp.concatenate([border, document_numbers[:, :-1]], axis=1)
    edges = jnp.zeros((runs, width), F32)
    states = jnp.zeros((runs, 2, width), F32)
    marks, lines = token_marks(document_numbers, earlier)
    through = (earlier[:, :1] == document_numbers[:, -1:]).astype(F32)[:, :, None]
    begins = (earlier[:, :1] == document_numbers[:, :1]).astype(F32)[:, :, None]
    rates = jnp.exp(fading_natural_logs_per_feature)
    bonuses = jnp.exp(feature_reward_logs)

    def layer_values(depth):
        gain, bias, mix = normalizer_scales[depth], normalizer_offsets[depth], shift_blend_factors[depth]
        rate, bonus = rates[depth : depth + 1], bonuses[depth : depth + 1]
        return gain, bias, mix, rate, bonus, jnp.exp(-length * rate)[None] * through

    kept = {}

    def run_time_in(depth, flow):
        gain, bias, mix, rate, _, _ = layer_values(depth)
        before = edges if swapped else edge_norm(flow, length, gain[0], bias[0])
        kept["time", depth] = (flow,) + tuple(
            time_in(
                cores, flow, before, marks, gain[0:1], bias[0:1], mix[:3], rate, *held["att", depth], length
            )
        )
        return kept["time", depth][4]

    def run_time_out(depth, *after):
        _, _, _, rate, bonus, chain = layer_values(depth)
        flow, xk, xv, xr, k, v, r, ends, lead = kept["time", depth]
        enter = states if swapped else entering(chain, ends, 1)
        k = tie(k, *after) if after else k
        z, sa, sb, middle = time_out(
            cores, flow, k, v, r, enter, marks, lines, rate, bonus, *held["att", depth], length
        )
        kept["time", depth] = (flow, lead, xk, xv, xr, k, v, r, z, sa, sb)
        gain, bias, _, _, _, _ = layer_values(depth)
        before = edges if swapped else edge_norm(middle, length, gain[1], bias[1])
        kept["middle", depth] = (middle, before)
        return middle

    def run_channel_one(depth, mine, cut, *after):
        gain, bias, mix, _, _, _ = layer_values(depth)
        middle, before = kept["middle", depth]
        before = tie(before, *after) if after else before
        kept["one", depth] = channel_one(
            middle, before, marks, gain[1:2], bias[1:2], mix[3:], mine[0], mine[1], cut, length
        )
        return kept["one", depth][4]

    def run_channel_two(depth, *after):
        middle, _ = kept["middle", depth]
        xk, xr, lead, act0, total = kept["one", depth]
        _, other, accept = held["chan", depth]
        total = tie(total, *after) if after else total
        kind = BF if depth == layers - 1 else F32
        act1, carried, gate, flow = channel_two(
            middle, xk, xr, total, other[0], other[1], accept, held["cut", depth], kind
        )
        kept["chan", depth] = (middle, lead, xk, xr, (act0, act1), carried, gate)
        return flow

    flow = entering_activations.reshape(tokens, width)
    if staged and layers == 2:
        att0, chan0, att1, chan1 = moves

        def place_att(depth, move):
            give_att(depth, *move.swap())

        def place_chan(depth, move, group):
            mine, other = move.swap()
            give_chan(depth, with_rows(mine, group), with_rows(other, group))

        att0.z()
        chan0.z(att0.end_z())
        att0.second(flow)
        far = att0.third(chan0.parts[0])
        att0.arrange()
        att0.mine = tie(att0.mine, chan0.parts)
        chan0.end_z(far)
        near = chan0.second()
        place_att(0, att0)
        done = run_time_in(0, flow)
        far = chan0.third(done)
        att1.z(done)
        done = run_time_out(0, near)
        line = att1.end_z(done)
        chan1.z(line)
        near = att1.second(far, done)
        mine = chan0.arrange(done, line, chan1.parts)
        place_chan(0, chan0, 1)
        far = att1.third(mine)
        own, _, _ = held["chan", 0]
        done = run_channel_one(0, own, held["cut", 0], near)
        line = chan1.end_z(done)
        near = chan1.second(far)
        mine = att1.arrange(done, line)
        place_att(1, att1)
        flow = run_channel_two(0, mine)
        far = chan1.third(flow)
        done = run_time_in(1, tie(flow, near))
        done = run_time_out(1)
        chan1.arrange(done)
        place_chan(1, chan1, 3)
        own, _, _ = held["chan", 1]
        run_channel_one(1, own, held["cut", 1])
        y_out = run_channel_two(1)
        if swapped:
            kept_rows, sent_rows = rows_cut(tie(result_cotangent, far))
            result_cotangent = rows_joined(kept_rows, partner_y(sent_rows))
            kept_runs, sent_runs = runs_cut(y_out.reshape(runs, length, width))
            y_out = runs_joined(kept_runs, partner_y(sent_runs))
    else:
        for depth in range(layers):
            if staged:
                for move in moves[2 * depth : 2 * depth + 2]:
                    move.z()
                    move.end_z()
                    move.second()
                    move.third()
                    move.arrange()
                give_att(depth, *moves[2 * depth].swap())
                mine, other = moves[2 * depth + 1].swap()
                group = 2 * depth + 1
                give_chan(depth, with_rows(mine, group), with_rows(other, group))
            else:
                mine, other = moves[2 * depth]
                give_att(depth, mine[0][0], other[0][0])
                give_chan(depth, *moves[2 * depth + 1])
            run_time_in(depth, flow)
            run_time_out(depth)
            run_channel_one(depth, held["chan", depth][0], held["cut", depth])
            flow = run_channel_two(depth)
        y_out = flow

    grad = result_cotangent.reshape(tokens, width)
    fix = jnp.zeros((runs, width), F32)
    small = [None] * layers
    sums = {}
    earlier_chan = earlier_att = None
    for depth in reversed(range(layers)):
        gain, bias, mix, rate, bonus, chain = layer_values(depth)
        flow, lead_t, xk_t, xv_t, xr_t, k, v, r, z, sa, sb = kept["time", depth]
        middle, lead, xk, xr, acts, carried, gate = kept["chan", depth]
        mine, other, accept = held["chan", depth]
        cut = held["cut", depth]
        part_rows = [cut.blocks * lookup_rows, grain, half_rows]
        part_spots = [0, part_rows[0], part_rows[0] + grain, part_rows[0] + grain + half_rows]
        if staged:
            packing = [(2, seq * dp // 4, 2, part_spots[3], columns)] * 2, part_spots
        else:
            widths = [cut.width, columns, columns]
            packing = [(2, seq, dp // 2, 2, n, w) for n, w in zip(part_rows, widths)], [0, 0, 0]
        *stores, grad, edge, small_chan = channel_back(
            cores, grad, fix, middle, lead, marks, gain[1:2], bias[1:2], mix[3:], gate, carried, xk, xr,
            acts, (mine[0], other[0]), (mine[1], other[1]), accept, cut, length, packing, table,
        )
        out_grad = grad
        if staged:
            flat = [s.reshape((2, seq * dp // 4, 2 * part_spots[3], columns)) for s in stores]
            if earlier_att:
                line = earlier_chan.end_second(grad)
                earlier_chan.z()
                away = earlier_att.third(line)
                edge, out_grad = tie((edge, grad), away)
                flat = tie(flat, away)
            elif swapped:
                edge, out_grad = tie((edge, grad), y_out)
                flat = tie(flat, y_out)
            chan_move = Scattering(*flat)
        if swapped:
            fix, edge_chan = edges, jnp.zeros((2, width), F32)
        else:
            fix, edge_chan = edge_back(edge, middle, length, gain[1])
        mine, other = held["att", depth]
        go, gr, gn, gd, ends = out_back(
            cores, out_grad, fix, k, v, r, sa, sb, marks, rate, bonus, mine, other, length
        )
        if staged:
            if earlier_att:
                near = earlier_att.end_third(go)
                earlier_att.second()
                go = tie(go, near, earlier_chan.parts[0])
            away = chan_move.third(go)
            gn = tie(gn, away)
        leave = states if swapped else entering(chain, begins * ends, -1)
        gk, gv, grad, edge, small_time = time_back(
            cores, grad, fix, flow, lead_t, k, v, sa, sb, gn, gd, gr, leave, marks, lines,
            gain[0:1], bias[0:1], mix[:3], rate, bonus, mine, other, length,
        )
        fading = small_time[5:6] * -rate * jnp.exp(-rate)
        small[depth] = jnp.concatenate(
            [
                small_time[0:1],
                small_chan[0:1] + edge_chan[0:1],
                small_time[1:2],
                small_chan[1:2] + edge_chan[1:2],
                small_time[2:5],
                small_chan[2:4],
                fading,
                small_time[6:7],
            ]
        )
        first_hop = None
        if staged and depth == 0:
            first_hop = hop_y(jnp.stack(small))
        if staged and earlier_chan:
            gk, gv = tie((gk, gv), earlier_chan.parts)
        stores_att = weight_grads([xk_t, xv_t], [xr_t, z], [gk, gv, gr, go], table)
        rows = width // dp
        if staged:
            more = []
            if depth == 0:
                sums_xy = hop_x(tie(first_hop, stores_att[0]))
                more.append(sums_xy)
            near = chan_move.end_third(stores_att[0], *more)
            if earlier_att:
                near = tie(near, earlier_att.end_second(near))
                earlier_att.z()
            flat = [s.reshape((2, seq * dp // 4, 4 * rows, columns)) for s in stores_att]
            att_move = Scattering(*tie(flat, near))
            chan_move.second()
            grad = tie(grad, near)
            if depth > 0:
                earlier_chan, earlier_att = chan_move, att_move
            sums["chan", depth], sums["att", depth] = chan_move, att_move
        else:
            sums["chan", depth] = scatter_plain(stores)
            sums["att", depth] = scatter_plain(stores_att)
        if swapped:
            edge_time = jnp.zeros((2, width), F32)
        else:
            fix, edge_time = edge_back(edge, flow, length, gain[0])
            small[depth] = small[depth].at[0].add(edge_time[0]).at[2].add(edge_time[1])
    small = jnp.stack(small)
    grad = grad.reshape(runs, length, width)
    if not swapped:
        grad = grad.at[:, -1].add(fix)
    if staged:
        last_chan, last_att = sums["chan", 0], sums["att", 0]
        sums_xy = sums_xy + moved(sums_xy, to_core)
        away, parts = last_att.away, earlier_att.parts
        line = last_chan.end_second(away)
        last_att.third(line, parts)
        last_chan.z(away, parts)
        last_att.end_third()
        small = summed_z(tie(sums_xy, last_chan.parts[:2]))
        last_att.second(last_chan.parts[:2])
        line = last_att.end_second(small)
        last_att.z()
        came = [last_att.parts]
        if swapped:
            kept_runs, sent_runs = runs_cut(tie(grad, line))
            came.append(partner_y(sent_runs.astype(BF)))
        small, came, *parts = tie((small, came, *[move.parts for move in sums.values()]))
        if swapped:
            grad = runs_joined(kept_runs, came[1].astype(F32))
        for move, part in zip(sums.values(), parts):
            move.parts = part
        totals = [move.total() for move in sums.values()]
        kept_all = [jnp.where(core == 0, total[0], total[1]) for total in totals]
        sent_all = [jnp.where(core == 0, total[1], total[0]) for total in totals]
        came_all = moved(jnp.concatenate(sent_all), to_core)
        spots = spots_of(kept_all)
        for name, mine, theirs in zip(list(sums), kept_all, cut_at(came_all, spots)):
            first, second = jnp.where(core == 0, mine, theirs), jnp.where(core == 0, theirs, mine)
            spots = part_spots if name[0] == "chan" else [0, 2 * rows]
            sums[name] = cut_at(first, spots), cut_at(second, spots)
    else:
        small = lax.psum(small, BOTH)
    large = []
    for depth in range(layers):
        first, second = sums["att", depth]
        triple = jnp.stack([first[0][:rows], first[0][rows:], second[0][:rows]])
        result = second[0][rows:]
        first, second = sums["chan", depth]
        lookup = join_lookup(first[0], second[0], lookup_rows, grain)
        content = jnp.concatenate([first[1], second[1]])
        large.append((triple, result, lookup, content, jnp.concatenate([first[2], second[2]])))
    large = [jnp.stack(members) for members in zip(*large)]
    return (
        y_out if swapped else y_out.reshape(runs, length, width),
        grad,
        small[:, 0:2],
        small[:, 2:4],
        small[:, 4:9],
        small[:, 9],
        small[:, 10],
        *large,
    )


def solution(mesh):
    return jax.shard_map(
        per_device,
        mesh=mesh,
        in_specs=(
            P("dp", "seq", None),
            P("dp", "seq"),
            P("dp", "seq", None),
            P(),
            P(),
            P(),
            P(),
            P(),
            P(None, None, "dp", "seq"),
            P(None, "dp", "seq"),
            P(None, "dp", "seq"),
            P(None, "dp", "seq"),
            P(None, "dp", "seq"),
        ),
        out_specs=(
            P("dp", "seq", None),
            P("dp", "seq", None),
            P(),
            P(),
            P(),
            P(),
            P(),
            P(None, None, "dp", "seq"),
            P(None, "dp", "seq"),
            P(None, "dp", "seq"),
            P(None, "dp", "seq"),
            P(None, "dp", "seq"),
        ),
        check_vma=False,
    )
```

```python
import jax
import jax.numpy as jnp
import numpy as np
from jax import lax
from jax.experimental import pallas as pl
from jax.experimental.pallas import tpu as pltpu
from jax.sharding import PartitionSpec as P

EPS = 1e-05
BF = jnp.bfloat16
F32 = jnp.float32
BOTH = ("dp", "seq")
VMEM = 58 * 2**20


def sizes():
    return lax.axis_size("dp"), lax.axis_size("seq")


def paired():
    dp, seq = sizes()
    return seq == 2 and dp % 4 == 0


def place(d):
    return d // 4, d // 2 % 2, d % 2


def core_of():
    if not paired():
        return jnp.int32(0)
    return lax.rem(lax.axis_index("dp"), 2)


def moved(array, target):
    dp, seq = sizes()
    pairs = []
    for d in range(dp):
        for y in range(seq):
            z, x, c, y2 = target(*place(d), y)
            pairs.append((d * seq + y, (z * 4 + x * 2 + c) * seq + y2))
    return lax.ppermute(array, BOTH, pairs)


def to_core(z, x, c, y):
    return z, x, 1 - c, y


def to_second(z, x, c, y):
    return (z, 1 - x, c, y) if c == 0 else (z, x, c, 1 - y)


def to_third(z, x, c, y):
    return (z, x, c, 1 - y) if c == 0 else (z, 1 - x, c, y)


def along_z(step):
    depth = sizes()[0] // 4

    def target(z, x, c, y):
        return (z + step) % depth, x, c, y

    return target


def unit_spots(z, x, c, y):
    depth = sizes()[0] // 4
    half, index = [], []
    for yy in range(2):
        for zz in range(depth):
            for xx in range(2):
                dx, dy, dz = xx ^ x, yy ^ y, (z - zz) % depth
                half.append(dy if c == 0 else dx)
                index.append((dx if c == 0 else dy) * depth + dz)
    return half, index


def unit_tables():
    dp, seq = sizes()
    rows = []
    for d in range(dp):
        for y in range(seq):
            z, x, c = place(d)
            half, index = unit_spots(z, x, c, y)
            lines = [half]
            for side in range(2):
                line, last = [], [i for i, h in zip(index, half) if h == side][0]
                for i, h in zip(index, half):
                    last = i if h == side else last
                    line.append(last)
                lines.append(line)
            for core in range(2):
                lines.extend(unit_spots(z, x, core, y))
            rows.append(lines)
    table = jnp.asarray(np.array(rows, np.int32))
    me = lax.axis_index("dp") * seq + lax.axis_index("seq")
    return lax.dynamic_index_in_dim(table, me, 0, keepdims=False)


SPOTS = 3


def arrange(table, own, other):
    units, block = 2 * own.shape[0], (1,) + own.shape[1:]

    def body(table_ref, own_ref, other_ref, out_ref):
        half = table_ref[0, pl.program_id(0)]

        @pl.when(half == 0)
        def _():
            out_ref[...] = own_ref[...]

        @pl.when(half == 1)
        def _():
            out_ref[...] = other_ref[...]

    return pl.pallas_call(
        body,
        grid_spec=pltpu.PrefetchScalarGridSpec(
            num_scalar_prefetch=1,
            grid=(units,),
            in_specs=[
                pl.BlockSpec(block, lambda i, t: (t[1, i], 0, 0)),
                pl.BlockSpec(block, lambda i, t: (t[2, i], 0, 0)),
            ],
            out_specs=pl.BlockSpec(block, lambda i, t: (i, 0, 0)),
        ),
        out_shape=jax.ShapeDtypeStruct((units,) + own.shape[1:], own.dtype),
        compiler_params=pltpu.CompilerParams(vmem_limit_bytes=VMEM),
        cost_estimate=pl.CostEstimate(flops=1, bytes_accessed=1, transcendentals=0),
    )(table, own, other)


def tie(arrays, *others):
    return lax.optimization_barrier((arrays, others))[0]


class Gathering:
    def __init__(self, table, pair):
        self.table, self.pair, self.depth = table, pair, sizes()[0] // 4

    def z(self, *after):
        pair = tie(self.pair, *after)
        self.parts = [moved(pair, along_z(step)) for step in range(1, self.depth)]

    def end_z(self, *after):
        line = jnp.stack([self.pair] + tie(self.parts, *after))
        self.line = line.reshape((self.depth, -1) + line.shape[3:])
        return self.line

    def second(self, *after):
        self.came = moved(tie(self.line, *after), to_second)
        return self.came

    def third(self, *after):
        self.half = jnp.concatenate(tie([self.line, self.came], *after))
        self.far = moved(self.half, to_third)
        return self.far

    def arrange(self, *after):
        self.mine = arrange(self.table, *tie((self.half, self.far), *after))
        return self.mine

    def swap(self):
        dp, seq = sizes()
        other = moved(self.mine, to_core)
        shape = (seq, dp, self.mine.shape[1] // 2) + self.mine.shape[2:]
        return self.mine.reshape(shape), other.reshape(shape)


class Scattering:
    def __init__(self, away, keep):
        self.depth = sizes()[0] // 4
        groups = [[2 * i, 2 * i + 1] for i in range(sizes()[0] // 2)]
        self.take = lambda array: lax.psum_scatter(array, "dp", scatter_dimension=0, axis_index_groups=groups)
        self.away, self.keep = self.take(away), keep

    def third(self, *after):
        self.away = tie(self.away, *after)
        self.keep = self.take(tie(self.keep, self.away))
        self.came = moved(self.away, to_third)
        return self.away

    def end_third(self, *after):
        depth, keep, came = self.depth, *tie((self.keep, self.came), *after)
        self.away = (keep[depth:].astype(F32) + came[depth:].astype(F32)).astype(BF)
        self.keep = (keep[:depth].astype(F32) + came[:depth].astype(F32)).astype(BF)
        return self.away

    def second(self, *after):
        self.came = moved(tie(self.away, *after), to_second)

    def end_second(self, *after):
        keep, came = tie((self.keep, self.came), *after)
        self.line = (keep.astype(F32) + came.astype(F32)).astype(BF)
        return self.line

    def z(self, *after):
        line = tie(self.line, *after)
        self.parts = [moved(line[step], along_z(-step)) for step in range(1, self.depth)]
        return self.parts

    def total(self):
        total = self.line[0].astype(F32)
        for part in self.parts:
            total = total + part.astype(F32)
        return total.reshape((2, -1) + total.shape[1:])


def summed_z(array):
    depth = sizes()[0] // 4
    if depth == 4:
        for bit in (1, 2):
            array = array + moved(array, lambda z, x, c, y, bit=bit: (z ^ bit, x, c, y))
        return array
    total = array
    for step in range(1, depth):
        total = total + moved(array, along_z(step))
    return total


def hop_y(array):
    return array + moved(array, lambda z, x, c, y: (z, x, c, 1 - y))


def hop_x(array):
    return array + moved(array, lambda z, x, c, y: (z, 1 - x, c, y))


def params(**more):
    return pltpu.CompilerParams(vmem_limit_bytes=VMEM, **more)


def cost(flops, bytes_accessed):
    return pl.CostEstimate(flops=1, bytes_accessed=1, transcendentals=0)


def held(shape):
    zeros = (0,) * len(shape)
    return pl.BlockSpec(shape, lambda *_: zeros, pipeline_mode=pl.Buffered(1))


def fixed(shape):
    zeros = (0,) * len(shape)
    return pl.BlockSpec(shape, lambda *_: zeros)


SCALAR = pl.BlockSpec(memory_space=pltpu.SMEM)


def dot(a, b):
    return lax.dot_general(a, b, (((1,), (0,)), ((), ())), preferred_element_type=F32)


def dot_nt(a, b):
    return lax.dot_general(a, b, (((1,), (1,)), ((), ())), preferred_element_type=F32)


def dot_tn(a, b):
    return lax.dot_general(a, b, (((0,), (0,)), ((), ())), preferred_element_type=F32)


def split_sum(mask, terms):
    high = terms.astype(BF)
    low = (terms - high.astype(F32)).astype(BF)
    return dot(mask, high) + dot(mask, low)


def centred_norm(s):
    centred = s - jnp.mean(s, axis=-1, keepdims=True)
    rate = lax.rsqrt(jnp.mean(centred * centred, axis=-1, keepdims=True) + EPS)
    return centred * rate, rate


def norm_back(grad, unit, rate, gain):
    grad = grad * gain
    return rate * (
        grad
        - jnp.mean(grad, axis=-1, keepdims=True)
        - unit * jnp.mean(grad * unit, axis=-1, keepdims=True)
    )


def down_one(tile, first):
    rows = lax.broadcasted_iota(jnp.int32, tile.shape, 0)
    return jnp.where(rows == 0, first, pltpu.roll(tile, 1, 0))


def up_one(tile, last):
    size = tile.shape[0]
    rows = lax.broadcasted_iota(jnp.int32, tile.shape, 0)
    return jnp.where(rows == size - 1, last, pltpu.roll(tile, size - 1, 0))


def summed_rows(tile):
    return jnp.sum(tile, axis=0, keepdims=True)


def times(x, store, lo, hi, out_ref, rows=slice(None)):
    seq, dp, _, columns = store.shape
    for y in range(seq):
        weight = store[y, :, lo:hi, :].reshape(dp * (hi - lo), columns)
        out_ref[rows, y * columns : (y + 1) * columns] = dot(x, weight)


def times_back(g, store, lo, hi):
    seq, dp, _, columns = store.shape
    total = None
    for y in range(seq):
        weight = store[y, :, lo:hi, :].reshape(dp * (hi - lo), columns)
        part = dot_nt(g[:, y * columns : (y + 1) * columns], weight)
        total = part if total is None else total + part
    return total


def by_core(core_ref, mine, other, run):
    @pl.when(core_ref[0] == 0)
    def _():
        run(mine, other)

    @pl.when(core_ref[0] != 0)
    def _():
        run(other, mine)


def tile_rows(length):
    return min(256, length)


ALIVE, ENTERS, TAIL, HEAD, LEAVES = range(5)


def col(marks, which):
    return marks[:, which : which + 1]


def token_marks(document_numbers, earlier):
    rows, length = document_numbers.shape
    tile = tile_rows(length)
    tiles = document_numbers.reshape(rows, length // tile, tile)
    before = earlier.reshape(tiles.shape)[:, :, :1]
    marks = [
        document_numbers == earlier,
        (tiles == before).reshape(rows, length),
        document_numbers == document_numbers[:, -1:],
        document_numbers == document_numbers[:, :1],
        (tiles == tiles[:, :, -1:]).reshape(rows, length),
        jnp.zeros_like(document_numbers, dtype=bool),
        jnp.zeros_like(document_numbers, dtype=bool),
    ]
    marks = [m.astype(F32) for m in marks] + [document_numbers.astype(F32)]
    marks = jnp.stack(marks, axis=-1).reshape(rows * length, 8)
    lines = document_numbers.astype(F32).reshape(rows * length // tile, 1, tile)
    return marks, lines


def time_in(core, s, before, marks, gain, bias, mix, rate, mine, other, length):
    tokens, width = s.shape
    tile = tile_rows(length)
    per_run = length // tile
    runs = tokens // length

    def body(
        core_ref, s_ref, before_ref, marks_ref, gain_ref, bias_ref, mix_ref, rate_ref,
        mine_ref, other_ref,
        xk_ref, xv_ref, xr_ref, k_ref, v_ref, r_ref, end_ref, lead_ref, carry_ref,
    ):
        step = pl.program_id(0)
        run, part = lax.div(step, per_run), lax.rem(step, per_run)
        unit, _ = centred_norm(s_ref[...].astype(F32))
        normed = unit * gain_ref[...] + bias_ref[...]

        @pl.when(part == 0)
        def _():
            carry_ref[...] = before_ref[pl.ds(run, 1), :]
            end_ref[pl.ds(run, 1)] = jnp.zeros((1, 2, width), F32)

        lead_ref[0] = carry_ref[...]
        shifted = down_one(normed, carry_ref[...]) * col(marks_ref[...], ALIVE)
        carry_ref[...] = normed[tile - 1 :, :]
        change = normed - shifted
        xk_ref[...] = (shifted + mix_ref[0:1, :] * change).astype(BF)
        xv_ref[...] = (shifted + mix_ref[1:2, :] * change).astype(BF)
        xr_ref[...] = (shifted + mix_ref[2:3, :] * change).astype(BF)

        def project(first, second):
            rows = first.shape[2] // 2
            times(xk_ref[...], first, 0, rows, k_ref)
            times(xv_ref[...], first, rows, 2 * rows, v_ref)
            times(xr_ref[...], second, 0, rows, r_ref)

        by_core(core_ref, mine_ref, other_ref, project)
        places = lax.broadcasted_iota(jnp.int32, (tile, 1), 0).astype(F32)
        left = (length - 1 - part * tile).astype(F32) - places
        weight = jnp.exp(k_ref[...] - left * rate_ref[...]) * col(marks_ref[...], TAIL)
        ends = jnp.concatenate([summed_rows(weight * v_ref[...]), summed_rows(weight)], axis=0)
        end_ref[pl.ds(run, 1)] += ends[None]

    block = pl.BlockSpec((tile, width), lambda i: (i, 0))
    half, full = jax.ShapeDtypeStruct((tokens, width), BF), jax.ShapeDtypeStruct((tokens, width), F32)
    return pl.pallas_call(
        body,
        grid=(tokens // tile,),
        in_specs=[
            SCALAR, block, fixed(before.shape), pl.BlockSpec((tile, 8), lambda i: (i, 0)),
            fixed(gain.shape), fixed(bias.shape), fixed(mix.shape), fixed(rate.shape),
            held(mine.shape), held(other.shape),
        ],
        out_specs=[block] * 6 + [fixed((runs, 2, width)), pl.BlockSpec((1, 1, width), lambda i: (i, 0, 0))],
        out_shape=[half] * 3 + [full] * 3 + [
            jax.ShapeDtypeStruct((runs, 2, width), F32),
            jax.ShapeDtypeStruct((tokens // tile, 1, width), F32),
        ],
        scratch_shapes=[pltpu.VMEM((1, width), F32)],
        compiler_params=params(),
        cost_estimate=cost(6 * tokens * width * width, 22 * tokens * width + 4 * mine.size),
    )(core, s, before, marks, gain, bias, mix, rate, mine, other)


def time_out(core, s, k, v, r, enter, marks, lines, rate, bonus, mine, other, length):
    tokens, width = s.shape
    tile = tile_rows(length)
    per_run = length // tile

    def body(
        core_ref, s_ref, k_ref, v_ref, r_ref, enter_ref, marks_ref, line_ref, rate_ref, bonus_ref,
        mine_ref, other_ref, z_ref, sa_ref, sb_ref, out_ref, state_ref,
    ):
        step = pl.program_id(0)
        run, part = lax.div(step, per_run), lax.rem(step, per_run)

        @pl.when(part == 0)
        def _():
            state_ref[...] = enter_ref[pl.ds(run, 1)][0]

        marks = marks_ref[...]
        places = lax.broadcasted_iota(jnp.int32, (tile, 1), 0).astype(F32)
        spread = places * rate_ref[...]
        falling, decay = jnp.exp(-spread), jnp.exp(-rate_ref[...])
        powered = jnp.exp(k_ref[...])
        content = v_ref[...]
        raised = jnp.exp(k_ref[...] + spread)
        at = lax.broadcasted_iota(jnp.int32, (tile, tile), 0)
        source = lax.broadcasted_iota(jnp.int32, (tile, tile), 1)
        same = col(marks, 7) == line_ref[0]
        mask = jnp.where(jnp.logical_and(same, source < at), 1.0, 0.0).astype(BF)
        carried = falling * col(marks, ENTERS)
        ahead = falling * jnp.exp(rate_ref[...])
        state_a = ahead * split_sum(mask, raised * content) + carried * state_ref[0:1, :]
        state_b = ahead * split_sum(mask, raised) + carried * state_ref[1:2, :]
        sa_ref[...] = state_a
        sb_ref[...] = state_b
        state_ref[0:1, :] = decay * state_a[tile - 1 :] + (powered * content)[tile - 1 :]
        state_ref[1:2, :] = decay * state_b[tile - 1 :] + powered[tile - 1 :]
        scaled = powered * bonus_ref[...]
        answer = (state_a + scaled * content) / (state_b + scaled)
        z_ref[...] = (jax.nn.sigmoid(r_ref[...]) * answer).astype(BF)

        def project(first, second):
            rows = first.shape[2] // 2
            times(z_ref[...], second, rows, 2 * rows, out_ref)

        by_core(core_ref, mine_ref, other_ref, project)
        out_ref[...] += s_ref[...].astype(F32)

    block = pl.BlockSpec((tile, width), lambda i: (i, 0))
    half, full = jax.ShapeDtypeStruct((tokens, width), BF), jax.ShapeDtypeStruct((tokens, width), F32)
    return pl.pallas_call(
        body,
        grid=(tokens // tile,),
        in_specs=[
            SCALAR, block, block, block, block, fixed(enter.shape),
            pl.BlockSpec((tile, 8), lambda i: (i, 0)), pl.BlockSpec((1, 1, tile), lambda i: (i, 0, 0)),
            fixed(rate.shape), fixed(bonus.shape), held(mine.shape), held(other.shape),
        ],
        out_specs=[block] * 4,
        out_shape=[half, full, full, full],
        scratch_shapes=[pltpu.VMEM((2, width), F32)],
        compiler_params=params(),
        cost_estimate=cost(4 * tokens * width * width, 30 * tokens * width + 4 * mine.size),
    )(core, s, k, v, r, enter, marks, lines, rate, bonus, mine, other)


def lookup_block(store, rows, blocks, step):
    seq, dp, _, width = store.shape
    return pl.BlockSpec(
        (1, dp, rows, width), lambda i: (lax.div(step(i), blocks), 0, lax.rem(step(i), blocks), 0)
    )


def content_block(store, grain, at, group, step):
    seq, _, _, columns = store.shape
    return pl.BlockSpec((seq, group, grain, columns), lambda i: (0, step(i), at // grain, 0))


class Cut:
    def __init__(self, lookup, content, lookup_rows, grain):
        store, _ = lookup
        seq, dp, _, self.width = store.shape
        self.rows, self.grain = lookup_rows, grain
        self.group = self.width // grain
        self.steps = dp // self.group
        self.blocks = self.steps // seq
        self.at = content[1]

    def specs(self, lookup, content, step):
        return [
            lookup_block(lookup[0], self.rows, self.blocks, step),
            content_block(content[0], self.grain, self.at, self.group, step),
        ]


def hidden_step(x_ref, lookup_ref, content_ref, act_ref, total_ref, first):
    tokens = x_ref.shape[0]
    tile = min(512, tokens)
    _, dp, rows, width = lookup_ref.shape
    seq, group, grain, columns = content_ref.shape
    up = lookup_ref[0].reshape(dp * rows, width)
    for t in range(0, tokens, tile):
        hidden = jnp.maximum(dot(x_ref[t : t + tile, :], up), 0.0)
        act = (hidden * hidden).astype(BF)
        act_ref[0, t : t + tile, :] = act
        for y in range(seq):
            part = dot(act, content_ref[y].reshape(group * grain, columns))
            where = (slice(t, t + tile), slice(y * columns, (y + 1) * columns))
            total_ref[where] = part if first else total_ref[where] + part


def channel_one(s, before, marks, gain, bias, mix, lookup, content, cut, length):
    tokens, width = s.shape
    tile = tile_rows(length)
    tiles, per_run = tokens // tile, length // tile

    def body(
        s_ref, before_ref, marks_ref, gain_ref, bias_ref, mix_ref, lookup_ref, content_ref,
        xk_ref, xr_ref, lead_ref, act_ref, total_ref,
    ):
        @pl.when(pl.program_id(0) == 0)
        def _():
            last = None
            for i in range(tiles):
                rows = slice(i * tile, (i + 1) * tile)
                unit, _ = centred_norm(s_ref[rows, :])
                normed = unit * gain_ref[...] + bias_ref[...]
                if i % per_run == 0:
                    last = before_ref[i // per_run : i // per_run + 1, :]
                lead_ref[i] = last
                shifted = down_one(normed, last) * col(marks_ref[rows, :], ALIVE)
                last = normed[tile - 1 :, :]
                change = normed - shifted
                xk_ref[rows, :] = (shifted + mix_ref[0:1, :] * change).astype(BF)
                xr_ref[rows, :] = (shifted + mix_ref[1:2, :] * change).astype(BF)
            hidden_step(xk_ref, lookup_ref, content_ref, act_ref, total_ref, True)

        @pl.when(pl.program_id(0) > 0)
        def _():
            hidden_step(xk_ref, lookup_ref, content_ref, act_ref, total_ref, False)

    half, full = jax.ShapeDtypeStruct((tokens, width), BF), jax.ShapeDtypeStruct((tokens, width), F32)
    return pl.pallas_call(
        body,
        grid=(cut.steps,),
        in_specs=[
            held(s.shape), fixed(before.shape), held(marks.shape),
            fixed(gain.shape), fixed(bias.shape), fixed(mix.shape),
        ] + cut.specs(lookup, content, lambda i: i),
        out_specs=[
            fixed((tokens, width)), fixed((tokens, width)), fixed((tiles, 1, width)),
            pl.BlockSpec((1, tokens, cut.width), lambda i: (i, 0, 0)), fixed((tokens, width)),
        ],
        out_shape=[
            half, half, jax.ShapeDtypeStruct((tiles, 1, width), F32),
            jax.ShapeDtypeStruct((cut.steps, tokens, cut.width), BF), full,
        ],
        compiler_params=params(),
        cost_estimate=cost(
            4 * tokens * width * cut.width * cut.steps,
            14 * tokens * width + cut.steps * cut.width * (4 * width + 2 * tokens),
        ),
    )(s, before, marks, gain, bias, mix, lookup[0], content[0])


def channel_two(s, xk, xr, total, lookup, content, accept, cut, kind):
    tokens, width = s.shape
    tile = min(256, tokens)

    def body(
        s_ref, xk_ref, xr_ref, total_ref, accept_ref, lookup_ref, content_ref,
        act_ref, carried_ref, gate_ref, out_ref, sum_ref, take_ref,
    ):
        @pl.when(pl.program_id(0) == 0)
        def _():
            sum_ref[...] = total_ref[...]

        hidden_step(xk_ref, lookup_ref, content_ref, act_ref, sum_ref, False)

        @pl.when(pl.program_id(0) == cut.steps - 1)
        def _():
            for t in range(0, tokens, tile):
                rows = slice(t, t + tile)
                times(xr_ref[rows, :], accept_ref, 0, accept_ref.shape[2], take_ref)
                gate = jax.nn.sigmoid(take_ref[...])
                carried = sum_ref[rows, :]
                gate_ref[rows, :] = gate.astype(BF)
                carried_ref[rows, :] = carried.astype(BF)
                out_ref[rows, :] = (s_ref[rows, :] + gate * carried).astype(kind)

    half = jax.ShapeDtypeStruct((tokens, width), BF)
    return pl.pallas_call(
        body,
        grid=(cut.steps,),
        in_specs=[held(s.shape), held(xk.shape), held(xr.shape), held(total.shape), held(accept.shape)]
        + cut.specs(lookup, content, lambda i: i),
        out_specs=[pl.BlockSpec((1, tokens, cut.width), lambda i: (i, 0, 0))] + [fixed((tokens, width))] * 3,
        out_shape=[
            jax.ShapeDtypeStruct((cut.steps, tokens, cut.width), BF), half, half,
            jax.ShapeDtypeStruct((tokens, width), kind),
        ],
        scratch_shapes=[pltpu.VMEM((tokens, width), F32), pltpu.VMEM((tile, width), F32)],
        compiler_params=params(),
        cost_estimate=cost(
            4 * tokens * width * cut.width * cut.steps + 2 * tokens * width * width,
            20 * tokens * width + cut.steps * cut.width * (4 * width + 2 * tokens) + 2 * accept.size,
        ),
    )(s, xk, xr, total, accept, lookup[0], content[0])


def mixed_back(grads, s, lead, alive, gain, bias, mix_ref, after):
    unit, rate = centred_norm(s)
    normed = unit * gain + bias
    change = normed - down_one(normed, lead) * alive
    own, before, mixes = None, None, []
    for j, grad in enumerate(grads):
        mix = mix_ref[j : j + 1, :]
        a, b = mix * grad, (1.0 - mix) * grad
        own, before = (a, b) if own is None else (own + a, before + b)
        mixes.append(summed_rows(change * grad))
    before = before * alive
    grad = own + up_one(before, after)
    small = [summed_rows(grad * unit), summed_rows(grad)] + mixes
    return norm_back(grad, unit, rate, gain), before[0:1, :], small


def channel_back(
    core, g, fix, s, lead, marks, gain, bias, mix, gate, carried, xk, xr, acts, lookups, contents, accept,
    cut, length, packing, table,
):
    tokens, width = s.shape
    tile = tile_rows(length)
    tiles, per_run = tokens // tile, length // tile
    steps = cut.steps
    shapes, spots = packing
    seq, dp = accept.shape[:2]
    columns = width // seq
    half_rows = accept.shape[2] // 2
    last = 2 * steps - 1
    slots = len(shapes)
    split = slots == 2
    units = dp // 2

    def body(
        core_ref, g_ref, fix_ref, s_ref, lead_ref, marks_ref, gain_ref, bias_ref, mix_ref,
        gate_ref, carried_ref, xk_ref, xr_ref, act0_ref, act1_ref, accept_ref,
        lookup0_ref, content0_ref, lookup1_ref, content1_ref, table_ref, *rest,
    ):
        outs, rest = rest[:slots], rest[slots:]
        out_ref, edge_ref, small_ref, gc_ref, gr_ref, sum_ref, key_ref, val_ref, take_ref, sem, stage_ref = rest
        if not split:
            lookup_out, content_out, accept_out = outs
        step = pl.program_id(0)
        slot = lax.rem(step, 2)

        def waits(which):
            if split:
                rows = pl.ds(0, cut.rows)
                key = outs[1].at[0, :, :, rows, :]
                val = outs[1].at[0, pl.ds(0, seq * cut.group // 2), :, pl.ds(0, cut.grain), :]
                val_from = val_ref.at[which].reshape(seq * cut.group // 2, 2, cut.grain, columns)
            else:
                key = lookup_out.at[0, 0, :, :, pl.ds(0, cut.rows), :]
                val = content_out.at[0, :, pl.ds(0, cut.group // 2), :, :, :]
                val_from = val_ref.at[which]
            pltpu.make_async_copy(key_ref.at[which], key, sem.at[which, 0]).wait()
            pltpu.make_async_copy(val_from, val, sem.at[which, 1]).wait()

        def send(source, unit, store, rows, sem):
            half = table_ref[SPOTS + 2 * store, unit]
            index = table_ref[SPOTS + 1 + 2 * store, unit]
            for side in range(2):

                @pl.when(half == 1 - side)
                def _(side=side):
                    pltpu.make_async_copy(source, outs[side].at[store, index, :, rows, :], sem).start()

        def start(which, store, q):
            y, block = lax.div(q, cut.blocks), lax.rem(q, cut.blocks)
            if split:
                rows = pl.ds(pl.multiple_of(spots[0] + block * cut.rows, 16), cut.rows)
                for unit in range(units):
                    send(key_ref.at[which, unit], y * units + unit, store, rows, sem.at[which, 0])
                for y in range(seq):
                    for part in range(cut.group // 2):
                        unit = y * units + q * (cut.group // 2) + part
                        rows = pl.ds(spots[1], cut.grain)
                        send(val_ref.at[which, y, part], unit, store, rows, sem.at[which, 1])
            else:
                rows = pl.ds(pl.multiple_of(block * cut.rows, 16), cut.rows)
                key = lookup_out.at[store, y, :, :, rows, :]
                pltpu.make_async_copy(key_ref.at[which], key, sem.at[which, 0]).start()
                val = content_out.at[store, :, pl.ds(q * (cut.group // 2), cut.group // 2), :, :, :]
                pltpu.make_async_copy(val_ref.at[which], val, sem.at[which, 1]).start()

        def store_of_step(i):
            core = core_ref[0]
            return jnp.where(i < steps, core, 1 - core), lax.rem(i, steps)

        @pl.when(step == 0)
        def _():
            for i in range(tiles):
                rows = slice(i * tile, (i + 1) * tile)
                grad = g_ref[rows, :].astype(F32)
                if (i + 1) % per_run == 0:
                    at = lax.broadcasted_iota(jnp.int32, grad.shape, 0)
                    run = i // per_run
                    grad = jnp.where(at == tile - 1, grad + fix_ref[run : run + 1, :], grad)
                gate = gate_ref[rows, :].astype(F32)
                passed = grad * gate
                out_ref[rows, :] = grad
                gc_ref[rows, :] = passed.astype(BF)
                gr_ref[rows, :] = (passed * carried_ref[rows, :].astype(F32) * (1.0 - gate)).astype(BF)

        @pl.when(step >= 2)
        def _():
            waits(slot)

        def work(act_ref, lookup_ref, content_ref, first):
            up = lookup_ref[0].reshape(dp * cut.rows, cut.width)
            size = min(512, tokens)
            for t in range(0, tokens, size):
                rows = slice(t, t + size)
                act = act_ref[0, rows, :].astype(F32)
                grad = None
                for y in range(seq):
                    part = dot_nt(
                        gc_ref[rows, y * columns : (y + 1) * columns],
                        content_ref[y].reshape(cut.group * cut.grain, columns),
                    )
                    grad = part if grad is None else grad + part
                grad = (grad * (2.0 * jnp.sqrt(act))).astype(BF)
                take_ref[rows, :] = grad
                part = dot_nt(grad, up)
                sum_ref[rows, :] = part if first else sum_ref[rows, :] + part
            key = dot_tn(xk_ref[...], take_ref[...])
            key_ref[slot] = key.astype(BF).reshape(units, 2, cut.rows, cut.width)
            for y in range(seq):
                val = dot_tn(act_ref[0], gc_ref[:, y * columns : (y + 1) * columns])
                val_ref[slot, y] = val.astype(BF).reshape(cut.group // 2, 2, cut.grain, columns)

        @pl.when(step == 0)
        def _():
            work(act0_ref, lookup0_ref, content0_ref, True)

        @pl.when(jnp.logical_and(step > 0, step < steps))
        def _():
            work(act0_ref, lookup0_ref, content0_ref, False)

        @pl.when(step >= steps)
        def _():
            work(act1_ref, lookup1_ref, content1_ref, False)

        start(slot, *store_of_step(step))

        @pl.when(step == last)
        def _():
            waits(1 - slot)
            waits(slot)
            rows = pl.ds(spots[2], half_rows)
            for y in range(seq):
                grad = dot_tn(xr_ref[...], gr_ref[:, y * columns : (y + 1) * columns])
                grad = grad.astype(BF).reshape(dp, 2 * half_rows, columns)
                for h in range(2):
                    part = grad[:, h * half_rows : (h + 1) * half_rows, :]
                    stage_ref[h, y] = part.reshape(units, 2, half_rows, columns)
                    if split:
                        for unit in range(units):
                            send(stage_ref.at[h, y, unit], y * units + unit, h, rows, sem.at[h, 2 + y])
                    else:
                        take = accept_out.at[h, y]
                        pltpu.make_async_copy(stage_ref.at[h, y], take, sem.at[h, 2 + y]).start()
            after = None
            small = None
            for i in reversed(range(tiles)):
                at = slice(i * tile, (i + 1) * tile)
                if (i + 1) % per_run == 0:
                    after = jnp.zeros((1, width), F32)
                grads = [sum_ref[at, :], times_back(gr_ref[at, :], accept_ref, 0, 2 * half_rows)]
                add, after, more = mixed_back(
                    grads, s_ref[at, :], lead_ref[i], col(marks_ref[at, :], ALIVE),
                    gain_ref[...], bias_ref[...], mix_ref, after,
                )
                out_ref[at, :] += add
                small = more if small is None else [a + b for a, b in zip(small, more)]
                if i % per_run == 0:
                    edge_ref[i // per_run : i // per_run + 1, :] = after
            for j, line in enumerate(small):
                small_ref[j : j + 1, :] = line
            for h in range(2):
                for y in range(seq):
                    if split:
                        take = outs[1].at[0, :, :, rows, :]
                    else:
                        take = accept_out.at[h, y]
                    pltpu.make_async_copy(stage_ref.at[h, y], take, sem.at[h, 2 + y]).wait()

    own = lambda i: jnp.minimum(i, steps - 1)
    partner = lambda i: jnp.maximum(i - steps, 0)
    act = lambda step: pl.BlockSpec((1, tokens, cut.width), lambda i: (step(i), 0, 0))
    any_space = pl.BlockSpec(memory_space=pl.ANY)
    return pl.pallas_call(
        body,
        grid=(2 * steps,),
        in_specs=[
            SCALAR, held(g.shape), fixed(fix.shape), held(s.shape), fixed(lead.shape), held(marks.shape),
            fixed(gain.shape), fixed(bias.shape), fixed(mix.shape), held(gate.shape), held(carried.shape),
            held(xk.shape), held(xr.shape), act(own), act(partner), held(accept.shape),
        ] + cut.specs(lookups[0], contents[0], own) + cut.specs(lookups[1], contents[1], partner) + [SCALAR],
        out_specs=[any_space] * slots + [fixed((tokens, width)), fixed(fix.shape), fixed((4, width))],
        out_shape=[jax.ShapeDtypeStruct(shape, BF) for shape in shapes] + [
            jax.ShapeDtypeStruct((tokens, width), F32), jax.ShapeDtypeStruct(fix.shape, F32),
            jax.ShapeDtypeStruct((4, width), F32),
        ],
        scratch_shapes=[
            pltpu.VMEM((tokens, width), BF), pltpu.VMEM((tokens, width), BF),
            pltpu.VMEM((tokens, width), F32),
            pltpu.VMEM((2, units, 2, cut.rows, cut.width), BF),
            pltpu.VMEM((2, seq, cut.group // 2, 2, cut.grain, columns), BF),
            pltpu.VMEM((tokens, cut.width), BF),
            pltpu.SemaphoreType.DMA((2, 2 + seq)),
            pltpu.VMEM((2, seq, units, 2, half_rows, columns), BF),
        ],
        compiler_params=params(),
        cost_estimate=cost(
            16 * tokens * width * cut.width * steps + 4 * tokens * width * width,
            30 * tokens * width + 2 * steps * cut.width * (8 * width + 2 * tokens),
        ),
    )(
        core, g, fix, s, lead, marks, gain, bias, mix, gate, carried, xk, xr, *acts, accept,
        lookups[0][0], contents[0][0], lookups[1][0], contents[1][0], table,
    )


def out_back(core, g, fix, k, v, r, sa, sb, marks, rate, bonus, mine, other, length):
    tokens, width = g.shape
    tile = tile_rows(length)
    per_run = length // tile
    runs = tokens // length

    def body(
        core_ref, g_ref, fix_ref, k_ref, v_ref, r_ref, sa_ref, sb_ref, marks_ref, rate_ref, bonus_ref,
        mine_ref, other_ref, go_ref, gr_ref, gn_ref, gd_ref, chain_ref, gz_ref,
    ):
        step = pl.program_id(0)
        run, part = lax.div(step, per_run), lax.rem(step, per_run)
        grad = g_ref[...]
        at = lax.broadcasted_iota(jnp.int32, grad.shape, 0)
        hit = jnp.logical_and(at == tile - 1, part == per_run - 1)
        go_ref[...] = jnp.where(hit, grad + fix_ref[pl.ds(run, 1), :], grad).astype(BF)

        def project(first, second):
            rows = first.shape[2] // 2
            gz_ref[...] = times_back(go_ref[...], second, rows, 2 * rows)

        by_core(core_ref, mine_ref, other_ref, project)
        gate = jax.nn.sigmoid(r_ref[...])
        scaled = jnp.exp(k_ref[...]) * bonus_ref[...]
        inverse = 1.0 / (sb_ref[...] + scaled)
        answer = (sa_ref[...] + scaled * v_ref[...]) * inverse
        gated = gz_ref[...] * gate
        gr_ref[...] = (gated * answer * (1.0 - gate)).astype(BF)
        gn = gated * inverse
        gd = -gn * answer
        gn_ref[...] = gn
        gd_ref[...] = gd

        @pl.when(part == 0)
        def _():
            chain_ref[pl.ds(run, 1)] = jnp.zeros((1, 2, width), F32)

        places = (lax.broadcasted_iota(jnp.int32, (tile, 1), 0) + part * tile).astype(F32)
        weight = jnp.exp(-places * rate_ref[...]) * col(marks_ref[...], HEAD)
        sums = jnp.concatenate([summed_rows(weight * gn), summed_rows(weight * gd)], axis=0)
        chain_ref[pl.ds(run, 1)] += sums[None]

    block = pl.BlockSpec((tile, width), lambda i: (i, 0))
    half, full = jax.ShapeDtypeStruct((tokens, width), BF), jax.ShapeDtypeStruct((tokens, width), F32)
    return pl.pallas_call(
        body,
        grid=(tokens // tile,),
        in_specs=[
            SCALAR, block, fixed(fix.shape), block, block, block, block, block,
            pl.BlockSpec((tile, 8), lambda i: (i, 0)), fixed(rate.shape), fixed(bonus.shape),
            held(mine.shape), held(other.shape),
        ],
        out_specs=[block] * 4 + [fixed((runs, 2, width))],
        out_shape=[half, half, full, full, jax.ShapeDtypeStruct((runs, 2, width), F32)],
        scratch_shapes=[pltpu.VMEM((tile, width), F32)],
        compiler_params=params(),
        cost_estimate=cost(2 * tokens * width * width, 36 * tokens * width + 4 * mine.size),
    )(core, g, fix, k, v, r, sa, sb, marks, rate, bonus, mine, other)


def time_back(
    core, g, fix, s, lead, k, v, sa, sb, gn, gd, gr, leave, marks, lines, gain, bias, mix, rate, bonus,
    mine, other, length,
):
    tokens, width = s.shape
    tile = tile_rows(length)
    tiles, per_run = tokens // tile, length // tile
    runs = tokens // length

    def body(
        core_ref, g_ref, fix_ref, s_ref, lead_ref, k_ref, v_ref, sa_ref, sb_ref, gn_ref, gd_ref, gr_ref,
        leave_ref, marks_ref, line_ref, gain_ref, bias_ref, mix_ref, rate_ref, bonus_ref,
        mine_ref, other_ref, gk_ref, gv_ref, out_ref, edge_ref, small_ref,
        state_ref, after_ref, xk_ref, xv_ref, xr_ref,
    ):
        step = pl.program_id(0)
        i = tiles - 1 - step
        run, part = lax.div(i, per_run), lax.rem(i, per_run)

        @pl.when(part == per_run - 1)
        def _():
            state_ref[...] = leave_ref[pl.ds(run, 1)][0]
            after_ref[...] = jnp.zeros((1, width), F32)

        marks = marks_ref[...]
        alive = col(marks, ALIVE)
        places = lax.broadcasted_iota(jnp.int32, (tile, 1), 0).astype(F32)
        spread = places * rate_ref[...]
        falling, decay = jnp.exp(-spread), jnp.exp(-rate_ref[...])
        rising = jnp.exp(spread + rate_ref[...])
        at = lax.broadcasted_iota(jnp.int32, (tile, tile), 0)
        source = lax.broadcasted_iota(jnp.int32, (tile, tile), 1)
        same = col(marks, 7) == line_ref[0]
        mask = jnp.where(jnp.logical_and(same, source > at), 1.0, 0.0).astype(BF)
        gn, gd = gn_ref[...], gd_ref[...]
        carried = jnp.exp(spread - (tile - 1) * rate_ref[...]) * col(marks, LEAVES)
        ga = rising * split_sum(mask, falling * gn) + carried * state_ref[0:1, :]
        gb = rising * split_sum(mask, falling * gd) + carried * state_ref[1:2, :]
        first = alive[0:1, :]
        state_ref[0:1, :] = first * (gn[0:1, :] + decay * ga[0:1, :])
        state_ref[1:2, :] = first * (gd[0:1, :] + decay * gb[0:1, :])
        powered, content = jnp.exp(k_ref[...]), v_ref[...]
        scaled = powered * bonus_ref[...]
        reward = (gn * content + gd) * scaled
        gv_ref[...] = (gn * scaled + powered * ga).astype(BF)
        gk_ref[...] = (reward + powered * (content * ga + gb)).astype(BF)
        sums = [summed_rows(ga * sa_ref[...] + gb * sb_ref[...]), summed_rows(reward)]

        def project(first, second):
            rows = first.shape[2] // 2
            xk_ref[...] = times_back(gk_ref[...], first, 0, rows)
            xv_ref[...] = times_back(gv_ref[...], first, rows, 2 * rows)
            xr_ref[...] = times_back(gr_ref[...], second, 0, rows)

        by_core(core_ref, mine_ref, other_ref, project)
        grads = [xk_ref[...], xv_ref[...], xr_ref[...]]
        add, after, small = mixed_back(
            grads, s_ref[...].astype(F32), lead_ref[0], alive, gain_ref[...], bias_ref[...], mix_ref,
            after_ref[...],
        )
        after_ref[...] = after
        grad = g_ref[...]
        row = lax.broadcasted_iota(jnp.int32, grad.shape, 0)
        hit = jnp.logical_and(row == tile - 1, part == per_run - 1)
        out_ref[...] = jnp.where(hit, grad + fix_ref[pl.ds(run, 1), :], grad) + add
        edge_ref[pl.ds(run, 1), :] = after

        @pl.when(step == 0)
        def _():
            small_ref[...] = jnp.zeros_like(small_ref)

        for j, line in enumerate(small + sums):
            small_ref[j : j + 1, :] += line

    back = lambda i: tiles - 1 - i
    block = pl.BlockSpec((tile, width), lambda i: (back(i), 0))
    half, full = jax.ShapeDtypeStruct((tokens, width), BF), jax.ShapeDtypeStruct((tokens, width), F32)
    return pl.pallas_call(
        body,
        grid=(tiles,),
        in_specs=[
            SCALAR, block, fixed(fix.shape), block, pl.BlockSpec((1, 1, width), lambda i: (back(i), 0, 0)),
            block, block, block, block, block, block, block, fixed(leave.shape),
            pl.BlockSpec((tile, 8), lambda i: (back(i), 0)),
            pl.BlockSpec((1, 1, tile), lambda i: (back(i), 0, 0)),
            fixed(gain.shape), fixed(bias.shape), fixed(mix.shape), fixed(rate.shape), fixed(bonus.shape),
            held(mine.shape), held(other.shape),
        ],
        out_specs=[block, block, block, fixed(fix.shape), fixed((7, width))],
        out_shape=[
            half, half, full, jax.ShapeDtypeStruct(fix.shape, F32), jax.ShapeDtypeStruct((7, width), F32),
        ],
        scratch_shapes=[
            pltpu.VMEM((2, width), F32), pltpu.VMEM((1, width), F32),
            pltpu.VMEM((tile, width), F32), pltpu.VMEM((tile, width), F32), pltpu.VMEM((tile, width), F32),
        ],
        compiler_params=params(),
        cost_estimate=cost(8 * tokens * width * width, 46 * tokens * width + 4 * mine.size),
    )(
        core, g, fix, s, lead, k, v, sa, sb, gn, gd, gr, leave, marks, lines, gain, bias, mix, rate, bonus,
        mine, other,
    )


def weight_grads(first, second, grads, table):
    dp, seq = sizes()
    tokens, width = grads[0].shape
    rows, columns = width // dp, width // seq
    pairs = list(zip(first + second, grads))
    split, units = paired(), dp // 2
    if split:
        shapes = [(2, units * seq // 2, 2, 2 * rows, columns)] * 2
    else:
        shapes = [(2, seq, units, 2, 2 * rows, columns)]

    def body(table_ref, *refs):
        ins, rest = refs[: 2 * len(pairs)], refs[2 * len(pairs) :]
        outs, (x_ref, g_ref, stage_ref, sem, out_sem) = rest[: len(shapes)], rest[len(shapes) :]
        which, y = pl.program_id(0), pl.program_id(1)
        slot = lax.rem(which, 2)
        step = which * seq + y
        place = lax.rem(step, 2)

        def copies(i):
            return (
                pltpu.make_async_copy(ins[2 * i], x_ref.at[i % 2], sem.at[i % 2, 0]),
                pltpu.make_async_copy(ins[2 * i + 1], g_ref.at[i % 2], sem.at[i % 2, 1]),
            )

        def wait(at):
            target = outs[0].at[0, :, :, pl.ds(0, rows), :] if split else outs[0].at[0, 0, :, :, pl.ds(0, rows), :]
            pltpu.make_async_copy(stage_ref.at[at], target, out_sem.at[at]).wait()

        @pl.when(step == 0)
        def _():
            for copy in copies(0):
                copy.start()

        for i in range(len(pairs)):

            @pl.when(jnp.logical_and(which == i, y == 0))
            def _(i=i):
                for copy in copies(i):
                    copy.wait()
                if i + 1 < len(pairs):
                    for copy in copies(i + 1):
                        copy.start()

        @pl.when(step >= 2)
        def _():
            wait(place)

        at = pl.ds(pl.multiple_of(y * columns, columns), columns)
        grad = dot_tn(x_ref[slot], g_ref[slot, :, at])
        stage_ref[place] = grad.astype(BF).reshape(units, 2, rows, columns)
        store = lax.div(which, 2)
        span = pl.ds(pl.multiple_of(lax.rem(which, 2) * rows, 16), rows)
        if split:
            for unit in range(units):
                half = table_ref[SPOTS + 2 * store, y * units + unit]
                index = table_ref[SPOTS + 1 + 2 * store, y * units + unit]
                for side in range(2):

                    @pl.when(half == 1 - side)
                    def _(side=side, unit=unit, index=index):
                        pltpu.make_async_copy(
                            stage_ref.at[place, unit], outs[side].at[store, index, :, span, :], out_sem.at[place]
                        ).start()
        else:
            target = outs[0].at[store, y, :, :, span, :]
            pltpu.make_async_copy(stage_ref.at[place], target, out_sem.at[place]).start()

        @pl.when(step == len(pairs) * seq - 1)
        def _():
            wait(1 - place)
            wait(place)

    any_space = pl.BlockSpec(memory_space=pl.ANY)
    return pl.pallas_call(
        body,
        grid=(len(pairs), seq),
        in_specs=[SCALAR] + [any_space] * (2 * len(pairs)),
        out_specs=[any_space] * len(shapes),
        out_shape=[jax.ShapeDtypeStruct(shape, BF) for shape in shapes],
        scratch_shapes=[
            pltpu.VMEM((2, tokens, width), BF), pltpu.VMEM((2, tokens, width), BF),
            pltpu.VMEM((2, units, 2, rows, columns), BF),
            pltpu.SemaphoreType.DMA((2, 2)), pltpu.SemaphoreType.DMA((2,)),
        ],
        compiler_params=params(),
        cost_estimate=cost(8 * tokens * width * width, 16 * tokens * width + 8 * width * width),
    )(table, *[array for pair in pairs for array in pair])


def passed_along(array, axis, by):
    devices = lax.axis_size(axis)
    pairs = [(i, i + by) for i in range(devices) if 0 <= i + by < devices]
    return lax.ppermute(array, axis, pairs)


def entering(chain, ends, by):
    came = passed_along(ends, "seq", by)
    for _ in range(lax.axis_size("seq") - 2):
        came = passed_along(ends + chain * came, "seq", by)
    return came


def last_tokens(s, length):
    return s.reshape(-1, length, s.shape[-1])[:, -1].astype(F32)


def edge_norm(s, length, gain, bias):
    unit, _ = centred_norm(last_tokens(s, length))
    return passed_along(unit * gain + bias, "seq", 1)


def edge_back(edge, s, length, gain):
    came = passed_along(edge, "seq", -1)
    unit, rate = centred_norm(last_tokens(s, length))
    small = jnp.concatenate([summed_rows(came * unit), summed_rows(came)])
    return norm_back(came, unit, rate, gain), small


def cut_lookup(shard, grain):
    rows, columns = shard.shape
    width = min(512, columns // 2)
    cut = shard.reshape(rows, columns // (2 * grain), 2, grain).transpose(2, 0, 1, 3)
    cut = cut.reshape(2, rows, columns // 2 // width, width).transpose(0, 2, 1, 3)
    return cut.reshape(2, -1, width)


def join_lookup(first, second, rows, grain):
    width = first.shape[-1]
    cut = jnp.stack([first, second]).reshape(2, -1, rows, width).transpose(0, 2, 1, 3)
    cut = cut.reshape(2, rows, -1, grain).transpose(1, 2, 0, 3)
    return cut.reshape(rows, -1)


def spots_of(shards):
    return [0] + np.cumsum([shard.shape[0] for shard in shards]).tolist()


def cut_at(array, spots):
    return [array[a:b] for a, b in zip(spots, spots[1:])]


def gather_plain(first, second):
    dp, seq = sizes()
    whole = lambda a: (lax.all_gather(a, ("seq", "dp")).reshape((seq, dp) + a.shape), 0)
    return [whole(a) for a in first], [whole(a) for a in second]


def scatter_plain(stores):
    dp, seq = sizes()
    take = lambda a: lax.psum_scatter(
        a.reshape((seq * dp,) + a.shape[-2:]), ("seq", "dp"), scatter_dimension=0
    ).astype(F32)
    return [take(s[0]) for s in stores], [take(s[1]) for s in stores]


def by_half(first_is_low, low, high):
    return jnp.where(first_is_low, low, high), jnp.where(first_is_low, high, low)


def partner_y(array):
    return lax.ppermute(array, "seq", [(0, 1), (1, 0)])


def rows_cut(array):
    half = array.shape[0] // 2
    return by_half(lax.axis_index("seq") == 0, array[:half], array[half:])


def rows_joined(kept, came):
    low = lax.axis_index("seq") == 0
    return jnp.concatenate(by_half(low, kept, came), axis=1)


def runs_cut(array):
    length = array.shape[1] // 2
    return by_half(lax.axis_index("seq") == 0, array[:, :length], array[:, length:])


def runs_joined(kept, came):
    low = lax.axis_index("seq") == 0
    return jnp.concatenate(by_half(low, kept, came), axis=0)


def per_device(
    entering_activations,
    document_numbers,
    result_cotangent,
    normalizer_scales,
    normalizer_offsets,
    shift_blend_factors,
    fading_natural_logs_per_feature,
    feature_reward_logs,
    attention_triple_matrix,
    attention_result_matrix,
    channelmix_lookup_matrix,
    channelmix_content_matrix,
    channelmix_accept_matrix,
):
    dp, seq = sizes()
    staged = paired()
    core = core_of()
    cores = core.reshape(1)
    table = unit_tables() if staged else jnp.zeros((1, 1), jnp.int32)
    layers = attention_triple_matrix.shape[0]
    runs, length, width = entering_activations.shape
    tokens, columns = runs * length, width // seq
    swapped = staged and layers == 2 and runs % 2 == 0
    if swapped:
        kept_rows, sent_rows = rows_cut(document_numbers)
        document_numbers = rows_joined(kept_rows, partner_y(sent_rows))
        kept_rows, sent_rows = rows_cut(entering_activations)
        entering_activations = rows_joined(kept_rows, partner_y(sent_rows))
        runs, length = runs // 2, length * 2

    lookup_rows = channelmix_lookup_matrix.shape[1]
    grain = channelmix_content_matrix.shape[1] // 2
    half_rows = channelmix_accept_matrix.shape[1] // 2

    shards = []
    for depth in range(layers):
        triple, result = attention_triple_matrix[depth], attention_result_matrix[depth]
        lookup = cut_lookup(channelmix_lookup_matrix[depth], grain)
        content, accept = channelmix_content_matrix[depth], channelmix_accept_matrix[depth]
        shards.append(([jnp.concatenate([triple[0], triple[1]])], [jnp.concatenate([triple[2], result])]))
        shards.append(
            (
                [lookup[0], content[:grain], accept[:half_rows]],
                [lookup[1], content[grain:], accept[half_rows:]],
            )
        )

    held = {}
    if staged:
        first = jnp.concatenate([shard for group in shards for shard in group[0]])
        second = jnp.concatenate([shard for group in shards for shard in group[1]])
        kept = jnp.where(core == 0, first, second)
        came = moved(jnp.where(core == 0, second, first), to_core)
        pair = jnp.where(core == 0, jnp.stack([kept, came]), jnp.stack([came, kept]))
        ends = spots_of([jnp.concatenate(group[0]) for group in shards])
        moves = [Gathering(table, pair[:, a:b]) for a, b in zip(ends, ends[1:])]
    else:
        moves = [gather_plain(*group) for group in shards]

    def give_att(depth, mine, other):
        held["att", depth] = (mine, other)

    def give_chan(depth, mine, other):
        takes = [array[:, :, at : at + half_rows] for array, at in (mine[2], other[2])]
        first = jnp.where(core == 0, takes[0], takes[1])
        second = jnp.where(core == 0, takes[1], takes[0])
        held["cut", depth] = Cut(mine[0], mine[1], lookup_rows, grain)
        held["chan", depth] = (mine, other, jnp.concatenate([first, second], axis=2))

    def with_rows(array, group):
        return [(array, at) for at in spots_of(shards[group][0])[:-1]]

    if swapped:
        border = jnp.full((runs, 1), -1, document_numbers.dtype)
    else:
        border = passed_along(document_numbers[:, -1:] + 1, "seq", 1) - 1
    earlier = jnp.concatenate([border, document_numbers[:, :-1]], axis=1)
    edges = jnp.zeros((runs, width), F32)
    states = jnp.zeros((runs, 2, width), F32)
    marks, lines = token_marks(document_numbers, earlier)
    through = (earlier[:, :1] == document_numbers[:, -1:]).astype(F32)[:, :, None]
    begins = (earlier[:, :1] == document_numbers[:, :1]).astype(F32)[:, :, None]
    rates = jnp.exp(fading_natural_logs_per_feature)
    bonuses = jnp.exp(feature_reward_logs)

    def layer_values(depth):
        gain, bias, mix = normalizer_scales[depth], normalizer_offsets[depth], shift_blend_factors[depth]
        rate, bonus = rates[depth : depth + 1], bonuses[depth : depth + 1]
        return gain, bias, mix, rate, bonus, jnp.exp(-length * rate)[None] * through

    kept = {}

    def run_time_in(depth, flow):
        gain, bias, mix, rate, _, _ = layer_values(depth)
        before = edges if swapped else edge_norm(flow, length, gain[0], bias[0])
        kept["time", depth] = (flow,) + tuple(
            time_in(
                cores, flow, before, marks, gain[0:1], bias[0:1], mix[:3], rate, *held["att", depth], length
            )
        )
        return kept["time", depth][4]

    def run_time_out(depth, *after):
        _, _, _, rate, bonus, chain = layer_values(depth)
        flow, xk, xv, xr, k, v, r, ends, lead = kept["time", depth]
        enter = states if swapped else entering(chain, ends, 1)
        k = tie(k, *after) if after else k
        z, sa, sb, middle = time_out(
            cores, flow, k, v, r, enter, marks, lines, rate, bonus, *held["att", depth], length
        )
        kept["time", depth] = (flow, lead, xk, xv, xr, k, v, r, z, sa, sb)
        gain, bias, _, _, _, _ = layer_values(depth)
        before = edges if swapped else edge_norm(middle, length, gain[1], bias[1])
        kept["middle", depth] = (middle, before)
        return middle

    def run_channel_one(depth, mine, cut, *after):
        gain, bias, mix, _, _, _ = layer_values(depth)
        middle, before = kept["middle", depth]
        before = tie(before, *after) if after else before
        kept["one", depth] = channel_one(
            middle, before, marks, gain[1:2], bias[1:2], mix[3:], mine[0], mine[1], cut, length
        )
        return kept["one", depth][4]

    def run_channel_two(depth, *after):
        middle, _ = kept["middle", depth]
        xk, xr, lead, act0, total = kept["one", depth]
        _, other, accept = held["chan", depth]
        total = tie(total, *after) if after else total
        kind = BF if depth == layers - 1 else F32
        act1, carried, gate, flow = channel_two(
            middle, xk, xr, total, other[0], other[1], accept, held["cut", depth], kind
        )
        kept["chan", depth] = (middle, lead, xk, xr, (act0, act1), carried, gate)
        return flow

    flow = entering_activations.reshape(tokens, width)
    if staged and layers == 2:
        att0, chan0, att1, chan1 = moves

        def place_att(depth, move):
            give_att(depth, *move.swap())

        def place_chan(depth, move, group):
            mine, other = move.swap()
            give_chan(depth, with_rows(mine, group), with_rows(other, group))

        att0.z()
        chan0.z(att0.end_z())
        att0.second(flow)
        far = att0.third(chan0.parts[0])
        att0.arrange()
        att0.mine = tie(att0.mine, chan0.parts)
        chan0.end_z(far)
        near = chan0.second()
        place_att(0, att0)
        done = run_time_in(0, flow)
        far = chan0.third(done)
        att1.z(done)
        done = run_time_out(0, near)
        line = att1.end_z(done)
        chan1.z(line)
        near = att1.second(far, done)
        mine = chan0.arrange(done, line, chan1.parts)
        place_chan(0, chan0, 1)
        far = att1.third(mine)
        own, _, _ = held["chan", 0]
        done = run_channel_one(0, own, held["cut", 0], near)
        line = chan1.end_z(done)
        near = chan1.second(far)
        mine = att1.arrange(done, line)
        place_att(1, att1)
        flow = run_channel_two(0, mine)
        far = chan1.third(flow)
        done = run_time_in(1, tie(flow, near))
        done = run_time_out(1)
        chan1.arrange(done)
        place_chan(1, chan1, 3)
        own, _, _ = held["chan", 1]
        run_channel_one(1, own, held["cut", 1])
        y_out = run_channel_two(1)
        if swapped:
            kept_rows, sent_rows = rows_cut(tie(result_cotangent, far))
            result_cotangent = rows_joined(kept_rows, partner_y(sent_rows))
            kept_runs, sent_runs = runs_cut(y_out.reshape(runs, length, width))
            y_out = runs_joined(kept_runs, partner_y(sent_runs))
    else:
        for depth in range(layers):
            if staged:
                for move in moves[2 * depth : 2 * depth + 2]:
                    move.z()
                    move.end_z()
                    move.second()
                    move.third()
                    move.arrange()
                give_att(depth, *moves[2 * depth].swap())
                mine, other = moves[2 * depth + 1].swap()
                group = 2 * depth + 1
                give_chan(depth, with_rows(mine, group), with_rows(other, group))
            else:
                mine, other = moves[2 * depth]
                give_att(depth, mine[0][0], other[0][0])
                give_chan(depth, *moves[2 * depth + 1])
            run_time_in(depth, flow)
            run_time_out(depth)
            run_channel_one(depth, held["chan", depth][0], held["cut", depth])
            flow = run_channel_two(depth)
        y_out = flow

    grad = result_cotangent.reshape(tokens, width)
    fix = jnp.zeros((runs, width), F32)
    small = [None] * layers
    sums = {}
    earlier_chan = earlier_att = None
    for depth in reversed(range(layers)):
        gain, bias, mix, rate, bonus, chain = layer_values(depth)
        flow, lead_t, xk_t, xv_t, xr_t, k, v, r, z, sa, sb = kept["time", depth]
        middle, lead, xk, xr, acts, carried, gate = kept["chan", depth]
        mine, other, accept = held["chan", depth]
        cut = held["cut", depth]
        part_rows = [cut.blocks * lookup_rows, grain, half_rows]
        part_spots = [0, part_rows[0], part_rows[0] + grain, part_rows[0] + grain + half_rows]
        if staged:
            packing = [(2, seq * dp // 4, 2, part_spots[3], columns)] * 2, part_spots
        else:
            widths = [cut.width, columns, columns]
            packing = [(2, seq, dp // 2, 2, n, w) for n, w in zip(part_rows, widths)], [0, 0, 0]
        *stores, grad, edge, small_chan = channel_back(
            cores, grad, fix, middle, lead, marks, gain[1:2], bias[1:2], mix[3:], gate, carried, xk, xr,
            acts, (mine[0], other[0]), (mine[1], other[1]), accept, cut, length, packing, table,
        )
        out_grad = grad
        if staged:
            flat = [s.reshape((2, seq * dp // 4, 2 * part_spots[3], columns)) for s in stores]
            if earlier_att:
                line = earlier_chan.end_second(grad)
                earlier_chan.z()
                away = earlier_att.third(line)
                edge, out_grad = tie((edge, grad), away)
                flat = tie(flat, away)
            elif swapped:
                edge, out_grad = tie((edge, grad), y_out)
                flat = tie(flat, y_out)
            chan_move = Scattering(*flat)
        if swapped:
            fix, edge_chan = edges, jnp.zeros((2, width), F32)
        else:
            fix, edge_chan = edge_back(edge, middle, length, gain[1])
        mine, other = held["att", depth]
        go, gr, gn, gd, ends = out_back(
            cores, out_grad, fix, k, v, r, sa, sb, marks, rate, bonus, mine, other, length
        )
        if staged:
            if earlier_att:
                near = earlier_att.end_third(go)
                earlier_att.second()
                go = tie(go, near, earlier_chan.parts[0])
            away = chan_move.third(go)
            gn = tie(gn, away)
        leave = states if swapped else entering(chain, begins * ends, -1)
        gk, gv, grad, edge, small_time = time_back(
            cores, grad, fix, flow, lead_t, k, v, sa, sb, gn, gd, gr, leave, marks, lines,
            gain[0:1], bias[0:1], mix[:3], rate, bonus, mine, other, length,
        )
        fading = small_time[5:6] * -rate * jnp.exp(-rate)
        small[depth] = jnp.concatenate(
            [
                small_time[0:1],
                small_chan[0:1] + edge_chan[0:1],
                small_time[1:2],
                small_chan[1:2] + edge_chan[1:2],
                small_time[2:5],
                small_chan[2:4],
                fading,
                small_time[6:7],
            ]
        )
        first_hop = None
        if staged and depth == 0:
            first_hop = hop_y(jnp.stack(small))
        if staged and earlier_chan:
            gk, gv = tie((gk, gv), earlier_chan.parts)
        stores_att = weight_grads([xk_t, xv_t], [xr_t, z], [gk, gv, gr, go], table)
        rows = width // dp
        if staged:
            more = []
            if depth == 0:
                sums_xy = hop_x(tie(first_hop, stores_att[0]))
                more.append(sums_xy)
            near = chan_move.end_third(stores_att[0], *more)
            if earlier_att:
                near = tie(near, earlier_att.end_second(near))
                earlier_att.z()
            flat = [s.reshape((2, seq * dp // 4, 4 * rows, columns)) for s in stores_att]
            att_move = Scattering(*tie(flat, near))
            chan_move.second()
            grad = tie(grad, near)
            if depth > 0:
                earlier_chan, earlier_att = chan_move, att_move
            sums["chan", depth], sums["att", depth] = chan_move, att_move
        else:
            sums["chan", depth] = scatter_plain(stores)
            sums["att", depth] = scatter_plain(stores_att)
        if swapped:
            edge_time = jnp.zeros((2, width), F32)
        else:
            fix, edge_time = edge_back(edge, flow, length, gain[0])
            small[depth] = small[depth].at[0].add(edge_time[0]).at[2].add(edge_time[1])
    small = jnp.stack(small)
    grad = grad.reshape(runs, length, width)
    if not swapped:
        grad = grad.at[:, -1].add(fix)
    if staged:
        last_chan, last_att = sums["chan", 0], sums["att", 0]
        sums_xy = sums_xy + moved(sums_xy, to_core)
        away, parts = last_att.away, earlier_att.parts
        line = last_chan.end_second(away)
        last_att.third(line, parts)
        last_chan.z(away, parts)
        last_att.end_third()
        small = summed_z(tie(sums_xy, last_chan.parts[:2]))
        last_att.second(last_chan.parts[:2])
        line = last_att.end_second(small)
        last_att.z()
        came = [last_att.parts]
        if swapped:
            kept_runs, sent_runs = runs_cut(tie(grad, line))
            came.append(partner_y(sent_runs.astype(BF)))
        small, came, *parts = tie((small, came, *[move.parts for move in sums.values()]))
        if swapped:
            grad = runs_joined(kept_runs, came[1].astype(F32))
        for move, part in zip(sums.values(), parts):
            move.parts = part
        totals = [move.total() for move in sums.values()]
        kept_all = [jnp.where(core == 0, total[0], total[1]) for total in totals]
        sent_all = [jnp.where(core == 0, total[1], total[0]) for total in totals]
        came_all = moved(jnp.concatenate(sent_all), to_core)
        spots = spots_of(kept_all)
        for name, mine, theirs in zip(list(sums), kept_all, cut_at(came_all, spots)):
            first, second = jnp.where(core == 0, mine, theirs), jnp.where(core == 0, theirs, mine)
            spots = part_spots if name[0] == "chan" else [0, 2 * rows]
            sums[name] = cut_at(first, spots), cut_at(second, spots)
    else:
        small = lax.psum(small, BOTH)
    large = []
    for depth in range(layers):
        first, second = sums["att", depth]
        triple = jnp.stack([first[0][:rows], first[0][rows:], second[0][:rows]])
        result = second[0][rows:]
        first, second = sums["chan", depth]
        lookup = join_lookup(first[0], second[0], lookup_rows, grain)
        content = jnp.concatenate([first[1], second[1]])
        large.append((triple, result, lookup, content, jnp.concatenate([first[2], second[2]])))
    large = [jnp.stack(members) for members in zip(*large)]
    return (
        y_out if swapped else y_out.reshape(runs, length, width),
        grad,
        small[:, 0:2],
        small[:, 2:4],
        small[:, 4:9],
        small[:, 9],
        small[:, 10],
        *large,
    )


def solution(mesh):
    return jax.shard_map(
        per_device,
        mesh=mesh,
        in_specs=(
            P("dp", "seq", None),
            P("dp", "seq"),
            P("dp", "seq", None),
            P(),
            P(),
            P(),
            P(),
            P(),
            P(None, None, "dp", "seq"),
            P(None, "dp", "seq"),
            P(None, "dp", "seq"),
            P(None, "dp", "seq"),
            P(None, "dp", "seq"),
        ),
        out_specs=(
            P("dp", "seq", None),
            P("dp", "seq", None),
            P(),
            P(),
            P(),
            P(),
            P(),
            P(None, None, "dp", "seq"),
            P(None, "dp", "seq"),
            P(None, "dp", "seq"),
            P(None, "dp", "seq"),
            P(None, "dp", "seq"),
        ),
        check_vma=False,
    )
```
